32 devices in a mesh: tm: 4 (over z), batch: 8 (over y, x, core).
Axes of the slice: x: 2, y: 2, z: 4, core: 2. Of those that a mesh axis runs over, the one named last changes fastest.
Arguments:
- mel_frames: float32 [24, 512, 512], P('batch', 'tm'), may hold values from -6 to 6
- lengths: int32 [8, 3], P('batch'), may hold values from 1 to 512, 1024 in all within a row
- cotangent: float32 [24, 4096, 256], P('batch', 'tm'), may hold values from -6 to 6
- matrices: float32 [3080192], P(('tm', 'batch')), may hold values from -8 to 8, as said below
- vectors: float32 [3840], P(('tm', 'batch')), may hold values from -3 to 3, as said below
- matrix_first: float32 [3080192], P(('tm', 'batch')), may hold values from -131072 to 131072, as said below
- matrix_second: float32 [3080192], P(('tm', 'batch')), may hold values from 8192 to 65536, as said below
- vector_first: float32 [3840], P(('tm', 'batch')), may hold values from -131072 to 131072, as said below
- vector_second: float32 [3840], P(('tm', 'batch')), may hold values from 8192 to 65536, as said below
Outputs:
- waveform: float32 [24, 4096, 256], P('batch', 'tm')
- frames_grad: float32 [24, 512, 512], P('batch', 'tm')
- new_matrices: float32 [3080192], P(('tm', 'batch'))
- matrix_copy: bfloat16 [3080192], P(('tm', 'batch'))
- matrix_first_new: float32 [3080192], P(('tm', 'batch'))
- matrix_second_new: float32 [3080192], P(('tm', 'batch'))
- new_vectors: float32 [3840], P(('tm', 'batch'))
- vector_copy: bfloat16 [3840], P(('tm', 'batch'))
- vector_first_new: float32 [3840], P(('tm', 'batch'))
- vector_second_new: float32 [3840], P(('tm', 'batch'))
- norm_table: float32 [2, 10], replicated
The draws below stay inside these ranges and needn't reach their ends.
Inputs may be any that keep to these rules, and one draw needn't show every extreme that they name: `matrices`: entries of both signs, of the size that keeps each layer's output of order one. `vectors`: the gains of the transposed convolution and the shortcuts are positive. `matrix_first`: both signs. `matrix_second`: positive. `vector_first`: both signs. `vector_second`: positive.
All inputs are finite; a program needn't handle non-finite values.
Results may differ from the reference program's by a relative error of at most 0.001.
Values sent between devices are 32-bit elements; how exact they have to be, the bound alone decides.
No kernel may reach another device: no remote copies, remote signals or barrier semaphores. Data moves between devices by JAX's collectives and lax.ppermute only.
A program may use at most 192 MiB of HBM per device.

```python
import math
import jax
import jax.numpy as jnp
import numpy as np
from jax import lax

IN_CH = 512
CH = 256
SEGS_DEV = 3
STEP = 5
SEG_FRAMES = 512
SEG_SAMPLES = 4096
SEGS = 24
MAT_ENTRIES = 3080192
VEC_ENTRIES = 3840
LIVE = 65536
N_BATCH = 8


def normal_like(key, count):
    return jax.random.truncated_normal(key, -4.0, 4.0, (count,), jnp.float32)


def draw_matrices(key, part):
    key = jax.random.fold_in(key, 11)
    position = jnp.arange(MAT_ENTRIES)
    up_end = 16 * IN_CH * CH
    within = (position - up_end) % (5 * CH * CH)
    scale = jnp.where(position < up_end, 1.0 / math.sqrt(16.0 * IN_CH), jnp.where(within < 3 * CH * CH, 1.0 / math.sqrt(3.0 * CH), jnp.where(within < 4 * CH * CH, 2.0 / math.sqrt(1.0 * CH), 1.0 / math.sqrt(1.0 * CH))))
    return (normal_like(key, MAT_ENTRIES) * scale).astype(jnp.float32)


def draw_vectors(key, part):
    key = jax.random.fold_in(key, 12)
    keys = jax.random.split(key, 3)
    position = jnp.arange(VEC_ENTRIES)
    relative = position - IN_CH - CH
    kind = relative % (4 * CH) // CH
    up_gains = jnp.exp(jax.random.uniform(keys[0], (VEC_ENTRIES,), jnp.float32, math.log(1.5), math.log(3.0)))
    short_gains = jax.random.uniform(keys[1], (VEC_ENTRIES,), jnp.float32, 0.6, 1.4)
    biases = 0.3 * normal_like(keys[2], VEC_ENTRIES)
    values = jnp.where(position < IN_CH, up_gains, jnp.where((relative >= 0) & (kind == 2), short_gains, biases))
    return values.astype(jnp.float32)


def first_moment(key, count):
    scale = 0.5 * math.sqrt(1.0 * LIVE)
    return (scale * normal_like(key, count)).astype(jnp.float32)


def second_moment(key, count):
    scale = 0.25 * LIVE
    factor = jnp.exp(jax.random.uniform(key, (count,), jnp.float32, 0.0, math.log(4.0)))
    return (scale * factor).astype(jnp.float32)


def draw_matrix_first(key, part):
    key = jax.random.fold_in(key, 13)
    return first_moment(key, MAT_ENTRIES)


def draw_matrix_second(key, part):
    key = jax.random.fold_in(key, 14)
    return second_moment(key, MAT_ENTRIES)


def draw_vector_first(key, part):
    key = jax.random.fold_in(key, 15)
    return first_moment(key, VEC_ENTRIES)


def draw_vector_second(key, part):
    key = jax.random.fold_in(key, 16)
    return second_moment(key, VEC_ENTRIES)


def block_scale(rng, shape, cuts, low, high):
    factor_of, own = 1.0, jax.random.fold_in(rng, 6)
    for dim, blocks in cuts:
        draws = jnp.exp(jax.random.uniform(jax.random.fold_in(own, dim), (blocks,), jnp.float32, low / len(cuts), high / len(cuts)))
        factor_of = factor_of * jnp.repeat(draws, shape[dim] // blocks).reshape([-1 if axis == dim else 1 for axis in range(len(shape))])
    return factor_of


def split_up(amount, total, most, skew):
    loads = [(1 << 20) // math.isqrt(rank ** skew) + 1 for rank in range(2, amount + 1)]
    spare, counts = total - most - (amount - 1), [1] * (amount - 1)
    while spare > 0:
        free = [i for i in range(amount - 1) if counts[i] < most]
        mass, remaining = sum([loads[i] for i in free]), spare
        for i in free:
            addition = min(most - counts[i], max(1, remaining * loads[i] // mass), spare)
            counts[i] = counts[i] + addition
            spare = spare - addition
    return np.array([most] + counts)


def ragged_sizes(rng, count, total, reach, lean):
    if count == 2:
        one = jax.random.randint(rng, (), max(1, total - reach), min(reach, total - 1) + 1)
        return jnp.stack([one, total - one])
    sizes = jnp.asarray(split_up(count, total, reach, lean), jnp.int32)
    couples = (count - 1) // 2
    giver, taker = sizes[1:1 + 2 * couples:2], sizes[2:2 + 2 * couples:2]
    margin = jnp.minimum(giver - 1, reach - taker)
    passed = jax.random.randint(jax.random.fold_in(rng, 1), (couples,), 0, 1 << 20) % (margin + 1)
    sizes = sizes.at[1:1 + 2 * couples:2].set(giver - passed).at[2:2 + 2 * couples:2].set(taker + passed)
    return sizes[jax.random.permutation(jax.random.fold_in(rng, 2), count)]


def bell_draw(own_key, extent, deviation, bound, cuts=(), dtype=jnp.bfloat16):
    array = jax.random.normal(own_key, extent, jnp.float32) * deviation
    if len(cuts) > 0:
        array = block_scale(own_key, extent, cuts, -0.22, 0.18) * array
    return jnp.clip(array, min=-bound, max=bound).astype(dtype)


def setup_inputs(seed: int = 0) -> dict:
    arg_keys = jax.random.split(jax.random.key(seed), 10)
    mel_frames = bell_draw(arg_keys[0], (SEGS, SEG_FRAMES, IN_CH), 1.0, 6.0, ((0, 8), (1, 4)), jnp.float32)
    lengths = jax.vmap(lambda own: ragged_sizes(own, SEGS_DEV, 2 * SEG_FRAMES, SEG_FRAMES, 2))(jax.random.split(arg_keys[1], N_BATCH)).reshape((N_BATCH, SEGS_DEV)).astype(jnp.int32)
    cotangent = bell_draw(arg_keys[2], (SEGS, SEG_SAMPLES, CH), 1.0, 6.0, ((0, 8), (1, 4)), jnp.float32)
    matrices = draw_matrices(jax.random.fold_in(arg_keys[9], 71), 0)
    vectors = draw_vectors(jax.random.fold_in(arg_keys[9], 71), 0)
    matrix_first = draw_matrix_first(jax.random.fold_in(arg_keys[9], 71), 0)
    matrix_second = draw_matrix_second(jax.random.fold_in(arg_keys[9], 71), 0)
    vector_first = draw_vector_first(jax.random.fold_in(arg_keys[9], 71), 0)
    vector_second = draw_vector_second(jax.random.fold_in(arg_keys[9], 71), 0)
    return {"mel_frames": mel_frames, "lengths": lengths, "cotangent": cotangent, "matrices": matrices, "vectors": vectors, "matrix_first": matrix_first, "matrix_second": matrix_second, "vector_first": vector_first, "vector_second": vector_second}


@jax.custom_vjp
def low(v):
    return lax.optimization_barrier(v.astype(jnp.bfloat16)).astype(jnp.float32)

@jax.custom_vjp
def low_back(v):
    return v

def low_keep(v):
    return (low(v), None)

def low_pass(kept, grad):
    return (grad,)

def back_keep(v):
    return (v, None)

def back_low(kept, grad):
    return (low(grad),)
low.defvjp(low_keep, low_pass)
low_back.defvjp(back_keep, back_low)
B_ONE = 0.5
B_TWO = 0.5
EPSILON = 1e-06
RATE = 0.5
DECAY = 0.01

def matrix_product(left, right):
    return jnp.dot(left, right, precision=lax.Precision.HIGHEST, preferred_element_type=jnp.float32)

def soft_leaky(value):
    return 0.2 * value + 0.8 * jax.nn.softplus(value)

def layout(in_channels, channels):
    shapes = [(in_channels, 16, channels)]
    for block_position_index in range(3):
        shapes = shapes + [(3, channels, channels), (channels, channels), (channels, channels)]
    starts = []
    position = 0
    for shape in shapes:
        starts.append(position)
        position = position + math.prod(shape)
    return (shapes, starts)

def unpack(matrices, vectors, in_channels, channels):
    shapes, starts = layout(in_channels, channels)
    weight_tensors = [matrices[first:first + math.prod(shape)].reshape(shape) for first, shape in zip(starts, shapes)]
    up_gain = vectors[:in_channels]
    remaining_items = vectors[in_channels:].reshape(13, channels)
    return (weight_tensors, up_gain, remaining_items)

def forward(matrices, vectors, frames_in, length):
    in_channels = frames_in.shape[1]
    channels = (vectors.shape[0] - in_channels) // 13
    weight_tensors, up_gain, remaining_items = unpack(matrices, vectors, in_channels, channels)
    frames = frames_in.shape[0]
    sample_values = 8 * frames
    frame_live = (jnp.arange(frames) < length).astype(jnp.float32)
    sample_live = (jnp.arange(sample_values) < 8 * length).astype(jnp.float32)
    masked = frames_in * frame_live[:, None]
    leaky = soft_leaky(masked)
    padded = jnp.pad(leaky, ((1, 1), (0, 0)))
    up_v = weight_tensors[0]
    up_w = up_gain[:, None, None] * up_v * lax.rsqrt(lax.optimization_barrier(jnp.sum(up_v * up_v, axis=(1, 2))))[:, None, None]
    centre = matrix_product(leaky, up_w[:, 4:12].reshape(in_channels, 8 * channels))
    side = jnp.concatenate([matrix_product(padded[:-2], up_w[:, 12:16].reshape(in_channels, 4 * channels)), matrix_product(padded[2:], up_w[:, 0:4].reshape(in_channels, 4 * channels))], axis=1)
    hidden = (centre + side).reshape(sample_values, channels) + remaining_items[0]
    for block_position_index in range(3):
        dilation_factor = 3 ** block_position_index
        dilated_weight, pointwise_weight, shortcut_direction = weight_tensors[1 + 3 * block_position_index:4 + 3 * block_position_index]
        dilated_bias, pointwise_bias, shortcut_gain, shortcut_bias = remaining_items[1 + 4 * block_position_index:5 + 4 * block_position_index]
        leaky_input = jnp.pad(soft_leaky(hidden), ((dilation_factor, dilation_factor), (0, 0)))
        dilated_output = dilated_bias
        for kernel_offset in range(3):
            dilated_output = dilated_output + matrix_product(leaky_input[kernel_offset * dilation_factor:kernel_offset * dilation_factor + sample_values], dilated_weight[kernel_offset])
        branch = pointwise_bias + matrix_product(soft_leaky(dilated_output), pointwise_weight)
        sc_w = shortcut_gain * shortcut_direction * lax.rsqrt(lax.optimization_barrier(jnp.sum(shortcut_direction * shortcut_direction, axis=0)))
        hidden = matrix_product(hidden, sc_w) + shortcut_bias + branch
    return hidden * sample_live[:, None]

def moments(gradient, first, second):
    first_new = B_ONE * first + (1.0 - B_ONE) * gradient
    second_new = B_TWO * second + (1.0 - B_TWO) * gradient * gradient
    direction = first_new / (1.0 - B_ONE ** STEP) / (jnp.sqrt(second_new / (1.0 - B_TWO ** STEP)) + EPSILON)
    return (first_new, second_new, direction)

def reference(mel_frames, lengths, cotangent, matrices, vectors, matrix_first, matrix_second, vector_first, vector_second):

    def one_segment(totals, inputs):
        frames_in, cot_in, length = inputs

        def run(mats_in, vecs_in, mel_in):
            return forward(mats_in, vecs_in, mel_in, length)
        wave_part, pull = jax.vjp(run, matrices, vectors, frames_in)
        mats_grad, vecs_grad, mel_grad = pull(cot_in)
        return ((totals[0] + mats_grad, totals[1] + vecs_grad), (wave_part, mel_grad))
    start = (jnp.zeros_like(matrices), jnp.zeros_like(vectors))
    (matrix_grad, vector_grad), (waveform, frames_grad) = lax.scan(one_segment, start, (mel_frames, cotangent, lengths.reshape(-1).astype(jnp.int32)))
    in_channels = mel_frames.shape[2]
    channels = cotangent.shape[2]
    shapes, starts = layout(in_channels, channels)
    owners = jnp.concatenate([jnp.full((math.prod(shape),), number, jnp.int32) for number, shape in enumerate(shapes)])
    matrix_first_new, matrix_second_new, direction = moments(matrix_grad, matrix_first, matrix_second)
    update = direction + DECAY * matrices
    weight_norm = jnp.sqrt(jax.ops.segment_sum(matrices * matrices, owners, num_segments=len(shapes)))
    update_norm = jnp.sqrt(jax.ops.segment_sum(update * update, owners, num_segments=len(shapes)))
    trust = weight_norm / update_norm
    new_matrices = matrices - RATE * trust[owners] * update
    vector_first_new, vector_second_new, vector_step = moments(vector_grad, vector_first, vector_second)
    new_vectors = vectors - RATE * vector_step
    norm_table = jnp.stack([weight_norm, update_norm])
    return (waveform, frames_grad, new_matrices, new_matrices.astype(jnp.bfloat16), matrix_first_new, matrix_second_new, new_vectors, new_vectors.astype(jnp.bfloat16), vector_first_new, vector_second_new, norm_table)
```

```python
import functools
import math

import jax
import jax.numpy as jnp
from jax import lax
from jax.experimental import pallas as pl
from jax.experimental.pallas import tpu as pltpu
from jax.sharding import Mesh
from jax.sharding import PartitionSpec as P

STEP = 5
B_ONE = 0.5
B_TWO = 0.5
EPSILON = 1e-06
RATE = 0.5
DECAY = 0.01
LANES = 128
EDGE_FRAMES = 8
EDGE = 32
PAD = 16
VMEM_LIMIT = 60 * 1024 * 1024
BF16 = jnp.bfloat16
F32 = jnp.float32


def soft_leaky(value):
    small = jnp.exp2(jnp.abs(value) * (-1.0 / math.log(2.0)))
    return jnp.maximum(value, 0.2 * value) + (0.8 * math.log(2.0)) * jnp.log2(1.0 + small)


def leaky_slope(value):
    return 0.6 + 0.4 * jnp.tanh(0.5 * value)


def split(value):
    high = value.astype(BF16)
    return high, (value - high.astype(F32)).astype(BF16)


def cat(parts, axis):
    return jnp.concatenate(parts, axis=axis)


def dot(left, right, dims=((1,), (0,))):
    return lax.dot_general(left, right, (dims, ((), ())), preferred_element_type=F32)


ROWS_COLS = ((1,), (0,))
ROWS_ROWS = ((1,), (1,))
COLS_COLS = ((0,), (0,))


def layout(in_channels, channels):
    shapes = [(in_channels, 16, channels)]
    for _ in range(3):
        shapes = shapes + [(3, channels, channels), (channels, channels), (channels, channels)]
    starts = []
    position = 0
    for shape in shapes:
        starts.append(position)
        position = position + math.prod(shape)
    return (shapes, starts, position)


def start_all(copies):
    for copy in copies:
        copy.start()


def wait_all(copies):
    for copy in copies:
        copy.wait()


def piece_copies(specs, numbers, pieces, flat, vecs, sem, vec_sem, outward):
    copies, vec_copies = [], []
    at = 0

    def move(one, other, signal):
        source, target = (other, one) if outward else (one, other)
        return pltpu.make_async_copy(source, target, signal)

    for spec, piece in zip(specs, pieces):
        for slot in range(spec["slots"]):
            owner = numbers[at]
            first = slot * spec["rows"]
            place = pl.multiple_of(owner * spec["pitch"] + spec["offset"], 8)
            signal = sem.at[at] if outward else sem.at[spec["part"], owner]
            copies.append(
                move(
                    piece.at[pl.ds(first, spec["valid"])],
                    flat.at[pl.ds(place, spec["valid"])],
                    signal,
                )
            )
            if spec["vec"] >= 0:
                place = pl.multiple_of(owner * 8, 8)
                vec_copies.append(
                    move(
                        piece.at[pl.ds(first + spec["vec"], 8)],
                        vecs.at[pl.ds(place, 8)],
                        vec_sem.at[at],
                    )
                )
            at += 1
    return copies, vec_copies


def copy_count(specs):
    return sum(spec["slots"] for spec in specs)


def prepare_kernel(geo, *refs):
    specs, in_ch, ch = geo["specs"], geo["in_ch"], geo["ch"]
    count = len(specs)
    numbers = refs[0]
    pieces = refs[1 : 1 + count]
    given = refs[1 + count : 1 + count + geo["given"]]
    outs = refs[1 + count + geo["given"] :]
    short, inverse, gains, items, squares = outs[6:11]
    flat, scratch, full, sem, vec_sem = outs[11:16]
    up_high, up_low, mat_high, mat_low, turn_high, turn_low = outs[16:22]
    up_sem, mat_sem = outs[22:]

    def up_copies(i):
        span = pl.ds(pl.multiple_of(i * 16, 16), 16)
        pairs = zip(outs[:2], (up_high, up_low))
        return [
            pltpu.make_async_copy(made.at[:, span], out.at[:, span], up_sem.at[n, i])
            for n, (out, made) in enumerate(pairs)
        ]

    def mat_copies(b):
        pairs = zip(outs[2:6], (mat_high, mat_low, turn_high, turn_low))
        return [
            pltpu.make_async_copy(made.at[b], out.at[b], mat_sem.at[n, b])
            for n, (out, made) in enumerate(pairs)
        ]
    vecs = given[0] if geo["given"] else scratch
    copies, vec_copies = piece_copies(specs, numbers, pieces, flat, scratch, sem, vec_sem, False)
    start_all(vec_copies)
    start_all(copies)
    parts = {spec["part"]: spec for spec in specs}
    pitch = specs[0]["pitch"] or flat.shape[0]

    def wait_for(owner):
        for part, spec in parts.items():
            span = pl.ds(0, spec["valid"])
            pltpu.make_async_copy(pieces[0].at[span], flat.at[span], sem.at[part, owner]).wait()

    wait_all(vec_copies)
    full[...] = jnp.zeros_like(full)
    for owner in range(geo["owners"]):
        row = owner * geo["vec_count"] // LANES
        full[row : row + 2] += vecs[8 * owner : 8 * owner + 2]
    columns = full[0:8].T
    gain = cat([columns[:, j : j + 1] for j in range(in_ch // LANES)], 0)
    gains[...] = jnp.broadcast_to(gain, gains.shape)
    items[...] = jnp.zeros_like(items)
    per_row = ch // LANES
    for i in range(13):
        for part in range(per_row):
            row = in_ch // LANES + per_row * i + part
            items[i : i + 1, part * LANES : (part + 1) * LANES] = full[row : row + 1]
    wide = 16 * ch // LANES
    squares[...] = jnp.zeros_like(squares)
    group = 16

    def channels(i, carry):
        first = i * (group * wide)
        now = (first + group * wide - 1) // pitch

        @pl.when((i == 0) | (now > (first - 1) // pitch))
        def _():
            wait_for(now)

        block = flat[pl.ds(pl.multiple_of(first, group * wide), group * wide), :]
        block = jnp.swapaxes(block.reshape(group, wide, LANES), 0, 1)
        square = jnp.sum(block * block, axis=0)
        squares[0:1, :] += jnp.sum(square, axis=0, keepdims=True)
        inv = lax.rsqrt(jnp.sum(square, axis=1, keepdims=True))
        span = pl.ds(pl.multiple_of(i * group, group), group)
        inverse[span, :] = jnp.broadcast_to(inv, (group, LANES))
        scale = gains[span, 0:1] * inv
        for place in range(wide):
            high, low = split(block[place] * scale)
            lanes = slice(place % 2 * LANES, place % 2 * LANES + LANES)
            up_high[place // 2, span, lanes] = high
            up_low[place // 2, span, lanes] = low
        start_all(up_copies(i))
        return carry

    lax.fori_loop(0, in_ch // group, channels, 0)
    for owner in range((in_ch * wide - 1) // pitch + 1, flat.shape[0] // pitch):
        wait_for(owner)
    base = in_ch * wide
    step = ch * ch // LANES
    for block in range(3):
        for number in range(5):
            first = base + (block * 5 + number) * step
            value = cat(
                [flat[pl.ds(first + part, ch, stride=per_row), :] for part in range(per_row)], 1
            )
            column = jnp.sum(value * value, axis=0, keepdims=True)
            which = 1 + 3 * block + max(number - 2, 0)
            squares[which : which + 1, :] += column[:, :LANES] + column[:, LANES:]
            if number == 4:
                short[block, 0:ch] = value
                root = lax.rsqrt(column)
                short[block, ch : ch + 8] = jnp.broadcast_to(root, (8, ch))
                value = value * (items[3 + 4 * block : 4 + 4 * block, :] * root)
            high, low = split(value)
            mat_high[block, number] = high
            mat_low[block, number] = low
            high, low = split(value.T)
            turn_high[block, number] = high
            turn_low[block, number] = low
        start_all(mat_copies(block))

    def finish(i, carry):
        wait_all(up_copies(i))
        return carry

    lax.fori_loop(0, in_ch // group, finish, 0)
    for block in range(3):
        wait_all(mat_copies(block))


def upsample_kernel(
    geo,
    scalars,
    mel_low,
    mel,
    mel_high,
    bias,
    mid_high,
    mid_low,
    side_high,
    side_low,
    out,
    wide,
    mid,
    sides,
):
    segments, frames, ahead = geo["segments"], geo["frames"], geo["ahead"]
    step = pl.program_id(0)
    kept = frames + 2 * (EDGE // 8)
    size = kept + 8
    in_ch = mel.shape[2]

    @pl.when(step == 0)
    def _():
        rows = frames + 2 * EDGE_FRAMES
        wide[...] = jnp.zeros_like(wide)
        place = scalars[segments] * frames - EDGE_FRAMES
        place = place + lax.broadcasted_iota(jnp.int32, (rows, 1), 0)
        inside = ((place >= 0) & (place < ahead)).astype(F32)
        for s in range(segments):
            live = (place < scalars[s]).astype(F32)
            first = 0
            for part in (mel_low, mel, mel_high):
                value = part[s]
                if part is not mel:
                    value = cat([value[0:EDGE_FRAMES], value[EDGE_FRAMES : 2 * EDGE_FRAMES]], 1)
                span = slice(first, first + value.shape[0])
                wide[s, span] = soft_leaky(value * live[span]) * inside[span]
                first = span.stop
        for s in range(segments):
            span = slice(s * size, (s + 1) * size)
            first = EDGE_FRAMES - EDGE // 8
            for target, shift in ((mid, 0), (sides.at[0], -1), (sides.at[1], 1)):
                high, low = split(wide[s, first + shift : first + shift + size])
                target[0, span] = high
                target[1, span] = low

    side = step // 4
    left_high = cat([mid[0], sides[side, 0]], 1)
    left_low = cat([mid[1], sides[side, 1]], 1)
    right_high = cat([mid_high[0], side_high[0]], 0)
    right_low = cat([mid_low[0], side_low[0]], 0)
    value = dot(cat([left_high, left_low, left_high], 1), cat([right_high, right_high, right_low], 0))
    value = value + bias[0:1, :]
    for s in range(segments):
        for half in range(out.shape[1]):
            out[s, half, pl.ds(step, kept, stride=8), :] = value[
                s * size : s * size + kept, half * LANES : (half + 1) * LANES
            ]


def blocks_kernel(
    geo,
    scalars,
    items,
    start,
    cot_low,
    cot,
    cot_high,
    mat_high,
    mat_low,
    turn_high,
    turn_low,
    short,
    wave,
    back,
    grads,
    sums,
    hidden,
    middle,
    padded,
    triple,
    act,
    mid_act,
    hid,
    flow,
    flow_pair,
    dil_acc,
    pair_acc,
):
    segments, ch, samples = geo["segments"], geo["ch"], geo["samples"]
    rows = samples + 2 * EDGE
    count = geo["tiles"]
    tile = rows // count
    tiles = [slice(r, r + tile) for r in range(0, rows, tile)]
    own = slice(EDGE, EDGE + samples)
    segment = pl.program_id(0)
    piece = scalars[segments]
    low_edge = jnp.where(piece > 0, 1.0, 0.0)
    high_edge = jnp.where(piece < scalars[segments + 1] - 1, 1.0, 0.0)
    position = piece * samples - EDGE + lax.broadcasted_iota(jnp.int32, (rows, 1), 0)
    live = position < 8 * scalars[segment]

    @pl.when(segment == 0)
    def _():
        for n in range(2):
            padded[n, 0:PAD] = jnp.zeros((PAD, ch), F32)
            padded[n, PAD + rows : PAD + rows + PAD] = jnp.zeros((PAD, ch), F32)
        dil_acc[...] = jnp.zeros_like(dil_acc)
        pair_acc[...] = jnp.zeros_like(pair_acc)
        sums[...] = jnp.zeros_like(sums)

    def put_padded(n, t, value):
        first, last = PAD + t * tile, PAD + (t + 1) * tile
        if t == 0:
            padded[n, first : first + EDGE] = value[:EDGE] * low_edge
            value, first = value[EDGE:], first + EDGE
        if t == count - 1:
            padded[n, last - EDGE : last] = value[value.shape[0] - EDGE :] * high_edge
            value, last = value[: value.shape[0] - EDGE], last - EDGE
        padded[n, first:last] = value

    def shift(n, t, gap):
        for k in range(3):
            first = PAD + t * tile + (k - 1) * gap
            high, low = split(padded[n, first : first + tile])
            triple[n, 0, tiles[t], k * ch : (k + 1) * ch] = high
            triple[n, 1, tiles[t], k * ch : (k + 1) * ch] = low

    def operand(parts, axis):
        high, low = parts
        return cat([high, high, low] if axis == 0 else [high, low, high], axis)

    def stack(refs, b, numbers):
        return [cat([ref[b, number] for number in numbers], 0) for ref in refs]

    weights = (mat_high, mat_low)
    turned = (turn_high, turn_low)

    def activate(b, t):
        value = hidden[b, tiles[t]]
        put_padded(b % 2, t, soft_leaky(value))
        hid[b, 0, tiles[t]], hid[b, 1, tiles[t]] = split(value)

    def widen(b, t):
        shift(b % 2, t, 3**b)
        act[b, :, tiles[t]] = triple[b % 2, :, tiles[t], ch : 2 * ch]

    def dilated(b, t):
        left = operand([triple[b % 2, n, tiles[t]] for n in range(2)], 1)
        right = operand(stack(weights, b, range(3)), 0)
        middle[b, tiles[t]] = dot(left, right) + items[1 + 4 * b : 2 + 4 * b, :]

    def bend(b, t):
        mid_act[b, 0, tiles[t]], mid_act[b, 1, tiles[t]] = split(soft_leaky(middle[b, tiles[t]]))

    def leave(b, t):
        left = cat(
            [
                operand([mid_act[b, n, tiles[t]] for n in range(2)], 1),
                operand([hid[b, n, tiles[t]] for n in range(2)], 1),
            ],
            1,
        )
        right = cat([operand(stack(weights, b, [number]), 0) for number in (3, 4)], 0)
        offset = items[2 + 4 * b : 3 + 4 * b, :] + items[4 + 4 * b : 5 + 4 * b, :]
        hidden[b + 1, tiles[t]] = dot(left, right) + offset

    for t in range(count):
        hidden[0, tiles[t]] = cat([start[0, half, tiles[t]] for half in range(start.shape[1])], 1)
        activate(0, t)
    for b in range(3):
        for t in range(count + 2):
            if t < count:
                widen(b, t)
                dilated(b, t)
            if 1 <= t <= count:
                bend(b, t - 1)
            if t >= 2:
                leave(b, t - 2)
                if b < 2:
                    activate(b + 1, t - 2)
    wave[0] = jnp.where(live[own], hidden[3, own], 0.0)
    first = 0
    for part in (cot_low[:, 2 * EDGE_FRAMES :], cot, cot_high[:, 2 * EDGE_FRAMES :]):
        span = slice(first, first + part.shape[1])
        flow[span] = jnp.where(live[span], part[0], 0.0)
        first = span.stop

    def part_flow(b, t):
        high, low = split(flow[tiles[t]])
        flow_pair[b % 2, 0, tiles[t]] = high
        flow_pair[b % 2, 1, tiles[t]] = low

    def inner(b, t):
        left = operand([flow_pair[b % 2, n, tiles[t]] for n in range(2)], 1)
        value = dot(left, operand(stack(turned, b, [3]), 0))
        put_padded(b % 2, t, value * leaky_slope(middle[b, tiles[t]]))

    def outer(b, t):
        left = operand([triple[b % 2, n, tiles[t]] for n in range(2)], 1)
        value = dot(left, operand(stack(turned, b, range(3)), 0))
        left = operand([flow_pair[b % 2, n, tiles[t]] for n in range(2)], 1)
        short_part = dot(left, operand(stack(turned, b, [4]), 0))
        flow[tiles[t]] = value * leaky_slope(hidden[b, tiles[t]]) + short_part

    def biases(b):
        body = padded[b % 2, PAD + EDGE : PAD + EDGE + samples]
        sums[8 * b : 8 * b + 1, :] += jnp.sum(body, axis=0, keepdims=True)
        sums[8 * b + 1 : 8 * b + 2, :] += jnp.sum(flow[own], axis=0, keepdims=True)

    def pair_weights(b):
        left = cat([flow_pair[b % 2, n, own].T for n in range(2)], 0)
        right = [cat([mid_act[b, n, own], hid[b, n, own]], 1) for n in range(2)]
        value = dot(left, right[0])
        pair_acc[b] += value[0:ch] + value[ch : 2 * ch] + dot(left[0:ch], right[1])

    def dilated_weights(b):
        left = cat([act[b, n, own].T for n in range(2)], 0)
        value = dot(left, triple[b % 2, 0, own])
        value = value[0:ch] + value[ch : 2 * ch]
        dil_acc[b] += value + dot(left[0:ch], triple[b % 2, 1, own])

    def backward_shift(b, t):
        shift(b % 2, t, -(3**b))

    for t in range(count):
        part_flow(2, t)
    for b in (2, 1, 0):
        for t in range(count):
            inner(b, t)
        pair_weights(b)
        backward_shift(b, 0)
        biases(b)
        for t in range(count):
            if t + 1 < count:
                backward_shift(b, t + 1)
            outer(b, t)
            if b > 0 and t >= 1:
                part_flow(b - 1, t - 1)
        dilated_weights(b)
        if b > 0:
            part_flow(b - 1, count - 1)
    flow[0:EDGE] = flow[0:EDGE] * low_edge
    flow[rows - EDGE : rows] = flow[rows - EDGE : rows] * high_edge
    sums[24:25, :] += jnp.sum(flow[own], axis=0, keepdims=True)
    for half in range(back.shape[1]):
        back[0, half] = flow[:, half * LANES : (half + 1) * LANES]

    @pl.when(segment == segments - 1)
    def _():
        step = ch * ch // LANES
        per_row = ch // LANES

        def put(number, value):
            for part in range(per_row):
                grads[pl.ds(number * step + part, ch, stride=per_row), :] = value[
                    :, part * LANES : (part + 1) * LANES
                ]

        for b in range(3):
            for k in range(3):
                put(5 * b + k, dil_acc[b, :, k * ch : (k + 1) * ch])
            put(5 * b + 3, pair_acc[b, :, 0:ch].T)
            whole = pair_acc[b, :, ch : 2 * ch].T
            inv = short[b, ch : ch + 1]
            direction = short[b, 0:ch] * inv
            along = jnp.sum(whole * direction, axis=0, keepdims=True)
            sums[8 * b + 2 : 8 * b + 3, :] = along
            gain = items[3 + 4 * b : 4 + 4 * b, :]
            put(5 * b + 4, gain * inv * (whole - along * direction))


def tap_window(back, tap, segments, frames):
    first = EDGE - 4 + tap
    halves = range(back.shape[1])
    return cat(
        [
            cat([back[s, half, pl.ds(first, frames, stride=8), :] for half in halves], 1)
            for s in range(segments)
        ],
        0,
    )


def weight_back_kernel(geo, scalars, numbers, mel, gain, inverse, sums, back, high, low, blocks, *refs):
    specs, segments, frames = geo["specs"], geo["segments"], geo["frames"]
    count = len(specs)
    pieces = refs[:count]
    outs = refs[count:]
    extra = outs[0] if geo["given"] else None
    turned, whole, kept, slope, flat, scratch, full, block_sem, sem, vec_sem = outs[
        geo["given"] :
    ]
    vecs = extra if geo["given"] else scratch
    step = pl.program_id(0)
    taps = pl.num_programs(0)
    in_ch = mel.shape[2]
    ch = high.shape[2]
    wide = 16 * ch // LANES
    body = in_ch * wide
    loads = [
        pltpu.make_async_copy(blocks, flat.at[pl.ds(body, blocks.shape[0])], block_sem.at[0]),
        pltpu.make_async_copy(high, kept.at[0], block_sem.at[1]),
        pltpu.make_async_copy(low, kept.at[1], block_sem.at[2]),
    ]

    @pl.when(step == 0)
    def _():
        start_all(loads)
        place = scalars[segments] * frames + lax.broadcasted_iota(jnp.int32, (frames, 1), 0)
        for s in range(segments):
            live = (place < scalars[s]).astype(F32)
            upper, lower = split(soft_leaky(mel[s] * live).T)
            for part, piece in enumerate((upper, lower, upper)):
                first = (part * segments + s) * frames
                turned[:, first : first + frames] = piece

    upper, lower = split(tap_window(back, step, segments, frames))
    whole[step] = dot(turned[...], cat([upper, upper, lower], 0))

    @pl.when(step == taps - 1)
    def _():
        wait_all(loads)
        group = 16

        def channels(i, carry):
            span = pl.ds(pl.multiple_of(i * group, group), group)
            along = jnp.zeros((group, ch), F32)
            for tap in range(16):
                raw = kept[0, tap, span].astype(F32) + kept[1, tap, span].astype(F32)
                along = along + raw * whole[tap, span]
            factor = gain[span, 0:1]
            column = jnp.sum(along, axis=1, keepdims=True) / factor
            slope[span] = jnp.broadcast_to(column, (group, LANES))
            inv = inverse[span, 0:1]
            scale = factor * inv
            turn = inv * column
            values = []
            for tap in range(16):
                raw = kept[0, tap, span].astype(F32) + kept[1, tap, span].astype(F32)
                value = scale * whole[tap, span] - turn * raw
                for half in range(ch // LANES):
                    values.append(value[:, half * LANES : (half + 1) * LANES])
            block = jnp.swapaxes(jnp.stack(values), 0, 1).reshape(group * wide, LANES)
            flat[pl.ds(pl.multiple_of(i * (group * wide), group * wide), group * wide), :] = block
            return carry

        lax.fori_loop(0, in_ch // group, channels, 0)
        for j in range(in_ch // LANES):
            full[j : j + 1] = slope[j * LANES : (j + 1) * LANES].T[0:1]
        order = [24]
        for b in range(3):
            order += [8 * b, 8 * b + 1, 8 * b + 2, 8 * b + 1]
        row = in_ch // LANES
        for number in order:
            for part in range(ch // LANES):
                full[row : row + 1] = sums[number : number + 1, part * LANES : (part + 1) * LANES]
                row += 1
        vecs[...] = jnp.zeros_like(vecs)
        for owner in range(geo["owners"]):
            row = owner * geo["vec_count"] // LANES
            vecs[8 * owner : 8 * owner + 2] = full[row : row + 2]

        copies, vec_copies = piece_copies(
            specs, numbers, pieces, flat, scratch, sem, vec_sem, True
        )
        start_all(copies + vec_copies)
        wait_all(copies + vec_copies)


def frames_back_kernel(geo, scalars, mel, back, high, low, out, total):
    segments, frames = geo["segments"], geo["frames"]
    step = pl.program_id(0)

    @pl.when(step == 0)
    def _():
        total[...] = jnp.zeros_like(total)

    upper, lower = split(tap_window(back, step, segments, frames))
    total[...] += dot(
        cat([upper, lower, upper], 1), cat([high[0], high[0], low[0]], 1), ROWS_ROWS
    )

    @pl.when(step == pl.num_programs(0) - 1)
    def _():
        place = scalars[segments] * frames + lax.broadcasted_iota(jnp.int32, (frames, 1), 0)
        for s in range(segments):
            live = (place < scalars[s]).astype(F32)
            value = total[s * frames : (s + 1) * frames]
            out[s] = value * leaky_slope(mel[s] * live) * live


def whole_spec(shape):
    return pl.BlockSpec(shape, lambda *_: (0,) * len(shape))


def vmem():
    return pl.BlockSpec(memory_space=pltpu.VMEM)


def smem():
    return pl.BlockSpec(memory_space=pltpu.SMEM)


def anywhere():
    return pl.BlockSpec(memory_space=pl.ANY)


def shape(dims, dtype=F32):
    return jax.ShapeDtypeStruct(dims, dtype)


def params():
    return pltpu.CompilerParams(vmem_limit_bytes=VMEM_LIMIT)


def prepare(pieces, specs, numbers, given, geo):
    in_ch, ch = geo["in_ch"], geo["ch"]
    entries = (in_ch * 16 * ch + 15 * ch * ch) // LANES
    geo = dict(geo, specs=specs, given=len(given))
    return pl.pallas_call(
        functools.partial(prepare_kernel, geo),
        out_shape=(
            shape((16, in_ch, ch), BF16),
            shape((16, in_ch, ch), BF16),
            shape((3, 5, ch, ch), BF16),
            shape((3, 5, ch, ch), BF16),
            shape((3, 5, ch, ch), BF16),
            shape((3, 5, ch, ch), BF16),
            shape((3, ch + 8, ch)),
            shape((in_ch, LANES)),
            shape((in_ch, LANES)),
            shape((16, ch)),
            shape((16, LANES)),
        ),
        in_specs=[smem()] + [anywhere()] * len(pieces) + [vmem()] * len(given),
        out_specs=(anywhere(),) * 6 + (vmem(),) * 5,
        scratch_shapes=[
            pltpu.VMEM((entries, LANES), F32),
            pltpu.VMEM((8 * geo["owners"], LANES), F32),
            pltpu.VMEM((40, LANES), F32),
            pltpu.SemaphoreType.DMA((3, geo["owners"])),
            pltpu.SemaphoreType.DMA((copy_count(specs),)),
            pltpu.VMEM((16, in_ch, ch), BF16),
            pltpu.VMEM((16, in_ch, ch), BF16),
        ]
        + [pltpu.VMEM((3, 5, ch, ch), BF16)] * 4
        + [
            pltpu.SemaphoreType.DMA((2, in_ch // 16)),
            pltpu.SemaphoreType.DMA((4, 3)),
        ],
        compiler_params=params(),
    )(numbers, *pieces, *given)


def upsample(scalars, mel_parts, items, up_high, up_low, ahead):
    segments, frames, in_ch = mel_parts[1].shape
    ch = up_high.shape[2]
    kept = frames + 2 * (EDGE // 8)
    size = kept + 8
    geo = {"segments": segments, "frames": frames, "ahead": ahead}
    out = (segments, ch // LANES, 8 * kept, LANES)
    return pl.pallas_call(
        functools.partial(upsample_kernel, geo),
        grid=(8,),
        out_shape=shape(out),
        in_specs=[smem()]
        + [whole_spec(part.shape) for part in mel_parts]
        + [
            whole_spec(items.shape),
            pl.BlockSpec((1, in_ch, ch), lambda j: (j + 4, 0, 0)),
            pl.BlockSpec((1, in_ch, ch), lambda j: (j + 4, 0, 0)),
            pl.BlockSpec((1, in_ch, ch), lambda j: ((j + 12) % 16, 0, 0)),
            pl.BlockSpec((1, in_ch, ch), lambda j: ((j + 12) % 16, 0, 0)),
        ],
        out_specs=whole_spec(out),
        scratch_shapes=[
            pltpu.VMEM((segments, frames + 2 * EDGE_FRAMES + 16, in_ch), F32),
            pltpu.VMEM((2, segments * size, in_ch), BF16),
            pltpu.VMEM((2, 2, segments * size, in_ch), BF16),
        ],
        compiler_params=params(),
    )(scalars, *mel_parts, items, up_high, up_low, up_high, up_low)


def blocks(scalars, items, start, cot_parts, mat_high, mat_low, turn_high, turn_low, short):
    segments, samples, ch = cot_parts[1].shape
    rows = samples + 2 * EDGE
    geo = {"segments": segments, "samples": samples, "ch": ch, "tiles": 4}
    halves = start.shape[1]
    flat = (15 * ch * ch // LANES, LANES)
    once = pl.Buffered(1)

    def fixed(dims):
        return pl.BlockSpec(dims, lambda s: (0,) * len(dims), pipeline_mode=once)

    return pl.pallas_call(
        functools.partial(blocks_kernel, geo),
        grid=(segments,),
        out_shape=(
            shape((segments, samples, ch)),
            shape((segments, halves, rows, LANES)),
            shape(flat),
            shape((32, ch)),
        ),
        in_specs=[
            smem(),
            fixed(items.shape),
            pl.BlockSpec((1, halves, rows, LANES), lambda s: (s, 0, 0, 0)),
        ]
        + [pl.BlockSpec((1,) + part.shape[1:], lambda s: (s, 0, 0)) for part in cot_parts]
        + [
            fixed(mat_high.shape),
            fixed(mat_low.shape),
            fixed(turn_high.shape),
            fixed(turn_low.shape),
            fixed(short.shape),
        ],
        out_specs=(
            pl.BlockSpec((1, samples, ch), lambda s: (s, 0, 0)),
            pl.BlockSpec((1, halves, rows, LANES), lambda s: (s, 0, 0, 0)),
            pl.BlockSpec(flat, lambda s: (0, 0), pipeline_mode=once),
            pl.BlockSpec((32, ch), lambda s: (0, 0)),
        ),
        scratch_shapes=[
            pltpu.VMEM((4, rows, ch), F32),
            pltpu.VMEM((3, rows, ch), F32),
            pltpu.VMEM((2, rows + 2 * PAD, ch), F32),
            pltpu.VMEM((2, 2, rows, 3 * ch), BF16),
            pltpu.VMEM((3, 2, rows, ch), BF16),
            pltpu.VMEM((3, 2, rows, ch), BF16),
            pltpu.VMEM((3, 2, rows, ch), BF16),
            pltpu.VMEM((rows, ch), F32),
            pltpu.VMEM((2, 2, rows, ch), BF16),
            pltpu.VMEM((3, ch, 3 * ch), F32),
            pltpu.VMEM((3, ch, 2 * ch), F32),
        ],
        compiler_params=params(),
    )(scalars, items, start, *cot_parts, mat_high, mat_low, turn_high, turn_low, short)


def weight_back(scalars, mel, gain, inverse, sums, back, high, low, block_grads, specs, numbers, geo):
    segments, frames, in_ch = mel.shape
    ch = high.shape[2]
    body = in_ch * 16 * ch // LANES
    given = 0 if specs[-1]["vec"] >= 0 else 1
    geo = dict(geo, specs=specs, segments=segments, frames=frames, given=given)
    vec_shape = (8 * geo["owners"], LANES)
    return pl.pallas_call(
        functools.partial(weight_back_kernel, geo),
        grid=(16,),
        out_shape=tuple(shape((spec["slots"] * spec["rows"], LANES)) for spec in specs)
        + (shape(vec_shape),) * given,
        in_specs=[
            smem(),
            smem(),
            whole_spec(mel.shape),
            whole_spec(gain.shape),
            whole_spec(inverse.shape),
            whole_spec(sums.shape),
            whole_spec(back.shape),
            anywhere(),
            anywhere(),
            anywhere(),
        ],
        out_specs=(anywhere(),) * len(specs) + (whole_spec(vec_shape),) * given,
        scratch_shapes=[
            pltpu.VMEM((in_ch, 3 * segments * frames), BF16),
            pltpu.VMEM((16, in_ch, ch), F32),
            pltpu.VMEM((2, 16, in_ch, ch), BF16),
            pltpu.VMEM((in_ch, LANES), F32),
            pltpu.VMEM((body + block_grads.shape[0], LANES), F32),
            pltpu.VMEM(vec_shape, F32),
            pltpu.VMEM((40, LANES), F32),
            pltpu.SemaphoreType.DMA((3,)),
            pltpu.SemaphoreType.DMA((copy_count(specs),)),
            pltpu.SemaphoreType.DMA((copy_count(specs),)),
        ],
        compiler_params=params(),
    )(scalars, numbers, mel, gain, inverse, sums, back, high, low, block_grads)


def frames_back(scalars, mel, back, high, low):
    segments, frames, in_ch = mel.shape
    ch = high.shape[2]
    geo = {"segments": segments, "frames": frames}
    weight = pl.BlockSpec((1, in_ch, ch), lambda k: (k, 0, 0))
    return pl.pallas_call(
        functools.partial(frames_back_kernel, geo),
        grid=(16,),
        out_shape=shape(mel.shape),
        in_specs=[smem(), whole_spec(mel.shape), whole_spec(back.shape), weight, weight],
        out_specs=whole_spec(mel.shape),
        scratch_shapes=[pltpu.VMEM((segments * frames, in_ch), F32)],
        compiler_params=params(),
        cost_estimate=pl.CostEstimate(
            flops=6 * segments * frames * in_ch * 16 * ch,
            bytes_accessed=4 * 16 * in_ch * ch + 8 * mel.size + 4 * back.size,
            transcendentals=0,
        ),
    )(scalars, mel, back, high, low)


def line_edges(low, high, axis):
    count = math.prod(lax.axis_size(name) for name in axis)
    forward = [(i, i + 1) for i in range(count - 1)]
    backward = [(target, source) for source, target in forward]
    return lax.ppermute(high, axis, forward), lax.ppermute(low, axis, backward)


def packed_edges(mel, cot):
    ch = cot.shape[2]
    edges = []
    for frames, samples in (
        (mel[:, :EDGE_FRAMES], cot[:, :EDGE]),
        (mel[:, mel.shape[1] - EDGE_FRAMES :], cot[:, cot.shape[1] - EDGE :]),
    ):
        edges.append(cat([frames[:, :, :ch], frames[:, :, ch:], samples], 1))
    return edges


def moments(gradient, first, second):
    first_new = B_ONE * first + (1.0 - B_ONE) * gradient
    second_new = B_TWO * second + (1.0 - B_TWO) * gradient * gradient
    direction = (
        first_new / (1.0 - B_ONE**STEP) / (jnp.sqrt(second_new / (1.0 - B_TWO**STEP)) + EPSILON)
    )
    return (first_new, second_new, direction)


def total(value, axes):
    for axis in axes:
        count = lax.axis_size(axis)
        step = 1
        while step < count:
            value = value + lax.ppermute(value, axis, [(i, i ^ step) for i in range(count)])
            step = 2 * step
    return value


FLIPS = {"wide": ("wide", 1), "deep": ("deep", 1), "near": ("line", 1), "far": ("line", 2), "core": ("core", 1)}
ORDERS = (("wide", "deep", "near", "far"), ("deep", "wide", "near", "far"), ("near", "far", "wide", "deep"))
LANE_ROWS = 8


def swap(value, flip):
    axis, step = FLIPS[flip]
    return lax.ppermute(value, axis, [(i, i ^ step) for i in range(lax.axis_size(axis))])


def owner_table(order, other_core):
    places = {name: lax.axis_index(name) for name in ("line", "deep", "wide", "core")}
    numbers = []
    for slot in range(16):
        here = dict(places)
        for bit, flip in enumerate(order):
            if slot >> (3 - bit) & 1:
                axis, step = FLIPS[flip]
                here[axis] = here[axis] ^ step
        core = here["core"] ^ other_core
        numbers.append(((here["line"] * 2 + here["deep"]) * 2 + here["wide"]) * 2 + core)
    return jnp.stack(numbers).astype(jnp.int32)


def part_sizes(shard_rows):
    last = shard_rows * 7 // 48 // 8 * 8
    first = (shard_rows - last) // 16 * 8
    return (first, first, shard_rows - 2 * first)


def part_specs(sizes, rows, slots):
    specs = []
    offset = 0
    for part, size in enumerate(sizes):
        valid = min(size, rows - offset)
        specs.append(
            {
                "part": part,
                "slots": slots,
                "rows": size,
                "pitch": rows,
                "offset": offset,
                "valid": valid,
                "vec": valid if valid < size else -1,
            }
        )
        offset += size
    return specs


def together(*values):
    return lax.optimization_barrier(values)


def gather_by_permutes(shard, sizes, edges, tm):
    first, second, third = sizes
    both, last = shard[: first + second], shard[first + second :]
    far, near, last_deep, last_wide, edges = together(
        swap(both, "far"),
        swap(both, "near"),
        swap(last, "deep"),
        swap(last, "wide"),
        line_edges(*edges, tm),
    )
    near_far, last_both = together(swap(far, "near"), swap(last_deep, "wide"))
    parts = (both, far, near, near_far)
    a = cat([part[:first] for part in parts], 0)
    b = cat([part[first:] for part in parts], 0)
    c = cat([last, last_deep, last_wide, last_both], 0)
    a, b, c = together(a, b, c)
    a_deep, b_wide, c_far = swap(a, "deep"), swap(b, "wide"), swap(c, "far")
    c_near = swap(c, "near")
    a_deep, b_wide, c_far, c_near, a, b = together(a_deep, b_wide, c_far, c_near, a, b)
    c_both = swap(c_far, "near")
    a_both, b_both = swap(a_deep, "wide"), swap(b_wide, "deep")
    a_wide, b_deep = swap(a, "wide"), swap(b, "deep")
    ready = [(0, 0, a), (1, 0, b), (2, 0, c), (0, 1, a_deep), (1, 1, b_wide), (2, 1, c_far)]
    ready.append((2, 2, c_near))
    others = [swap(array, "core") for _, _, array in ready]
    a_both, b_both, a_wide, b_deep, c_both, others = together(
        a_both, b_both, a_wide, b_deep, c_both, others
    )
    held = [(n, quarter, 0, array) for n, quarter, array in ready]
    held += [(n, quarter, 1, array) for (n, quarter, _), array in zip(ready, others)]
    rest = [(0, 2, a_wide), (1, 2, b_deep), (0, 3, a_both), (1, 3, b_both), (2, 3, c_both)]
    for n, quarter, array in rest:
        held += [(n, quarter, 0, array), (n, quarter, 1, swap(array, "core"))]
    return held, edges


def scatter_by_permutes(mine, theirs, sizes, beside):
    came = together(*[swap(value, "core") for value in theirs])
    terms = [[own, other] for own, other in zip(mine, came)]
    slots = 16
    for level in range(4):
        slots = slots // 2
        away = []
        for part, size in zip(terms, sizes):
            away.append(sum(term[slots * size : 2 * slots * size] for term in part))
        came = [swap(value, order[level]) for value, order in zip(away, ORDERS)]
        if level == 0:
            came, other = together(came, beside())
        else:
            came = together(*came)
        for part, value in zip(terms, came):
            part.append(value)
    summed = cat([sum(term[:size] for term in part) for part, size in zip(terms, sizes)], 0)
    return summed, other


def by_owner(mine, theirs, plan):
    grid, core_dim = plan["grid"], plan["core_dim"]
    first = lax.axis_index("core") == 0
    parts = [jnp.where(first, mine, theirs), jnp.where(first, theirs, mine)]
    chips = [size for place, size in enumerate(grid) if place != core_dim]
    parts = [part.reshape(chips + list(mine.shape[1:])) for part in parts]
    return jnp.stack(parts, axis=core_dim).reshape((-1,) + mine.shape[1:])


def by_core(shards, plan):
    grid, core_dim = plan["grid"], plan["core_dim"]
    grouped = shards.reshape(tuple(grid) + shards.shape[1:])
    core = lax.axis_index("core")
    mine = lax.dynamic_index_in_dim(grouped, core, core_dim, keepdims=False)
    theirs = lax.dynamic_index_in_dim(grouped, 1 - core, core_dim, keepdims=False)
    after = (-1,) + shards.shape[1:]
    return mine.reshape(after), theirs.reshape(after)


def body(
    plan,
    mel_frames,
    lengths,
    cotangent,
    matrices,
    vectors,
    matrix_first,
    matrix_second,
    vector_first,
    vector_second,
):
    tm, every, chip_axes = plan["tm"], plan["every"], plan["chip_axes"]
    segments, frames, in_ch = mel_frames.shape
    ch = cotangent.shape[2]
    pieces = math.prod(lax.axis_size(name) for name in tm)
    rows = matrices.shape[0] // LANES
    shard_rows = -(-(rows + 2) // 48) * 48
    vec_count = vectors.shape[0]
    spare = shard_rows - rows - 2
    owners = math.prod(plan["grid"])
    geo = {"in_ch": in_ch, "ch": ch, "owners": owners, "vec_count": vec_count}
    vec_first = lax.axis_index(every) * vec_count % LANES
    placed = lax.dynamic_update_slice(jnp.zeros((2 * LANES,), F32), vectors, (vec_first,))
    shard = jnp.concatenate(
        [
            matrices.reshape(rows, LANES),
            placed.reshape(2, LANES),
            jnp.zeros((spare, LANES), F32),
        ]
    )
    edges = packed_edges(mel_frames, cotangent)
    cubic = rows % 8 == 0 and plan["grid"] == (4, 2, 2, 2)
    sizes = part_sizes(shard_rows)
    if cubic:
        specs = part_specs(sizes, rows, 16)
        numbers = [[owner_table(order, core) for order in ORDERS] for core in range(2)]
        held, edges = gather_by_permutes(shard, sizes, edges, tm)
        held_numbers = jnp.concatenate(
            [numbers[c][n][4 * quarter : 4 * quarter + 4] for n, quarter, c, _ in held]
        )
        held_specs = [dict(specs[n], slots=4) for n, _, _, _ in held]
        held = [array for _, _, _, array in held]
        given = []
    else:
        edges = line_edges(*edges, tm)
        mine = lax.all_gather(shard, chip_axes, axis=0, tiled=False)
        gathered = by_owner(mine, swap(mine, "core"), plan)
        held = [gathered[:, :rows].reshape(-1, LANES)]
        whole = held[0].shape[0]
        specs = [
            {
                "part": 0,
                "slots": 1,
                "rows": whole,
                "pitch": 0,
                "offset": 0,
                "valid": whole,
                "vec": -1,
            }
        ]
        held_specs, held_numbers = specs, jnp.zeros((1,), jnp.int32)
        vec_rows = jnp.pad(gathered[:, rows : rows + 2], ((0, 0), (0, LANE_ROWS - 2), (0, 0)))
        given = [vec_rows.reshape(-1, LANES)]
    mel_parts = (edges[0], mel_frames, edges[1])
    cot_parts = (edges[0], cotangent, edges[1])
    scalars = jnp.concatenate(
        [lengths[0], jnp.stack([lax.axis_index(tm), jnp.int32(pieces)]).astype(jnp.int32)]
    )
    up_high, up_low, *mats, short, inverse, gain, items, squares = prepare(
        held, held_specs, held_numbers, given, geo
    )
    start = upsample(scalars, mel_parts, items, up_high, up_low, pieces * frames)
    waveform, back, block_grads, sums = blocks(scalars, items, start, cot_parts, *mats, short)
    if cubic:
        out_specs = specs * 2
        out_numbers = jnp.concatenate(numbers[0] + numbers[1])
    else:
        out_specs, out_numbers = held_specs, held_numbers
    grads = weight_back(
        scalars,
        mel_frames,
        gain,
        inverse,
        sums,
        back,
        up_high,
        up_low,
        block_grads,
        out_specs,
        out_numbers,
        geo,
    )
    if cubic:
        summed, frames_grad = scatter_by_permutes(
            grads[:3],
            grads[3:],
            sizes,
            lambda: frames_back(scalars, mel_frames, back, up_high, up_low),
        )
    else:
        vec_rows = grads[1].reshape(owners, LANE_ROWS, LANES)[:, :2]
        shards = jnp.concatenate(
            [
                grads[0].reshape(owners, rows, LANES),
                vec_rows,
                jnp.zeros((owners, spare, LANES), F32),
            ],
            axis=1,
        )
        mine, theirs = by_core(shards, plan)
        mine = mine + swap(theirs, "core")
        summed = lax.psum_scatter(mine, chip_axes, scatter_dimension=0, tiled=True)[0]
        frames_grad = frames_back(scalars, mel_frames, back, up_high, up_low)
    matrix_grad = summed[:rows]
    vec_rows = summed[rows : rows + 2].reshape(-1)
    vector_grad = lax.dynamic_slice(vec_rows, (vec_first,), (vec_count,))

    shapes, starts, whole = layout(in_ch, ch)
    matrices = matrices.reshape(rows, LANES)
    position = lax.axis_index(every) * rows + jnp.arange(rows, dtype=jnp.int32)
    lower = jnp.array([first // LANES for first in starts], jnp.int32)
    upper = jnp.array([first // LANES for first in starts[1:] + [whole]], jnp.int32)
    member = (position[:, None] >= lower[None, :]) & (position[:, None] < upper[None, :])
    member = member.astype(F32)
    matrix_first_new, matrix_second_new, direction = moments(
        matrix_grad, matrix_first.reshape(rows, LANES), matrix_second.reshape(rows, LANES)
    )
    update = direction + DECAY * matrices
    update_sq = jnp.sum(member * jnp.sum(update * update, axis=1)[:, None], axis=0)
    update_sq = total(update_sq, every)
    weight_norm = jnp.sqrt(jnp.sum(squares[:10], axis=1))
    update_norm = jnp.sqrt(update_sq)
    trust = weight_norm / update_norm
    row_trust = jnp.sum(member * trust[None, :], axis=1)
    new_matrices = (matrices - RATE * row_trust[:, None] * update).reshape(-1)
    vector_first_new, vector_second_new, vector_step = moments(
        vector_grad, vector_first, vector_second
    )
    new_vectors = vectors - RATE * vector_step
    norm_table = jnp.stack([weight_norm, update_norm])
    return (
        waveform,
        frames_grad,
        new_matrices,
        new_matrices.astype(BF16),
        matrix_first_new.reshape(-1),
        matrix_second_new.reshape(-1),
        new_vectors,
        new_vectors.astype(BF16),
        vector_first_new,
        vector_second_new,
        norm_table,
    )


def make_plan(mesh):
    tm, batch = mesh.shape["tm"], mesh.shape["batch"]
    if tm > 4:
        root = math.isqrt(batch)
        grid = (tm // 2, 2, root, batch // root)
        names = ("line", "core", "deep", "wide")
        tm_axes, batch_axes = ("line", "core"), ("deep", "wide")
        core_dim = 1
    else:
        root = math.isqrt(batch // 2)
        grid = (tm, root, batch // 2 // root, 2)
        names = ("line", "deep", "wide", "core")
        tm_axes, batch_axes = ("line",), ("deep", "wide", "core")
        core_dim = 3
    inner = Mesh(mesh.devices.reshape(grid), names)
    plan = {
        "tm": tm_axes,
        "batch": batch_axes,
        "every": names,
        "grid": grid,
        "core_dim": core_dim,
        "chip_axes": tuple(name for name in names if name != "core"),
    }
    return inner, plan


def solution(mesh):
    inner, plan = make_plan(mesh)
    tm, batch, every = plan["tm"], plan["batch"], plan["every"]
    pieces, flat = P(batch, tm, None), P(every)
    in_specs = (pieces, P(batch, None), pieces, flat, flat, flat, flat, flat, flat)
    out_specs = (pieces, pieces, flat, flat, flat, flat, flat, flat, flat, flat, P())
    return jax.shard_map(
        functools.partial(body, plan),
        mesh=inner,
        in_specs=in_specs,
        out_specs=out_specs,
        check_vma=False,
    )
```

```python
import functools
import math

import jax
import jax.numpy as jnp
from jax import lax
from jax.experimental import pallas as pl
from jax.experimental.pallas import tpu as pltpu
from jax.sharding import Mesh
from jax.sharding import PartitionSpec as P

STEP = 5
B_ONE = 0.5
B_TWO = 0.5
EPSILON = 1e-06
RATE = 0.5
DECAY = 0.01
LANES = 128
EDGE_FRAMES = 8
EDGE = 32
PAD = 16
VMEM_LIMIT = 60 * 1024 * 1024
BF16 = jnp.bfloat16
F32 = jnp.float32


def soft_leaky(value):
    small = jnp.exp2(jnp.abs(value) * (-1.0 / math.log(2.0)))
    return jnp.maximum(value, 0.2 * value) + (0.8 * math.log(2.0)) * jnp.log2(1.0 + small)


def leaky_slope(value):
    return 0.6 + 0.4 * jnp.tanh(0.5 * value)


def split(value):
    high = value.astype(BF16)
    return high, (value - high.astype(F32)).astype(BF16)


def cat(parts, axis):
    return jnp.concatenate(parts, axis=axis)


def dot(left, right, dims=((1,), (0,))):
    return lax.dot_general(left, right, (dims, ((), ())), preferred_element_type=F32)


ROWS_COLS = ((1,), (0,))
ROWS_ROWS = ((1,), (1,))
COLS_COLS = ((0,), (0,))


def layout(in_channels, channels):
    shapes = [(in_channels, 16, channels)]
    for _ in range(3):
        shapes = shapes + [(3, channels, channels), (channels, channels), (channels, channels)]
    starts = []
    position = 0
    for shape in shapes:
        starts.append(position)
        position = position + math.prod(shape)
    return (shapes, starts, position)


def start_all(copies):
    for copy in copies:
        copy.start()


def wait_all(copies):
    for copy in copies:
        copy.wait()


def piece_copies(specs, numbers, pieces, flat, vecs, sem, vec_sem, outward):
    copies, vec_copies = [], []
    at = 0

    def move(one, other, signal):
        source, target = (other, one) if outward else (one, other)
        return pltpu.make_async_copy(source, target, signal)

    for spec, piece in zip(specs, pieces):
        for slot in range(spec["slots"]):
            owner = numbers[at]
            first = slot * spec["rows"]
            place = pl.multiple_of(owner * spec["pitch"] + spec["offset"], 8)
            signal = sem.at[at] if outward else sem.at[spec["part"], owner]
            copies.append(
                move(
                    piece.at[pl.ds(first, spec["valid"])],
                    flat.at[pl.ds(place, spec["valid"])],
                    signal,
                )
            )
            if spec["vec"] >= 0:
                place = pl.multiple_of(owner * 8, 8)
                vec_copies.append(
                    move(
                        piece.at[pl.ds(first + spec["vec"], 8)],
                        vecs.at[pl.ds(place, 8)],
                        vec_sem.at[at],
                    )
                )
            at += 1
    return copies, vec_copies


def copy_count(specs):
    return sum(spec["slots"] for spec in specs)


def prepare_kernel(geo, *refs):
    specs, in_ch, ch = geo["specs"], geo["in_ch"], geo["ch"]
    count = len(specs)
    numbers = refs[0]
    pieces = refs[1 : 1 + count]
    given = refs[1 + count : 1 + count + geo["given"]]
    outs = refs[1 + count + geo["given"] :]
    short, inverse, gains, items, squares = outs[6:11]
    flat, scratch, full, sem, vec_sem = outs[11:16]
    up_high, up_low, mat_high, mat_low, turn_high, turn_low = outs[16:22]
    up_sem, mat_sem = outs[22:]

    def up_copies(i):
        span = pl.ds(pl.multiple_of(i * 16, 16), 16)
        pairs = zip(outs[:2], (up_high, up_low))
        return [
            pltpu.make_async_copy(made.at[:, span], out.at[:, span], up_sem.at[n, i])
            for n, (out, made) in enumerate(pairs)
        ]

    def mat_copies(b):
        pairs = zip(outs[2:6], (mat_high, mat_low, turn_high, turn_low))
        return [
            pltpu.make_async_copy(made.at[b], out.at[b], mat_sem.at[n, b])
            for n, (out, made) in enumerate(pairs)
        ]
    vecs = given[0] if geo["given"] else scratch
    copies, vec_copies = piece_copies(specs, numbers, pieces, flat, scratch, sem, vec_sem, False)
    start_all(vec_copies)
    start_all(copies)
    parts = {spec["part"]: spec for spec in specs}
    pitch = specs[0]["pitch"] or flat.shape[0]

    def wait_for(owner):
        for part, spec in parts.items():
            span = pl.ds(0, spec["valid"])
            pltpu.make_async_copy(pieces[0].at[span], flat.at[span], sem.at[part, owner]).wait()

    wait_all(vec_copies)
    full[...] = jnp.zeros_like(full)
    for owner in range(geo["owners"]):
        row = owner * geo["vec_count"] // LANES
        full[row : row + 2] += vecs[8 * owner : 8 * owner + 2]
    columns = full[0:8].T
    gain = cat([columns[:, j : j + 1] for j in range(in_ch // LANES)], 0)
    gains[...] = jnp.broadcast_to(gain, gains.shape)
    items[...] = jnp.zeros_like(items)
    per_row = ch // LANES
    for i in range(13):
        for part in range(per_row):
            row = in_ch // LANES + per_row * i + part
            items[i : i + 1, part * LANES : (part + 1) * LANES] = full[row : row + 1]
    wide = 16 * ch // LANES
    squares[...] = jnp.zeros_like(squares)
    group = 16

    def channels(i, carry):
        first = i * (group * wide)
        now = (first + group * wide - 1) // pitch

        @pl.when((i == 0) | (now > (first - 1) // pitch))
        def _():
            wait_for(now)

        block = flat[pl.ds(pl.multiple_of(first, group * wide), group * wide), :]
        block = jnp.swapaxes(block.reshape(group, wide, LANES), 0, 1)
        square = jnp.sum(block * block, axis=0)
        squares[0:1, :] += jnp.sum(square, axis=0, keepdims=True)
        inv = lax.rsqrt(jnp.sum(square, axis=1, keepdims=True))
        span = pl.ds(pl.multiple_of(i * group, group), group)
        inverse[span, :] = jnp.broadcast_to(inv, (group, LANES))
        scale = gains[span, 0:1] * inv
        for place in range(wide):
            high, low = split(block[place] * scale)
            lanes = slice(place % 2 * LANES, place % 2 * LANES + LANES)
            up_high[place // 2, span, lanes] = high
            up_low[place // 2, span, lanes] = low
        start_all(up_copies(i))
        return carry

    lax.fori_loop(0, in_ch // group, channels, 0)
    for owner in range((in_ch * wide - 1) // pitch + 1, flat.shape[0] // pitch):
        wait_for(owner)
    base = in_ch * wide
    step = ch * ch // LANES
    for block in range(3):
        for number in range(5):
            first = base + (block * 5 + number) * step
            value = cat(
                [flat[pl.ds(first + part, ch, stride=per_row), :] for part in range(per_row)], 1
            )
            column = jnp.sum(value * value, axis=0, keepdims=True)
            which = 1 + 3 * block + max(number - 2, 0)
            squares[which : which + 1, :] += column[:, :LANES] + column[:, LANES:]
            if number == 4:
                short[block, 0:ch] = value
                root = lax.rsqrt(column)
                short[block, ch : ch + 8] = jnp.broadcast_to(root, (8, ch))
                value = value * (items[3 + 4 * block : 4 + 4 * block, :] * root)
            high, low = split(value)
            mat_high[block, number] = high
            mat_low[block, number] = low
            high, low = split(value.T)
            turn_high[block, number] = high
            turn_low[block, number] = low
        start_all(mat_copies(block))

    def finish(i, carry):
        wait_all(up_copies(i))
        return carry

    lax.fori_loop(0, in_ch // group, finish, 0)
    for block in range(3):
        wait_all(mat_copies(block))


def upsample_kernel(
    geo,
    scalars,
    mel_low,
    mel,
    mel_high,
    bias,
    mid_high,
    mid_low,
    side_high,
    side_low,
    out,
    wide,
    mid,
    sides,
):
    segments, frames, ahead = geo["segments"], geo["frames"], geo["ahead"]
    step = pl.program_id(0)
    kept = frames + 2 * (EDGE // 8)
    size = kept + 8
    in_ch = mel.shape[2]

    @pl.when(step == 0)
    def _():
        rows = frames + 2 * EDGE_FRAMES
        wide[...] = jnp.zeros_like(wide)
        place = scalars[segments] * frames - EDGE_FRAMES
        place = place + lax.broadcasted_iota(jnp.int32, (rows, 1), 0)
        inside = ((place >= 0) & (place < ahead)).astype(F32)
        for s in range(segments):
            live = (place < scalars[s]).astype(F32)
            first = 0
            for part in (mel_low, mel, mel_high):
                value = part[s]
                if part is not mel:
                    value = cat([value[0:EDGE_FRAMES], value[EDGE_FRAMES : 2 * EDGE_FRAMES]], 1)
                span = slice(first, first + value.shape[0])
                wide[s, span] = soft_leaky(value * live[span]) * inside[span]
                first = span.stop
        for s in range(segments):
            span = slice(s * size, (s + 1) * size)
            first = EDGE_FRAMES - EDGE // 8
            for target, shift in ((mid, 0), (sides.at[0], -1), (sides.at[1], 1)):
                high, low = split(wide[s, first + shift : first + shift + size])
                target[0, span] = high
                target[1, span] = low

    side = step // 2
    left_high = cat([mid[0], sides[side, 0]], 1)
    left_low = cat([mid[1], sides[side, 1]], 1)
    left = cat([left_high, left_low, left_high], 1)
    for n in range(mid_high.shape[0]):
        right_high = cat([mid_high[n], side_high[n]], 0)
        right_low = cat([mid_low[n], side_low[n]], 0)
        value = dot(left, cat([right_high, right_high, right_low], 0)) + bias[0:1, :]
        place = step * mid_high.shape[0] + n
        for s in range(segments):
            for half in range(out.shape[1]):
                out[s, half, pl.ds(place, kept, stride=8), :] = value[
                    s * size : s * size + kept, half * LANES : (half + 1) * LANES
                ]


def blocks_kernel(
    geo,
    scalars,
    items,
    start,
    cot_low,
    cot,
    cot_high,
    mat_high,
    mat_low,
    turn_high,
    turn_low,
    short,
    wave,
    back,
    grads,
    sums,
    hidden,
    middle,
    padded,
    triple,
    act,
    mid_act,
    hid,
    flow,
    flow_pair,
    dil_acc,
    pair_acc,
):
    segments, ch, samples = geo["segments"], geo["ch"], geo["samples"]
    rows = samples + 2 * EDGE
    count = geo["tiles"]
    tile = rows // count
    tiles = [slice(r, r + tile) for r in range(0, rows, tile)]
    own = slice(EDGE, EDGE + samples)
    segment = pl.program_id(0)
    piece = scalars[segments]
    low_edge = jnp.where(piece > 0, 1.0, 0.0)
    high_edge = jnp.where(piece < scalars[segments + 1] - 1, 1.0, 0.0)
    position = piece * samples - EDGE + lax.broadcasted_iota(jnp.int32, (rows, 1), 0)
    live = position < 8 * scalars[segment]

    @pl.when(segment == 0)
    def _():
        for n in range(2):
            padded[n, 0:PAD] = jnp.zeros((PAD, ch), F32)
            padded[n, PAD + rows : PAD + rows + PAD] = jnp.zeros((PAD, ch), F32)
        dil_acc[...] = jnp.zeros_like(dil_acc)
        pair_acc[...] = jnp.zeros_like(pair_acc)
        sums[...] = jnp.zeros_like(sums)

    def put_padded(n, t, value):
        first, last = PAD + t * tile, PAD + (t + 1) * tile
        if t == 0:
            padded[n, first : first + EDGE] = value[:EDGE] * low_edge
            value, first = value[EDGE:], first + EDGE
        if t == count - 1:
            padded[n, last - EDGE : last] = value[value.shape[0] - EDGE :] * high_edge
            value, last = value[: value.shape[0] - EDGE], last - EDGE
        padded[n, first:last] = value

    def shift(n, t, gap):
        for k in range(3):
            first = PAD + t * tile + (k - 1) * gap
            high, low = split(padded[n, first : first + tile])
            triple[n, 0, tiles[t], k * ch : (k + 1) * ch] = high
            triple[n, 1, tiles[t], k * ch : (k + 1) * ch] = low

    def operand(parts, axis):
        high, low = parts
        return cat([high, high, low] if axis == 0 else [high, low, high], axis)

    def stack(refs, b, numbers):
        return [cat([ref[b, number] for number in numbers], 0) for ref in refs]

    weights = (mat_high, mat_low)
    turned = (turn_high, turn_low)

    def activate(b, t):
        value = hidden[b, tiles[t]]
        put_padded(b % 2, t, soft_leaky(value))
        hid[b, 0, tiles[t]], hid[b, 1, tiles[t]] = split(value)

    def widen(b, t):
        shift(b % 2, t, 3**b)
        act[b, :, tiles[t]] = triple[b % 2, :, tiles[t], ch : 2 * ch]

    def dilated(b, t):
        left = operand([triple[b % 2, n, tiles[t]] for n in range(2)], 1)
        right = operand(stack(weights, b, range(3)), 0)
        middle[b, tiles[t]] = dot(left, right) + items[1 + 4 * b : 2 + 4 * b, :]

    def bend(b, t):
        mid_act[b, 0, tiles[t]], mid_act[b, 1, tiles[t]] = split(soft_leaky(middle[b, tiles[t]]))

    def leave(b, t):
        left = cat(
            [
                operand([mid_act[b, n, tiles[t]] for n in range(2)], 1),
                operand([hid[b, n, tiles[t]] for n in range(2)], 1),
            ],
            1,
        )
        right = cat([operand(stack(weights, b, [number]), 0) for number in (3, 4)], 0)
        offset = items[2 + 4 * b : 3 + 4 * b, :] + items[4 + 4 * b : 5 + 4 * b, :]
        hidden[b + 1, tiles[t]] = dot(left, right) + offset

    for t in range(count):
        hidden[0, tiles[t]] = cat([start[0, half, tiles[t]] for half in range(start.shape[1])], 1)
        activate(0, t)
    for b in range(3):
        for t in range(count + 2):
            if t < count:
                widen(b, t)
                dilated(b, t)
            if 1 <= t <= count:
                bend(b, t - 1)
            if t >= 2:
                leave(b, t - 2)
                if b < 2:
                    activate(b + 1, t - 2)
    wave[0] = jnp.where(live[own], hidden[3, own], 0.0)
    first = 0
    for part in (cot_low[:, 2 * EDGE_FRAMES :], cot, cot_high[:, 2 * EDGE_FRAMES :]):
        span = slice(first, first + part.shape[1])
        flow[span] = jnp.where(live[span], part[0], 0.0)
        first = span.stop

    def part_flow(b, t):
        high, low = split(flow[tiles[t]])
        flow_pair[b % 2, 0, tiles[t]] = high
        flow_pair[b % 2, 1, tiles[t]] = low

    def inner(b, t):
        left = operand([flow_pair[b % 2, n, tiles[t]] for n in range(2)], 1)
        value = dot(left, operand(stack(turned, b, [3]), 0))
        put_padded(b % 2, t, value * leaky_slope(middle[b, tiles[t]]))

    def outer(b, t):
        left = operand([triple[b % 2, n, tiles[t]] for n in range(2)], 1)
        value = dot(left, operand(stack(turned, b, range(3)), 0))
        left = operand([flow_pair[b % 2, n, tiles[t]] for n in range(2)], 1)
        short_part = dot(left, operand(stack(turned, b, [4]), 0))
        flow[tiles[t]] = value * leaky_slope(hidden[b, tiles[t]]) + short_part

    def biases(b):
        body = padded[b % 2, PAD + EDGE : PAD + EDGE + samples]
        sums[8 * b : 8 * b + 1, :] += jnp.sum(body, axis=0, keepdims=True)
        sums[8 * b + 1 : 8 * b + 2, :] += jnp.sum(flow[own], axis=0, keepdims=True)

    def pair_weights(b):
        left = cat([flow_pair[b % 2, n, own].T for n in range(2)], 0)
        right = [cat([mid_act[b, n, own], hid[b, n, own]], 1) for n in range(2)]
        value = dot(left, right[0])
        pair_acc[b] += value[0:ch] + value[ch : 2 * ch] + dot(left[0:ch], right[1])

    def dilated_weights(b):
        left = cat([act[b, n, own].T for n in range(2)], 0)
        value = dot(left, triple[b % 2, 0, own])
        value = value[0:ch] + value[ch : 2 * ch]
        dil_acc[b] += value + dot(left[0:ch], triple[b % 2, 1, own])

    def backward_shift(b, t):
        shift(b % 2, t, -(3**b))

    for t in range(count):
        part_flow(2, t)
    for b in (2, 1, 0):
        for t in range(count):
            inner(b, t)
        pair_weights(b)
        backward_shift(b, 0)
        biases(b)
        for t in range(count):
            if t + 1 < count:
                backward_shift(b, t + 1)
            outer(b, t)
            if b > 0 and t >= 1:
                part_flow(b - 1, t - 1)
        dilated_weights(b)
        if b > 0:
            part_flow(b - 1, count - 1)
    flow[0:EDGE] = flow[0:EDGE] * low_edge
    flow[rows - EDGE : rows] = flow[rows - EDGE : rows] * high_edge
    sums[24:25, :] += jnp.sum(flow[own], axis=0, keepdims=True)
    for half in range(back.shape[1]):
        back[0, half] = flow[:, half * LANES : (half + 1) * LANES]

    @pl.when(segment == segments - 1)
    def _():
        step = ch * ch // LANES
        per_row = ch // LANES

        def put(number, value):
            for part in range(per_row):
                grads[pl.ds(number * step + part, ch, stride=per_row), :] = value[
                    :, part * LANES : (part + 1) * LANES
                ]

        for b in range(3):
            for k in range(3):
                put(5 * b + k, dil_acc[b, :, k * ch : (k + 1) * ch])
            put(5 * b + 3, pair_acc[b, :, 0:ch].T)
            whole = pair_acc[b, :, ch : 2 * ch].T
            inv = short[b, ch : ch + 1]
            direction = short[b, 0:ch] * inv
            along = jnp.sum(whole * direction, axis=0, keepdims=True)
            sums[8 * b + 2 : 8 * b + 3, :] = along
            gain = items[3 + 4 * b : 4 + 4 * b, :]
            put(5 * b + 4, gain * inv * (whole - along * direction))


def tap_window(back, tap, segments, frames):
    first = EDGE - 4 + tap
    halves = range(back.shape[1])
    return cat(
        [
            cat([back[s, half, pl.ds(first, frames, stride=8), :] for half in halves], 1)
            for s in range(segments)
        ],
        0,
    )


def weight_back_kernel(
    geo, scalars, numbers, slots, mel, gain, inverse, sums, back, high, low, blocks, *refs
):
    specs, segments, frames = geo["specs"], geo["segments"], geo["frames"]
    count = len(specs)
    pieces = refs[:count]
    outs = refs[count:]
    extra = outs[0] if geo["given"] else None
    turned, whole, kept, slope, flat, scratch, full, block_sem, sem, vec_sem = outs[geo["given"] :]
    vecs = extra if geo["given"] else scratch
    in_ch = mel.shape[2]
    ch = high.shape[2]
    wide = 16 * ch // LANES
    body = in_ch * wide
    pitch = specs[0]["pitch"] or flat.shape[0]
    owners = flat.shape[0] // pitch
    loads = [
        pltpu.make_async_copy(blocks, flat.at[pl.ds(body, blocks.shape[0])], block_sem.at[0]),
        pltpu.make_async_copy(high, kept.at[0], block_sem.at[1]),
        pltpu.make_async_copy(low, kept.at[1], block_sem.at[2]),
    ]
    start_all(loads)

    def send(owner):
        for number, (spec, piece) in enumerate(zip(specs, pieces)):

            @pl.when(slots[number * owners + owner] >= 0)
            def _():
                slot = slots[number * owners + owner]
                first = pl.multiple_of(slot * spec["rows"], 8)
                place = pl.multiple_of(owner * pitch + spec["offset"], 8)
                pltpu.make_async_copy(
                    flat.at[pl.ds(place, spec["valid"])],
                    piece.at[pl.ds(first, spec["valid"])],
                    sem.at[number, slot],
                ).start()

    def send_each(first, last):
        def step(owner, carry):
            send(owner)
            return carry

        lax.fori_loop(first, last, step, 0)

    place = scalars[segments] * frames + lax.broadcasted_iota(jnp.int32, (frames, 1), 0)
    for s in range(segments):
        live = (place < scalars[s]).astype(F32)
        upper, lower = split(soft_leaky(mel[s] * live).T)
        for part, piece in enumerate((upper, lower, upper)):
            first = (part * segments + s) * frames
            turned[:, first : first + frames] = piece

    def taps(tap, carry):
        upper, lower = split(tap_window(back, tap, segments, frames))
        whole[tap] = dot(turned[...], cat([upper, upper, lower], 0))
        return carry

    lax.fori_loop(0, 16, taps, 0)
    wait_all(loads)
    shared = body // pitch
    send_each(-(-body // pitch), owners)
    group = 16

    def channels(i, carry):
        span = pl.ds(pl.multiple_of(i * group, group), group)
        along = jnp.zeros((group, ch), F32)
        for tap in range(16):
            raw = kept[0, tap, span].astype(F32) + kept[1, tap, span].astype(F32)
            along = along + raw * whole[tap, span]
        factor = gain[span, 0:1]
        column = jnp.sum(along, axis=1, keepdims=True) / factor
        slope[span] = jnp.broadcast_to(column, (group, LANES))
        inv = inverse[span, 0:1]
        scale = factor * inv
        turn = inv * column
        values = []
        for tap in range(16):
            raw = kept[0, tap, span].astype(F32) + kept[1, tap, span].astype(F32)
            value = scale * whole[tap, span] - turn * raw
            for half in range(ch // LANES):
                values.append(value[:, half * LANES : (half + 1) * LANES])
        block = jnp.swapaxes(jnp.stack(values), 0, 1).reshape(group * wide, LANES)
        first = pl.multiple_of(i * (group * wide), group * wide)
        flat[pl.ds(first, group * wide), :] = block
        done = (first + group * wide) // pitch

        @pl.when(done > first // pitch)
        def _():
            send(done - 1)

        return carry

    lax.fori_loop(0, in_ch // group, channels, 0)
    if body % pitch:
        send(shared)
    for j in range(in_ch // LANES):
        full[j : j + 1] = slope[j * LANES : (j + 1) * LANES].T[0:1]
    order = [24]
    for b in range(3):
        order += [8 * b, 8 * b + 1, 8 * b + 2, 8 * b + 1]
    row = in_ch // LANES
    for number in order:
        for part in range(ch // LANES):
            full[row : row + 1] = sums[number : number + 1, part * LANES : (part + 1) * LANES]
            row += 1
    vecs[...] = jnp.zeros_like(vecs)
    for owner in range(geo["owners"]):
        row = owner * geo["vec_count"] // LANES
        vecs[8 * owner : 8 * owner + 2] = full[row : row + 2]
    _, vec_copies = piece_copies(specs, numbers, pieces, flat, scratch, vec_sem, vec_sem, True)
    start_all(vec_copies)
    for number, (spec, piece) in enumerate(zip(specs, pieces)):
        for slot in range(spec["slots"]):
            pltpu.make_async_copy(
                flat.at[pl.ds(0, spec["valid"])],
                piece.at[pl.ds(slot * spec["rows"], spec["valid"])],
                sem.at[number, slot],
            ).wait()
    wait_all(vec_copies)


def frames_back_kernel(geo, scalars, mel, back, high, low, out, total):
    segments, frames = geo["segments"], geo["frames"]
    step = pl.program_id(0)

    @pl.when(step == 0)
    def _():
        total[...] = jnp.zeros_like(total)

    upper, lower = split(tap_window(back, step, segments, frames))
    total[...] += dot(
        cat([upper, lower, upper], 1), cat([high[0], high[0], low[0]], 1), ROWS_ROWS
    )

    @pl.when(step == pl.num_programs(0) - 1)
    def _():
        place = scalars[segments] * frames + lax.broadcasted_iota(jnp.int32, (frames, 1), 0)
        for s in range(segments):
            live = (place < scalars[s]).astype(F32)
            value = total[s * frames : (s + 1) * frames]
            out[s] = value * leaky_slope(mel[s] * live) * live


def whole_spec(shape):
    return pl.BlockSpec(shape, lambda *_: (0,) * len(shape))


def vmem():
    return pl.BlockSpec(memory_space=pltpu.VMEM)


def smem():
    return pl.BlockSpec(memory_space=pltpu.SMEM)


def anywhere():
    return pl.BlockSpec(memory_space=pl.ANY)


def shape(dims, dtype=F32):
    return jax.ShapeDtypeStruct(dims, dtype)


def params():
    return pltpu.CompilerParams(vmem_limit_bytes=VMEM_LIMIT)


def prepare(pieces, specs, numbers, given, geo):
    in_ch, ch = geo["in_ch"], geo["ch"]
    entries = (in_ch * 16 * ch + 15 * ch * ch) // LANES
    geo = dict(geo, specs=specs, given=len(given))
    return pl.pallas_call(
        functools.partial(prepare_kernel, geo),
        out_shape=(
            shape((16, in_ch, ch), BF16),
            shape((16, in_ch, ch), BF16),
            shape((3, 5, ch, ch), BF16),
            shape((3, 5, ch, ch), BF16),
            shape((3, 5, ch, ch), BF16),
            shape((3, 5, ch, ch), BF16),
            shape((3, ch + 8, ch)),
            shape((in_ch, LANES)),
            shape((in_ch, LANES)),
            shape((16, ch)),
            shape((16, LANES)),
        ),
        in_specs=[smem()] + [anywhere()] * len(pieces) + [vmem()] * len(given),
        out_specs=(anywhere(),) * 6 + (vmem(),) * 5,
        scratch_shapes=[
            pltpu.VMEM((entries, LANES), F32),
            pltpu.VMEM((8 * geo["owners"], LANES), F32),
            pltpu.VMEM((40, LANES), F32),
            pltpu.SemaphoreType.DMA((3, geo["owners"])),
            pltpu.SemaphoreType.DMA((copy_count(specs),)),
            pltpu.VMEM((16, in_ch, ch), BF16),
            pltpu.VMEM((16, in_ch, ch), BF16),
        ]
        + [pltpu.VMEM((3, 5, ch, ch), BF16)] * 4
        + [
            pltpu.SemaphoreType.DMA((2, in_ch // 16)),
            pltpu.SemaphoreType.DMA((4, 3)),
        ],
        compiler_params=params(),
    )(numbers, *pieces, *given)


def upsample(scalars, mel_parts, items, up_high, up_low, ahead):
    segments, frames, in_ch = mel_parts[1].shape
    ch = up_high.shape[2]
    kept = frames + 2 * (EDGE // 8)
    size = kept + 8
    geo = {"segments": segments, "frames": frames, "ahead": ahead}
    out = (segments, ch // LANES, 8 * kept, LANES)
    return pl.pallas_call(
        functools.partial(upsample_kernel, geo),
        grid=(4,),
        out_shape=shape(out),
        in_specs=[smem()]
        + [whole_spec(part.shape) for part in mel_parts]
        + [
            whole_spec(items.shape),
            pl.BlockSpec((2, in_ch, ch), lambda j: (j + 2, 0, 0)),
            pl.BlockSpec((2, in_ch, ch), lambda j: (j + 2, 0, 0)),
            pl.BlockSpec((2, in_ch, ch), lambda j: ((j + 6) % 8, 0, 0)),
            pl.BlockSpec((2, in_ch, ch), lambda j: ((j + 6) % 8, 0, 0)),
        ],
        out_specs=whole_spec(out),
        scratch_shapes=[
            pltpu.VMEM((segments, frames + 2 * EDGE_FRAMES + 16, in_ch), F32),
            pltpu.VMEM((2, segments * size, in_ch), BF16),
            pltpu.VMEM((2, 2, segments * size, in_ch), BF16),
        ],
        compiler_params=params(),
    )(scalars, *mel_parts, items, up_high, up_low, up_high, up_low)


def blocks(scalars, items, start, cot_parts, mat_high, mat_low, turn_high, turn_low, short):
    segments, samples, ch = cot_parts[1].shape
    rows = samples + 2 * EDGE
    geo = {"segments": segments, "samples": samples, "ch": ch, "tiles": 4}
    halves = start.shape[1]
    flat = (15 * ch * ch // LANES, LANES)
    once = pl.Buffered(1)

    def fixed(dims):
        return pl.BlockSpec(dims, lambda s: (0,) * len(dims), pipeline_mode=once)

    return pl.pallas_call(
        functools.partial(blocks_kernel, geo),
        grid=(segments,),
        out_shape=(
            shape((segments, samples, ch)),
            shape((segments, halves, rows, LANES)),
            shape(flat),
            shape((32, ch)),
        ),
        in_specs=[
            smem(),
            fixed(items.shape),
            pl.BlockSpec((1, halves, rows, LANES), lambda s: (s, 0, 0, 0)),
        ]
        + [pl.BlockSpec((1,) + part.shape[1:], lambda s: (s, 0, 0)) for part in cot_parts]
        + [
            fixed(mat_high.shape),
            fixed(mat_low.shape),
            fixed(turn_high.shape),
            fixed(turn_low.shape),
            fixed(short.shape),
        ],
        out_specs=(
            pl.BlockSpec((1, samples, ch), lambda s: (s, 0, 0)),
            pl.BlockSpec((1, halves, rows, LANES), lambda s: (s, 0, 0, 0)),
            pl.BlockSpec(flat, lambda s: (0, 0), pipeline_mode=once),
            pl.BlockSpec((32, ch), lambda s: (0, 0)),
        ),
        scratch_shapes=[
            pltpu.VMEM((4, rows, ch), F32),
            pltpu.VMEM((3, rows, ch), F32),
            pltpu.VMEM((2, rows + 2 * PAD, ch), F32),
            pltpu.VMEM((2, 2, rows, 3 * ch), BF16),
            pltpu.VMEM((3, 2, rows, ch), BF16),
            pltpu.VMEM((3, 2, rows, ch), BF16),
            pltpu.VMEM((3, 2, rows, ch), BF16),
            pltpu.VMEM((rows, ch), F32),
            pltpu.VMEM((2, 2, rows, ch), BF16),
            pltpu.VMEM((3, ch, 3 * ch), F32),
            pltpu.VMEM((3, ch, 2 * ch), F32),
        ],
        compiler_params=params(),
    )(scalars, items, start, *cot_parts, mat_high, mat_low, turn_high, turn_low, short)


def weight_back(
    scalars, mel, gain, inverse, sums, back, high, low, block_grads, specs, numbers, slots, geo
):
    segments, frames, in_ch = mel.shape
    ch = high.shape[2]
    body = in_ch * 16 * ch // LANES
    given = 0 if specs[-1]["vec"] >= 0 else 1
    geo = dict(geo, specs=specs, segments=segments, frames=frames, given=given)
    vec_shape = (8 * geo["owners"], LANES)
    return pl.pallas_call(
        functools.partial(weight_back_kernel, geo),
        out_shape=tuple(shape((spec["slots"] * spec["rows"], LANES)) for spec in specs)
        + (shape(vec_shape),) * given,
        in_specs=[smem()] * 3 + [vmem()] * 5 + [anywhere()] * 3,
        out_specs=(anywhere(),) * len(specs) + (vmem(),) * given,
        scratch_shapes=[
            pltpu.VMEM((in_ch, 3 * segments * frames), BF16),
            pltpu.VMEM((16, in_ch, ch), F32),
            pltpu.VMEM((2, 16, in_ch, ch), BF16),
            pltpu.VMEM((in_ch, LANES), F32),
            pltpu.VMEM((body + block_grads.shape[0], LANES), F32),
            pltpu.VMEM(vec_shape, F32),
            pltpu.VMEM((40, LANES), F32),
            pltpu.SemaphoreType.DMA((3,)),
            pltpu.SemaphoreType.DMA((len(specs), max(spec["slots"] for spec in specs))),
            pltpu.SemaphoreType.DMA((copy_count(specs),)),
        ],
        compiler_params=params(),
    )(scalars, numbers, slots, mel, gain, inverse, sums, back, high, low, block_grads)


def frames_back(scalars, mel, back, high, low):
    segments, frames, in_ch = mel.shape
    ch = high.shape[2]
    geo = {"segments": segments, "frames": frames}
    weight = pl.BlockSpec((1, in_ch, ch), lambda k: (k, 0, 0))
    return pl.pallas_call(
        functools.partial(frames_back_kernel, geo),
        grid=(16,),
        out_shape=shape(mel.shape),
        in_specs=[smem(), whole_spec(mel.shape), whole_spec(back.shape), weight, weight],
        out_specs=whole_spec(mel.shape),
        scratch_shapes=[pltpu.VMEM((segments * frames, in_ch), F32)],
        compiler_params=params(),
        cost_estimate=pl.CostEstimate(
            flops=6 * segments * frames * in_ch * 16 * ch,
            bytes_accessed=4 * 16 * in_ch * ch + 8 * mel.size + 4 * back.size,
            transcendentals=0,
        ),
    )(scalars, mel, back, high, low)


def line_edges(low, high, axis):
    count = math.prod(lax.axis_size(name) for name in axis)
    forward = [(i, i + 1) for i in range(count - 1)]
    backward = [(target, source) for source, target in forward]
    return lax.ppermute(high, axis, forward), lax.ppermute(low, axis, backward)


def packed_edges(mel, cot):
    ch = cot.shape[2]
    edges = []
    for frames, samples in (
        (mel[:, :EDGE_FRAMES], cot[:, :EDGE]),
        (mel[:, mel.shape[1] - EDGE_FRAMES :], cot[:, cot.shape[1] - EDGE :]),
    ):
        edges.append(cat([frames[:, :, :ch], frames[:, :, ch:], samples], 1))
    return edges


def moments(gradient, first, second):
    first_new = B_ONE * first + (1.0 - B_ONE) * gradient
    second_new = B_TWO * second + (1.0 - B_TWO) * gradient * gradient
    direction = (
        first_new / (1.0 - B_ONE**STEP) / (jnp.sqrt(second_new / (1.0 - B_TWO**STEP)) + EPSILON)
    )
    return (first_new, second_new, direction)


def total(value, groups):
    for group in groups:
        count = math.prod(lax.axis_size(name) for name in group)
        far = 1
        while far < count:
            near = min(4, count // far)
            terms = [value]
            for step in range(1, near):
                moves = [(i, i ^ (step * far)) for i in range(count)]
                terms.append(lax.ppermute(value, group, moves))
            while len(terms) > 1:
                terms = [one + other for one, other in zip(terms[::2], terms[1::2])]
            value = terms[0]
            far = near * far
    return value


FLIPS = {"wide": ("wide", 1), "deep": ("deep", 1), "near": ("line", 1), "far": ("line", 2), "core": ("core", 1)}
ORDERS = (("wide", "deep", "near", "far"), ("deep", "wide", "near", "far"), ("near", "far", "wide", "deep"))
LANE_ROWS = 8


def swap(value, flip):
    axis, step = FLIPS[flip]
    return lax.ppermute(value, axis, [(i, i ^ step) for i in range(lax.axis_size(axis))])


def owner_table(order, other_core):
    places = {name: lax.axis_index(name) for name in ("line", "deep", "wide", "core")}
    numbers = []
    for slot in range(16):
        here = dict(places)
        for bit, flip in enumerate(order):
            if slot >> (3 - bit) & 1:
                axis, step = FLIPS[flip]
                here[axis] = here[axis] ^ step
        core = here["core"] ^ other_core
        numbers.append(((here["line"] * 2 + here["deep"]) * 2 + here["wide"]) * 2 + core)
    return jnp.stack(numbers).astype(jnp.int32)


def slot_table(order, other_core, owners):
    numbers = jnp.arange(owners, dtype=jnp.int32)
    there = {"core": numbers % 2, "wide": numbers // 2 % 2, "deep": numbers // 4 % 2}
    there["line"] = numbers // 8
    away = {name: lax.axis_index(name).astype(jnp.int32) ^ place for name, place in there.items()}
    slot = jnp.zeros_like(numbers)
    for flip in order:
        axis, step = FLIPS[flip]
        slot = 2 * slot + (away[axis] // step) % 2
    return jnp.where(away["core"] == other_core, slot, -1)


def part_sizes(shard_rows):
    last = shard_rows * 11 // 48 // 8 * 8
    first = (shard_rows - last) // 16 * 8
    return (first, first, shard_rows - 2 * first)


def part_specs(sizes, rows, slots):
    specs = []
    offset = 0
    for part, size in enumerate(sizes):
        valid = min(size, rows - offset)
        specs.append(
            {
                "part": part,
                "slots": slots,
                "rows": size,
                "pitch": rows,
                "offset": offset,
                "valid": valid,
                "vec": valid if valid < size else -1,
            }
        )
        offset += size
    return specs


def together(*values):
    return lax.optimization_barrier(values)


def gather_by_permutes(shard, sizes, edges, tm):
    first, second, third = sizes
    both, last = shard[: first + second], shard[first + second :]
    far, near, last_deep, last_wide, edges = together(
        swap(both, "far"),
        swap(both, "near"),
        swap(last, "deep"),
        swap(last, "wide"),
        line_edges(*edges, tm),
    )
    near_far, last_both = together(swap(far, "near"), swap(last_deep, "wide"))
    parts = (both, far, near, near_far)
    a = cat([part[:first] for part in parts], 0)
    b = cat([part[first:] for part in parts], 0)
    c = cat([last, last_deep, last_wide, last_both], 0)
    a, b, c = together(a, b, c)
    a_deep, b_wide, c_far = swap(a, "deep"), swap(b, "wide"), swap(c, "far")
    c_near = swap(c, "near")
    a_deep, b_wide, c_far, c_near, a, b = together(a_deep, b_wide, c_far, c_near, a, b)
    c_both = swap(c_far, "near")
    a_both, b_both = swap(a_deep, "wide"), swap(b_wide, "deep")
    a_wide, b_deep = swap(a, "wide"), swap(b, "deep")
    ready = [(0, 0, a), (1, 0, b), (2, 0, c), (0, 1, a_deep), (1, 1, b_wide), (2, 1, c_far)]
    ready.append((2, 2, c_near))
    others = [swap(array, "core") for _, _, array in ready]
    a_both, b_both, a_wide, b_deep, c_both, others = together(
        a_both, b_both, a_wide, b_deep, c_both, others
    )
    held = [(n, quarter, 0, array) for n, quarter, array in ready]
    held += [(n, quarter, 1, array) for (n, quarter, _), array in zip(ready, others)]
    rest = [(0, 2, a_wide), (1, 2, b_deep), (0, 3, a_both), (1, 3, b_both), (2, 3, c_both)]
    for n, quarter, array in rest:
        held += [(n, quarter, 0, array), (n, quarter, 1, swap(array, "core"))]
    return held, edges


def scatter_by_permutes(mine, theirs, sizes, beside):
    came = [swap(value, "core") for value in theirs]
    terms = [[own, other] for own, other in zip(mine, came)]
    slots = 16
    for level in range(4):
        slots = slots // 2
        away = []
        for number, (part, size) in enumerate(zip(terms, sizes)):
            if level == 0 and number > 0:
                part[1], away[-1] = together(part[1], away[-1])
            away.append(sum(term[slots * size : 2 * slots * size] for term in part))
        came = [swap(value, order[level]) for value, order in zip(away, ORDERS)]
        if level == 0:
            came, other = together(came, beside())
        else:
            came = together(*came)
        for part, value in zip(terms, came):
            part.append(value)
    summed = cat([sum(term[:size] for term in part) for part, size in zip(terms, sizes)], 0)
    return summed, other


def by_owner(mine, theirs, plan):
    grid, core_dim = plan["grid"], plan["core_dim"]
    first = lax.axis_index("core") == 0
    parts = [jnp.where(first, mine, theirs), jnp.where(first, theirs, mine)]
    chips = [size for place, size in enumerate(grid) if place != core_dim]
    parts = [part.reshape(chips + list(mine.shape[1:])) for part in parts]
    return jnp.stack(parts, axis=core_dim).reshape((-1,) + mine.shape[1:])


def by_core(shards, plan):
    grid, core_dim = plan["grid"], plan["core_dim"]
    grouped = shards.reshape(tuple(grid) + shards.shape[1:])
    core = lax.axis_index("core")
    mine = lax.dynamic_index_in_dim(grouped, core, core_dim, keepdims=False)
    theirs = lax.dynamic_index_in_dim(grouped, 1 - core, core_dim, keepdims=False)
    after = (-1,) + shards.shape[1:]
    return mine.reshape(after), theirs.reshape(after)


def body(
    plan,
    mel_frames,
    lengths,
    cotangent,
    matrices,
    vectors,
    matrix_first,
    matrix_second,
    vector_first,
    vector_second,
):
    tm, every, chip_axes = plan["tm"], plan["every"], plan["chip_axes"]
    segments, frames, in_ch = mel_frames.shape
    ch = cotangent.shape[2]
    pieces = math.prod(lax.axis_size(name) for name in tm)
    rows = matrices.shape[0] // LANES
    shard_rows = -(-(rows + 2) // 48) * 48
    vec_count = vectors.shape[0]
    spare = shard_rows - rows - 2
    owners = math.prod(plan["grid"])
    geo = {"in_ch": in_ch, "ch": ch, "owners": owners, "vec_count": vec_count}
    vec_first = lax.axis_index(every) * vec_count % LANES
    placed = lax.dynamic_update_slice(jnp.zeros((2 * LANES,), F32), vectors, (vec_first,))
    shard = jnp.concatenate(
        [
            matrices.reshape(rows, LANES),
            placed.reshape(2, LANES),
            jnp.zeros((spare, LANES), F32),
        ]
    )
    edges = packed_edges(mel_frames, cotangent)
    cubic = rows % 8 == 0 and plan["grid"] == (4, 2, 2, 2)
    sizes = part_sizes(shard_rows)
    if cubic:
        specs = part_specs(sizes, rows, 16)
        numbers = [[owner_table(order, core) for order in ORDERS] for core in range(2)]
        held, edges = gather_by_permutes(shard, sizes, edges, tm)
        held_numbers = jnp.concatenate(
            [numbers[c][n][4 * quarter : 4 * quarter + 4] for n, quarter, c, _ in held]
        )
        held_specs = [dict(specs[n], slots=4) for n, _, _, _ in held]
        held = [array for _, _, _, array in held]
        given = []
    else:
        edges = line_edges(*edges, tm)
        mine = lax.all_gather(shard, chip_axes, axis=0, tiled=False)
        gathered = by_owner(mine, swap(mine, "core"), plan)
        held = [gathered[:, :rows].reshape(-1, LANES)]
        whole = held[0].shape[0]
        specs = [
            {
                "part": 0,
                "slots": 1,
                "rows": whole,
                "pitch": 0,
                "offset": 0,
                "valid": whole,
                "vec": -1,
            }
        ]
        held_specs, held_numbers = specs, jnp.zeros((1,), jnp.int32)
        vec_rows = jnp.pad(gathered[:, rows : rows + 2], ((0, 0), (0, LANE_ROWS - 2), (0, 0)))
        given = [vec_rows.reshape(-1, LANES)]
    mel_parts = (edges[0], mel_frames, edges[1])
    cot_parts = (edges[0], cotangent, edges[1])
    scalars = jnp.concatenate(
        [lengths[0], jnp.stack([lax.axis_index(tm), jnp.int32(pieces)]).astype(jnp.int32)]
    )
    up_high, up_low, *mats, short, inverse, gain, items, squares = prepare(
        held, held_specs, held_numbers, given, geo
    )
    start = upsample(scalars, mel_parts, items, up_high, up_low, pieces * frames)
    waveform, back, block_grads, sums = blocks(scalars, items, start, cot_parts, *mats, short)
    if cubic:
        out_specs = specs * 2
        out_numbers = jnp.concatenate(numbers[0] + numbers[1])
        out_slots = jnp.concatenate(
            [slot_table(order, core, owners) for core in range(2) for order in ORDERS]
        )
    else:
        out_specs, out_numbers, out_slots = held_specs, held_numbers, held_numbers
    grads = weight_back(
        scalars,
        mel_frames,
        gain,
        inverse,
        sums,
        back,
        up_high,
        up_low,
        block_grads,
        out_specs,
        out_numbers,
        out_slots,
        geo,
    )
    if cubic:
        summed, frames_grad = scatter_by_permutes(
            grads[:3],
            grads[3:],
            sizes,
            lambda: frames_back(scalars, mel_frames, back, up_high, up_low),
        )
    else:
        vec_rows = grads[1].reshape(owners, LANE_ROWS, LANES)[:, :2]
        shards = jnp.concatenate(
            [
                grads[0].reshape(owners, rows, LANES),
                vec_rows,
                jnp.zeros((owners, spare, LANES), F32),
            ],
            axis=1,
        )
        mine, theirs = by_core(shards, plan)
        mine = mine + swap(theirs, "core")
        summed = lax.psum_scatter(mine, chip_axes, scatter_dimension=0, tiled=True)[0]
        frames_grad = frames_back(scalars, mel_frames, back, up_high, up_low)
    matrix_grad = summed[:rows]
    vec_rows = summed[rows : rows + 2].reshape(-1)
    vector_grad = lax.dynamic_slice(vec_rows, (vec_first,), (vec_count,))

    shapes, starts, whole = layout(in_ch, ch)
    matrices = matrices.reshape(rows, LANES)
    position = lax.axis_index(every) * rows + jnp.arange(rows, dtype=jnp.int32)
    lower = jnp.array([first // LANES for first in starts], jnp.int32)
    upper = jnp.array([first // LANES for first in starts[1:] + [whole]], jnp.int32)
    member = (position[:, None] >= lower[None, :]) & (position[:, None] < upper[None, :])
    member = member.astype(F32)
    matrix_first_new, matrix_second_new, direction = moments(
        matrix_grad, matrix_first.reshape(rows, LANES), matrix_second.reshape(rows, LANES)
    )
    update = direction + DECAY * matrices
    update_sq = jnp.sum(member * jnp.sum(update * update, axis=1)[:, None], axis=0)
    update_sq = total(update_sq, (("core",), ("deep", "wide"), ("line",)))
    weight_norm = jnp.sqrt(jnp.sum(squares[:10], axis=1))
    update_norm = jnp.sqrt(update_sq)
    trust = weight_norm / update_norm
    row_trust = jnp.sum(member * trust[None, :], axis=1)
    new_matrices = (matrices - RATE * row_trust[:, None] * update).reshape(-1)
    vector_first_new, vector_second_new, vector_step = moments(
        vector_grad, vector_first, vector_second
    )
    new_vectors = vectors - RATE * vector_step
    norm_table = jnp.stack([weight_norm, update_norm])
    return (
        waveform,
        frames_grad,
        new_matrices,
        new_matrices.astype(BF16),
        matrix_first_new.reshape(-1),
        matrix_second_new.reshape(-1),
        new_vectors,
        new_vectors.astype(BF16),
        vector_first_new,
        vector_second_new,
        norm_table,
    )


def make_plan(mesh):
    tm, batch = mesh.shape["tm"], mesh.shape["batch"]
    if tm > 4:
        root = math.isqrt(batch)
        grid = (tm // 2, 2, root, batch // root)
        names = ("line", "core", "deep", "wide")
        tm_axes, batch_axes = ("line", "core"), ("deep", "wide")
        core_dim = 1
    else:
        root = math.isqrt(batch // 2)
        grid = (tm, root, batch // 2 // root, 2)
        names = ("line", "deep", "wide", "core")
        tm_axes, batch_axes = ("line",), ("deep", "wide", "core")
        core_dim = 3
    inner = Mesh(mesh.devices.reshape(grid), names)
    plan = {
        "tm": tm_axes,
        "batch": batch_axes,
        "every": names,
        "grid": grid,
        "core_dim": core_dim,
        "chip_axes": tuple(name for name in names if name != "core"),
    }
    return inner, plan


def solution(mesh):
    inner, plan = make_plan(mesh)
    tm, batch, every = plan["tm"], plan["batch"], plan["every"]
    pieces, flat = P(batch, tm, None), P(every)
    in_specs = (pieces, P(batch, None), pieces, flat, flat, flat, flat, flat, flat)
    out_specs = (pieces, pieces, flat, flat, flat, flat, flat, flat, flat, flat, P())
    return jax.shard_map(
        functools.partial(body, plan),
        mesh=inner,
        in_specs=in_specs,
        out_specs=out_specs,
        check_vma=False,
    )
```

```python
import functools
import math

import jax
import jax.numpy as jnp
from jax import lax
from jax.experimental import pallas as pl
from jax.experimental.pallas import tpu as pltpu
from jax.sharding import Mesh
from jax.sharding import PartitionSpec as P

STEP = 5
B_ONE = 0.5
B_TWO = 0.5
EPSILON = 1e-06
RATE = 0.5
DECAY = 0.01
LANES = 128
EDGE_FRAMES = 8
EDGE = 32
PAD = 16
VMEM_LIMIT = 60 * 1024 * 1024
BF16 = jnp.bfloat16
F32 = jnp.float32


def soft_leaky(value):
    small = jnp.exp2(jnp.abs(value) * (-1.0 / math.log(2.0)))
    return jnp.maximum(value, 0.2 * value) + (0.8 * math.log(2.0)) * jnp.log2(1.0 + small)


def leaky_slope(value):
    return 0.6 + 0.4 * jnp.tanh(0.5 * value)


def split(value):
    high = value.astype(BF16)
    return high, (value - high.astype(F32)).astype(BF16)


def cat(parts, axis):
    return jnp.concatenate(parts, axis=axis)


def dot(left, right, dims=((1,), (0,))):
    return lax.dot_general(left, right, (dims, ((), ())), preferred_element_type=F32)


ROWS_COLS = ((1,), (0,))
ROWS_ROWS = ((1,), (1,))
COLS_COLS = ((0,), (0,))


def layout(in_channels, channels):
    shapes = [(in_channels, 16, channels)]
    for _ in range(3):
        shapes = shapes + [(3, channels, channels), (channels, channels), (channels, channels)]
    starts = []
    position = 0
    for shape in shapes:
        starts.append(position)
        position = position + math.prod(shape)
    return (shapes, starts, position)


def start_all(copies):
    for copy in copies:
        copy.start()


def wait_all(copies):
    for copy in copies:
        copy.wait()


def piece_copies(specs, numbers, pieces, flat, vecs, sem, vec_sem, outward):
    copies, vec_copies = [], []
    at = 0

    def move(one, other, signal):
        source, target = (other, one) if outward else (one, other)
        return pltpu.make_async_copy(source, target, signal)

    for spec, piece in zip(specs, pieces):
        for slot in range(spec["slots"]):
            owner = numbers[at]
            first = slot * spec["rows"]
            place = pl.multiple_of(owner * spec["pitch"] + spec["offset"], 8)
            signal = sem.at[at] if outward else sem.at[spec["part"], owner]
            copies.append(
                move(
                    piece.at[pl.ds(first, spec["valid"])],
                    flat.at[pl.ds(place, spec["valid"])],
                    signal,
                )
            )
            if spec["vec"] >= 0:
                place = pl.multiple_of(owner * 8, 8)
                vec_copies.append(
                    move(
                        piece.at[pl.ds(first + spec["vec"], 8)],
                        vecs.at[pl.ds(place, 8)],
                        vec_sem.at[at],
                    )
                )
            at += 1
    return copies, vec_copies


def copy_count(specs):
    return sum(spec["slots"] for spec in specs)


def prepare_kernel(geo, *refs):
    specs, in_ch, ch = geo["specs"], geo["in_ch"], geo["ch"]
    count = len(specs)
    numbers = refs[0]
    pieces = refs[1 : 1 + count]
    given = refs[1 + count : 1 + count + geo["given"]]
    outs = refs[1 + count + geo["given"] :]
    short, inverse, gains, items, squares = outs[6:11]
    flat, scratch, full, sem, vec_sem = outs[11:16]
    up_high, up_low, mat_high, mat_low, turn_high, turn_low = outs[16:22]
    up_sem, mat_sem = outs[22:]

    def up_copies(i):
        span = pl.ds(pl.multiple_of(i * 16, 16), 16)
        pairs = zip(outs[:2], (up_high, up_low))
        return [
            pltpu.make_async_copy(made.at[:, span], out.at[:, span], up_sem.at[n, i])
            for n, (out, made) in enumerate(pairs)
        ]

    def mat_copies(b):
        pairs = zip(outs[2:6], (mat_high, mat_low, turn_high, turn_low))
        return [
            pltpu.make_async_copy(made.at[b], out.at[b], mat_sem.at[n, b])
            for n, (out, made) in enumerate(pairs)
        ]
    vecs = given[0] if geo["given"] else scratch
    copies, vec_copies = piece_copies(specs, numbers, pieces, flat, scratch, sem, vec_sem, False)
    start_all(vec_copies)
    start_all(copies)
    parts = {spec["part"]: spec for spec in specs}
    pitch = specs[0]["pitch"] or flat.shape[0]

    def wait_for(owner):
        for part, spec in parts.items():
            span = pl.ds(0, spec["valid"])
            pltpu.make_async_copy(pieces[0].at[span], flat.at[span], sem.at[part, owner]).wait()

    wait_all(vec_copies)
    full[...] = jnp.zeros_like(full)
    for owner in range(geo["owners"]):
        row = owner * geo["vec_count"] // LANES
        full[row : row + 2] += vecs[8 * owner : 8 * owner + 2]
    columns = full[0:8].T
    gain = cat([columns[:, j : j + 1] for j in range(in_ch // LANES)], 0)
    gains[...] = jnp.broadcast_to(gain, gains.shape)
    items[...] = jnp.zeros_like(items)
    per_row = ch // LANES
    for i in range(13):
        for part in range(per_row):
            row = in_ch // LANES + per_row * i + part
            items[i : i + 1, part * LANES : (part + 1) * LANES] = full[row : row + 1]
    wide = 16 * ch // LANES
    squares[...] = jnp.zeros_like(squares)
    group = 16

    def channels(i, carry):
        first = i * (group * wide)
        now = (first + group * wide - 1) // pitch

        @pl.when((i == 0) | (now > (first - 1) // pitch))
        def _():
            wait_for(now)

        block = flat[pl.ds(pl.multiple_of(first, group * wide), group * wide), :]
        block = jnp.swapaxes(block.reshape(group, wide, LANES), 0, 1)
        square = jnp.sum(block * block, axis=0)
        squares[0:1, :] += jnp.sum(square, axis=0, keepdims=True)
        inv = lax.rsqrt(jnp.sum(square, axis=1, keepdims=True))
        span = pl.ds(pl.multiple_of(i * group, group), group)
        inverse[span, :] = jnp.broadcast_to(inv, (group, LANES))
        scale = gains[span, 0:1] * inv
        for place in range(wide):
            high, low = split(block[place] * scale)
            lanes = slice(place % 2 * LANES, place % 2 * LANES + LANES)
            up_high[place // 2, span, lanes] = high
            up_low[place // 2, span, lanes] = low
        start_all(up_copies(i))
        return carry

    lax.fori_loop(0, in_ch // group, channels, 0)
    for owner in range((in_ch * wide - 1) // pitch + 1, flat.shape[0] // pitch):
        wait_for(owner)
    base = in_ch * wide
    step = ch * ch // LANES
    for block in range(3):
        for number in range(5):
            first = base + (block * 5 + number) * step
            value = cat(
                [flat[pl.ds(first + part, ch, stride=per_row), :] for part in range(per_row)], 1
            )
            column = jnp.sum(value * value, axis=0, keepdims=True)
            which = 1 + 3 * block + max(number - 2, 0)
            squares[which : which + 1, :] += column[:, :LANES] + column[:, LANES:]
            if number == 4:
                short[block, 0:ch] = value
                root = lax.rsqrt(column)
                short[block, ch : ch + 8] = jnp.broadcast_to(root, (8, ch))
                value = value * (items[3 + 4 * block : 4 + 4 * block, :] * root)
            high, low = split(value)
            mat_high[block, number] = high
            mat_low[block, number] = low
            high, low = split(value.T)
            turn_high[block, number] = high
            turn_low[block, number] = low
        start_all(mat_copies(block))

    def finish(i, carry):
        wait_all(up_copies(i))
        return carry

    lax.fori_loop(0, in_ch // group, finish, 0)
    for block in range(3):
        wait_all(mat_copies(block))


def upsample_kernel(
    geo,
    scalars,
    mel_low,
    mel,
    mel_high,
    bias,
    mid_high,
    mid_low,
    side_high,
    side_low,
    out,
    wide,
    mid,
    sides,
):
    segments, frames, ahead = geo["segments"], geo["frames"], geo["ahead"]
    step = pl.program_id(0)
    kept = frames + 2 * (EDGE // 8)
    size = kept + 8
    in_ch = mel.shape[2]

    @pl.when(step == 0)
    def _():
        rows = frames + 2 * EDGE_FRAMES
        wide[...] = jnp.zeros_like(wide)
        place = scalars[segments] * frames - EDGE_FRAMES
        place = place + lax.broadcasted_iota(jnp.int32, (rows, 1), 0)
        inside = ((place >= 0) & (place < ahead)).astype(F32)
        for s in range(segments):
            live = (place < scalars[s]).astype(F32)
            first = 0
            for part in (mel_low, mel, mel_high):
                value = part[s]
                if part is not mel:
                    value = cat([value[0:EDGE_FRAMES], value[EDGE_FRAMES : 2 * EDGE_FRAMES]], 1)
                span = slice(first, first + value.shape[0])
                wide[s, span] = soft_leaky(value * live[span]) * inside[span]
                first = span.stop
        for s in range(segments):
            span = slice(s * size, (s + 1) * size)
            first = EDGE_FRAMES - EDGE // 8
            for target, shift in ((mid, 0), (sides.at[0], -1), (sides.at[1], 1)):
                high, low = split(wide[s, first + shift : first + shift + size])
                target[0, span] = high
                target[1, span] = low

    side = step // 2
    left_high = cat([mid[0], sides[side, 0]], 1)
    left_low = cat([mid[1], sides[side, 1]], 1)
    left = cat([left_high, left_low, left_high], 1)
    for n in range(mid_high.shape[0]):
        right_high = cat([mid_high[n], side_high[n]], 0)
        right_low = cat([mid_low[n], side_low[n]], 0)
        value = dot(left, cat([right_high, right_high, right_low], 0)) + bias[0:1, :]
        place = step * mid_high.shape[0] + n
        for s in range(segments):
            for half in range(out.shape[1]):
                out[s, half, pl.ds(place, kept, stride=8), :] = value[
                    s * size : s * size + kept, half * LANES : (half + 1) * LANES
                ]


def blocks_kernel(
    geo,
    scalars,
    items,
    start,
    cot_low,
    cot,
    cot_high,
    mat_high,
    mat_low,
    turn_high,
    turn_low,
    short,
    wave,
    back,
    grads,
    sums,
    hidden,
    middle,
    padded,
    triple,
    act,
    mid_act,
    hid,
    flow,
    flow_pair,
    dil_acc,
    pair_acc,
):
    segments, ch, samples = geo["segments"], geo["ch"], geo["samples"]
    rows = samples + 2 * EDGE
    count = geo["tiles"]
    tile = rows // count
    tiles = [slice(r, r + tile) for r in range(0, rows, tile)]
    own = slice(EDGE, EDGE + samples)
    segment = pl.program_id(0)
    piece = scalars[segments]
    low_edge = jnp.where(piece > 0, 1.0, 0.0)
    high_edge = jnp.where(piece < scalars[segments + 1] - 1, 1.0, 0.0)
    position = piece * samples - EDGE + lax.broadcasted_iota(jnp.int32, (rows, 1), 0)
    live = position < 8 * scalars[segment]

    @pl.when(segment == 0)
    def _():
        for n in range(2):
            padded[n, 0:PAD] = jnp.zeros((PAD, ch), F32)
            padded[n, PAD + rows : PAD + rows + PAD] = jnp.zeros((PAD, ch), F32)
        dil_acc[...] = jnp.zeros_like(dil_acc)
        pair_acc[...] = jnp.zeros_like(pair_acc)
        sums[...] = jnp.zeros_like(sums)

    def put_padded(n, t, value):
        first, last = PAD + t * tile, PAD + (t + 1) * tile
        if t == 0:
            padded[n, first : first + EDGE] = value[:EDGE] * low_edge
            value, first = value[EDGE:], first + EDGE
        if t == count - 1:
            padded[n, last - EDGE : last] = value[value.shape[0] - EDGE :] * high_edge
            value, last = value[: value.shape[0] - EDGE], last - EDGE
        padded[n, first:last] = value

    def shift(n, t, gap):
        for k in range(3):
            first = PAD + t * tile + (k - 1) * gap
            high, low = split(padded[n, first : first + tile])
            triple[n, 0, tiles[t], k * ch : (k + 1) * ch] = high
            triple[n, 1, tiles[t], k * ch : (k + 1) * ch] = low

    def operand(parts, axis):
        high, low = parts
        return cat([high, high, low] if axis == 0 else [high, low, high], axis)

    def stack(refs, b, numbers):
        return [cat([ref[b, number] for number in numbers], 0) for ref in refs]

    weights = (mat_high, mat_low)
    turned = (turn_high, turn_low)

    def activate(b, t):
        value = hidden[b, tiles[t]]
        put_padded(b % 2, t, soft_leaky(value))
        hid[b, 0, tiles[t]], hid[b, 1, tiles[t]] = split(value)

    def widen(b, t):
        shift(b % 2, t, 3**b)
        act[b, :, tiles[t]] = triple[b % 2, :, tiles[t], ch : 2 * ch]

    def dilated(b, t):
        left = operand([triple[b % 2, n, tiles[t]] for n in range(2)], 1)
        right = operand(stack(weights, b, range(3)), 0)
        middle[b, tiles[t]] = dot(left, right) + items[1 + 4 * b : 2 + 4 * b, :]

    def bend(b, t):
        mid_act[b, 0, tiles[t]], mid_act[b, 1, tiles[t]] = split(soft_leaky(middle[b, tiles[t]]))

    def leave(b, t):
        left = cat(
            [
                operand([mid_act[b, n, tiles[t]] for n in range(2)], 1),
                operand([hid[b, n, tiles[t]] for n in range(2)], 1),
            ],
            1,
        )
        right = cat([operand(stack(weights, b, [number]), 0) for number in (3, 4)], 0)
        offset = items[2 + 4 * b : 3 + 4 * b, :] + items[4 + 4 * b : 5 + 4 * b, :]
        hidden[b + 1, tiles[t]] = dot(left, right) + offset

    for t in range(count):
        hidden[0, tiles[t]] = cat([start[0, half, tiles[t]] for half in range(start.shape[1])], 1)
        activate(0, t)
    for b in range(3):
        for t in range(count + 2):
            if t < count:
                widen(b, t)
                dilated(b, t)
            if 1 <= t <= count:
                bend(b, t - 1)
            if t >= 2:
                leave(b, t - 2)
                if b < 2:
                    activate(b + 1, t - 2)
    wave[0] = jnp.where(live[own], hidden[3, own], 0.0)
    first = 0
    for part in (cot_low[:, 2 * EDGE_FRAMES :], cot, cot_high[:, 2 * EDGE_FRAMES :]):
        span = slice(first, first + part.shape[1])
        flow[span] = jnp.where(live[span], part[0], 0.0)
        first = span.stop

    def part_flow(b, t):
        high, low = split(flow[tiles[t]])
        flow_pair[b % 2, 0, tiles[t]] = high
        flow_pair[b % 2, 1, tiles[t]] = low

    def inner(b, t):
        left = operand([flow_pair[b % 2, n, tiles[t]] for n in range(2)], 1)
        value = dot(left, operand(stack(turned, b, [3]), 0))
        put_padded(b % 2, t, value * leaky_slope(middle[b, tiles[t]]))

    def outer(b, t):
        left = operand([triple[b % 2, n, tiles[t]] for n in range(2)], 1)
        value = dot(left, operand(stack(turned, b, range(3)), 0))
        left = operand([flow_pair[b % 2, n, tiles[t]] for n in range(2)], 1)
        short_part = dot(left, operand(stack(turned, b, [4]), 0))
        flow[tiles[t]] = value * leaky_slope(hidden[b, tiles[t]]) + short_part

    def biases(b):
        body = padded[b % 2, PAD + EDGE : PAD + EDGE + samples]
        sums[8 * b : 8 * b + 1, :] += jnp.sum(body, axis=0, keepdims=True)
        sums[8 * b + 1 : 8 * b + 2, :] += jnp.sum(flow[own], axis=0, keepdims=True)

    def pair_weights(b):
        left = cat([flow_pair[b % 2, n, own].T for n in range(2)], 0)
        right = [cat([mid_act[b, n, own], hid[b, n, own]], 1) for n in range(2)]
        value = dot(left, right[0])
        pair_acc[b] += value[0:ch] + value[ch : 2 * ch] + dot(left[0:ch], right[1])

    def dilated_weights(b):
        left = cat([act[b, n, own].T for n in range(2)], 0)
        value = dot(left, triple[b % 2, 0, own])
        value = value[0:ch] + value[ch : 2 * ch]
        dil_acc[b] += value + dot(left[0:ch], triple[b % 2, 1, own])

    def backward_shift(b, t):
        shift(b % 2, t, -(3**b))

    for t in range(count):
        part_flow(2, t)
    for b in (2, 1, 0):
        for t in range(count):
            inner(b, t)
        pair_weights(b)
        backward_shift(b, 0)
        biases(b)
        for t in range(count):
            if t + 1 < count:
                backward_shift(b, t + 1)
            outer(b, t)
            if b > 0 and t >= 1:
                part_flow(b - 1, t - 1)
        dilated_weights(b)
        if b > 0:
            part_flow(b - 1, count - 1)
    flow[0:EDGE] = flow[0:EDGE] * low_edge
    flow[rows - EDGE : rows] = flow[rows - EDGE : rows] * high_edge
    sums[24:25, :] += jnp.sum(flow[own], axis=0, keepdims=True)
    for half in range(back.shape[1]):
        back[0, half] = flow[:, half * LANES : (half + 1) * LANES]

    @pl.when(segment == segments - 1)
    def _():
        step = ch * ch // LANES
        per_row = ch // LANES

        def put(number, value):
            for part in range(per_row):
                grads[pl.ds(number * step + part, ch, stride=per_row), :] = value[
                    :, part * LANES : (part + 1) * LANES
                ]

        for b in range(3):
            for k in range(3):
                put(5 * b + k, dil_acc[b, :, k * ch : (k + 1) * ch])
            put(5 * b + 3, pair_acc[b, :, 0:ch].T)
            whole = pair_acc[b, :, ch : 2 * ch].T
            inv = short[b, ch : ch + 1]
            direction = short[b, 0:ch] * inv
            along = jnp.sum(whole * direction, axis=0, keepdims=True)
            sums[8 * b + 2 : 8 * b + 3, :] = along
            gain = items[3 + 4 * b : 4 + 4 * b, :]
            put(5 * b + 4, gain * inv * (whole - along * direction))


def tap_window(back, tap, segments, frames):
    first = EDGE - 4 + tap
    halves = range(back.shape[1])
    return cat(
        [
            cat([back[s, half, pl.ds(first, frames, stride=8), :] for half in halves], 1)
            for s in range(segments)
        ],
        0,
    )


def weight_back_kernel(
    geo, scalars, numbers, slots, mel, gain, inverse, sums, back, high, low, blocks, *refs
):
    specs, segments, frames = geo["specs"], geo["segments"], geo["frames"]
    count = len(specs)
    pieces = refs[:count]
    outs = refs[count:]
    extra = outs[0] if geo["given"] else None
    turned, whole, kept, slope, flat, scratch, full, block_sem, sem, vec_sem = outs[geo["given"] :]
    vecs = extra if geo["given"] else scratch
    in_ch = mel.shape[2]
    ch = high.shape[2]
    wide = 16 * ch // LANES
    body = in_ch * wide
    pitch = specs[0]["pitch"] or flat.shape[0]
    owners = flat.shape[0] // pitch
    loads = [
        pltpu.make_async_copy(blocks, flat.at[pl.ds(body, blocks.shape[0])], block_sem.at[0]),
        pltpu.make_async_copy(high, kept.at[0], block_sem.at[1]),
        pltpu.make_async_copy(low, kept.at[1], block_sem.at[2]),
    ]
    start_all(loads)

    def send(owner):
        for number, (spec, piece) in enumerate(zip(specs, pieces)):

            @pl.when(slots[number * owners + owner] >= 0)
            def _():
                slot = slots[number * owners + owner]
                first = pl.multiple_of(slot * spec["rows"], 8)
                place = pl.multiple_of(owner * pitch + spec["offset"], 8)
                pltpu.make_async_copy(
                    flat.at[pl.ds(place, spec["valid"])],
                    piece.at[pl.ds(first, spec["valid"])],
                    sem.at[number, slot],
                ).start()

    def send_each(first, last):
        def step(owner, carry):
            send(owner)
            return carry

        lax.fori_loop(first, last, step, 0)

    place = scalars[segments] * frames + lax.broadcasted_iota(jnp.int32, (frames, 1), 0)
    for s in range(segments):
        live = (place < scalars[s]).astype(F32)
        upper, lower = split(soft_leaky(mel[s] * live).T)
        for part, piece in enumerate((upper, lower, upper)):
            first = (part * segments + s) * frames
            turned[:, first : first + frames] = piece

    def taps(tap, carry):
        upper, lower = split(tap_window(back, tap, segments, frames))
        whole[tap] = dot(turned[...], cat([upper, upper, lower], 0))
        return carry

    lax.fori_loop(0, 16, taps, 0)
    wait_all(loads)
    shared = body // pitch
    send_each(-(-body // pitch), owners)
    group = 16

    def channels(i, carry):
        span = pl.ds(pl.multiple_of(i * group, group), group)
        along = jnp.zeros((group, ch), F32)
        for tap in range(16):
            raw = kept[0, tap, span].astype(F32) + kept[1, tap, span].astype(F32)
            along = along + raw * whole[tap, span]
        factor = gain[span, 0:1]
        column = jnp.sum(along, axis=1, keepdims=True) / factor
        slope[span] = jnp.broadcast_to(column, (group, LANES))
        inv = inverse[span, 0:1]
        scale = factor * inv
        turn = inv * column
        values = []
        for tap in range(16):
            raw = kept[0, tap, span].astype(F32) + kept[1, tap, span].astype(F32)
            value = scale * whole[tap, span] - turn * raw
            for half in range(ch // LANES):
                values.append(value[:, half * LANES : (half + 1) * LANES])
        block = jnp.swapaxes(jnp.stack(values), 0, 1).reshape(group * wide, LANES)
        first = pl.multiple_of(i * (group * wide), group * wide)
        flat[pl.ds(first, group * wide), :] = block
        done = (first + group * wide) // pitch

        @pl.when(done > first // pitch)
        def _():
            send(done - 1)

        return carry

    lax.fori_loop(0, in_ch // group, channels, 0)
    if body % pitch:
        send(shared)
    for j in range(in_ch // LANES):
        full[j : j + 1] = slope[j * LANES : (j + 1) * LANES].T[0:1]
    order = [24]
    for b in range(3):
        order += [8 * b, 8 * b + 1, 8 * b + 2, 8 * b + 1]
    row = in_ch // LANES
    for number in order:
        for part in range(ch // LANES):
            full[row : row + 1] = sums[number : number + 1, part * LANES : (part + 1) * LANES]
            row += 1
    vecs[...] = jnp.zeros_like(vecs)
    for owner in range(geo["owners"]):
        row = owner * geo["vec_count"] // LANES
        vecs[8 * owner : 8 * owner + 2] = full[row : row + 2]
    _, vec_copies = piece_copies(specs, numbers, pieces, flat, scratch, vec_sem, vec_sem, True)
    start_all(vec_copies)
    for number, (spec, piece) in enumerate(zip(specs, pieces)):
        for slot in range(spec["slots"]):
            pltpu.make_async_copy(
                flat.at[pl.ds(0, spec["valid"])],
                piece.at[pl.ds(slot * spec["rows"], spec["valid"])],
                sem.at[number, slot],
            ).wait()
    wait_all(vec_copies)


def frames_back_kernel(geo, scalars, mel, back, high, low, out, total):
    segments, frames = geo["segments"], geo["frames"]
    step = pl.program_id(0)

    @pl.when(step == 0)
    def _():
        total[...] = jnp.zeros_like(total)

    upper, lower = split(tap_window(back, step, segments, frames))
    total[...] += dot(
        cat([upper, lower, upper], 1), cat([high[0], high[0], low[0]], 1), ROWS_ROWS
    )

    @pl.when(step == pl.num_programs(0) - 1)
    def _():
        place = scalars[segments] * frames + lax.broadcasted_iota(jnp.int32, (frames, 1), 0)
        for s in range(segments):
            live = (place < scalars[s]).astype(F32)
            value = total[s * frames : (s + 1) * frames]
            out[s] = value * leaky_slope(mel[s] * live) * live


def whole_spec(shape):
    return pl.BlockSpec(shape, lambda *_: (0,) * len(shape))


def vmem():
    return pl.BlockSpec(memory_space=pltpu.VMEM)


def smem():
    return pl.BlockSpec(memory_space=pltpu.SMEM)


def anywhere():
    return pl.BlockSpec(memory_space=pl.ANY)


def shape(dims, dtype=F32):
    return jax.ShapeDtypeStruct(dims, dtype)


def params():
    return pltpu.CompilerParams(vmem_limit_bytes=VMEM_LIMIT)


def prepare(pieces, specs, numbers, given, geo):
    in_ch, ch = geo["in_ch"], geo["ch"]
    entries = (in_ch * 16 * ch + 15 * ch * ch) // LANES
    geo = dict(geo, specs=specs, given=len(given))
    return pl.pallas_call(
        functools.partial(prepare_kernel, geo),
        out_shape=(
            shape((16, in_ch, ch), BF16),
            shape((16, in_ch, ch), BF16),
            shape((3, 5, ch, ch), BF16),
            shape((3, 5, ch, ch), BF16),
            shape((3, 5, ch, ch), BF16),
            shape((3, 5, ch, ch), BF16),
            shape((3, ch + 8, ch)),
            shape((in_ch, LANES)),
            shape((in_ch, LANES)),
            shape((16, ch)),
            shape((16, LANES)),
        ),
        in_specs=[smem()] + [anywhere()] * len(pieces) + [vmem()] * len(given),
        out_specs=(anywhere(),) * 6 + (vmem(),) * 5,
        scratch_shapes=[
            pltpu.VMEM((entries, LANES), F32),
            pltpu.VMEM((8 * geo["owners"], LANES), F32),
            pltpu.VMEM((40, LANES), F32),
            pltpu.SemaphoreType.DMA((3, geo["owners"])),
            pltpu.SemaphoreType.DMA((copy_count(specs),)),
            pltpu.VMEM((16, in_ch, ch), BF16),
            pltpu.VMEM((16, in_ch, ch), BF16),
        ]
        + [pltpu.VMEM((3, 5, ch, ch), BF16)] * 4
        + [
            pltpu.SemaphoreType.DMA((2, in_ch // 16)),
            pltpu.SemaphoreType.DMA((4, 3)),
        ],
        compiler_params=params(),
    )(numbers, *pieces, *given)


def upsample(scalars, mel_parts, items, up_high, up_low, ahead):
    segments, frames, in_ch = mel_parts[1].shape
    ch = up_high.shape[2]
    kept = frames + 2 * (EDGE // 8)
    size = kept + 8
    geo = {"segments": segments, "frames": frames, "ahead": ahead}
    out = (segments, ch // LANES, 8 * kept, LANES)
    return pl.pallas_call(
        functools.partial(upsample_kernel, geo),
        grid=(4,),
        out_shape=shape(out),
        in_specs=[smem()]
        + [whole_spec(part.shape) for part in mel_parts]
        + [
            whole_spec(items.shape),
            pl.BlockSpec((2, in_ch, ch), lambda j: (j + 2, 0, 0)),
            pl.BlockSpec((2, in_ch, ch), lambda j: (j + 2, 0, 0)),
            pl.BlockSpec((2, in_ch, ch), lambda j: ((j + 6) % 8, 0, 0)),
            pl.BlockSpec((2, in_ch, ch), lambda j: ((j + 6) % 8, 0, 0)),
        ],
        out_specs=whole_spec(out),
        scratch_shapes=[
            pltpu.VMEM((segments, frames + 2 * EDGE_FRAMES + 16, in_ch), F32),
            pltpu.VMEM((2, segments * size, in_ch), BF16),
            pltpu.VMEM((2, 2, segments * size, in_ch), BF16),
        ],
        compiler_params=params(),
    )(scalars, *mel_parts, items, up_high, up_low, up_high, up_low)


def blocks(scalars, items, start, cot_parts, mat_high, mat_low, turn_high, turn_low, short):
    segments, samples, ch = cot_parts[1].shape
    rows = samples + 2 * EDGE
    geo = {"segments": segments, "samples": samples, "ch": ch, "tiles": 4}
    halves = start.shape[1]
    flat = (15 * ch * ch // LANES, LANES)
    once = pl.Buffered(1)

    def fixed(dims):
        return pl.BlockSpec(dims, lambda s: (0,) * len(dims), pipeline_mode=once)

    return pl.pallas_call(
        functools.partial(blocks_kernel, geo),
        grid=(segments,),
        out_shape=(
            shape((segments, samples, ch)),
            shape((segments, halves, rows, LANES)),
            shape(flat),
            shape((32, ch)),
        ),
        in_specs=[
            smem(),
            fixed(items.shape),
            pl.BlockSpec((1, halves, rows, LANES), lambda s: (s, 0, 0, 0)),
        ]
        + [pl.BlockSpec((1,) + part.shape[1:], lambda s: (s, 0, 0)) for part in cot_parts]
        + [
            fixed(mat_high.shape),
            fixed(mat_low.shape),
            fixed(turn_high.shape),
            fixed(turn_low.shape),
            fixed(short.shape),
        ],
        out_specs=(
            pl.BlockSpec((1, samples, ch), lambda s: (s, 0, 0)),
            pl.BlockSpec((1, halves, rows, LANES), lambda s: (s, 0, 0, 0)),
            pl.BlockSpec(flat, lambda s: (0, 0), pipeline_mode=once),
            pl.BlockSpec((32, ch), lambda s: (0, 0)),
        ),
        scratch_shapes=[
            pltpu.VMEM((4, rows, ch), F32),
            pltpu.VMEM((3, rows, ch), F32),
            pltpu.VMEM((2, rows + 2 * PAD, ch), F32),
            pltpu.VMEM((2, 2, rows, 3 * ch), BF16),
            pltpu.VMEM((3, 2, rows, ch), BF16),
            pltpu.VMEM((3, 2, rows, ch), BF16),
            pltpu.VMEM((3, 2, rows, ch), BF16),
            pltpu.VMEM((rows, ch), F32),
            pltpu.VMEM((2, 2, rows, ch), BF16),
            pltpu.VMEM((3, ch, 3 * ch), F32),
            pltpu.VMEM((3, ch, 2 * ch), F32),
        ],
        compiler_params=params(),
    )(scalars, items, start, *cot_parts, mat_high, mat_low, turn_high, turn_low, short)


def weight_back(
    scalars, mel, gain, inverse, sums, back, high, low, block_grads, specs, numbers, slots, geo
):
    segments, frames, in_ch = mel.shape
    ch = high.shape[2]
    body = in_ch * 16 * ch // LANES
    given = 0 if specs[-1]["vec"] >= 0 else 1
    geo = dict(geo, specs=specs, segments=segments, frames=frames, given=given)
    vec_shape = (8 * geo["owners"], LANES)
    return pl.pallas_call(
        functools.partial(weight_back_kernel, geo),
        out_shape=tuple(shape((spec["slots"] * spec["rows"], LANES)) for spec in specs)
        + (shape(vec_shape),) * given,
        in_specs=[smem()] * 3 + [vmem()] * 5 + [anywhere()] * 3,
        out_specs=(anywhere(),) * len(specs) + (vmem(),) * given,
        scratch_shapes=[
            pltpu.VMEM((in_ch, 3 * segments * frames), BF16),
            pltpu.VMEM((16, in_ch, ch), F32),
            pltpu.VMEM((2, 16, in_ch, ch), BF16),
            pltpu.VMEM((in_ch, LANES), F32),
            pltpu.VMEM((body + block_grads.shape[0], LANES), F32),
            pltpu.VMEM(vec_shape, F32),
            pltpu.VMEM((40, LANES), F32),
            pltpu.SemaphoreType.DMA((3,)),
            pltpu.SemaphoreType.DMA((len(specs), max(spec["slots"] for spec in specs))),
            pltpu.SemaphoreType.DMA((copy_count(specs),)),
        ],
        compiler_params=params(),
    )(scalars, numbers, slots, mel, gain, inverse, sums, back, high, low, block_grads)


def frames_back(scalars, mel, back, high, low):
    segments, frames, in_ch = mel.shape
    ch = high.shape[2]
    geo = {"segments": segments, "frames": frames}
    weight = pl.BlockSpec((1, in_ch, ch), lambda k: (k, 0, 0))
    return pl.pallas_call(
        functools.partial(frames_back_kernel, geo),
        grid=(16,),
        out_shape=shape(mel.shape),
        in_specs=[smem(), whole_spec(mel.shape), whole_spec(back.shape), weight, weight],
        out_specs=whole_spec(mel.shape),
        scratch_shapes=[pltpu.VMEM((segments * frames, in_ch), F32)],
        compiler_params=params(),
        cost_estimate=pl.CostEstimate(
            flops=6 * segments * frames * in_ch * 16 * ch,
            bytes_accessed=4 * 16 * in_ch * ch + 8 * mel.size + 4 * back.size,
            transcendentals=0,
        ),
    )(scalars, mel, back, high, low)


def line_edges(low, high, axis):
    count = math.prod(lax.axis_size(name) for name in axis)
    forward = [(i, i + 1) for i in range(count - 1)]
    backward = [(target, source) for source, target in forward]
    return lax.ppermute(high, axis, forward), lax.ppermute(low, axis, backward)


def packed_edges(mel, cot):
    ch = cot.shape[2]
    edges = []
    for frames, samples in (
        (mel[:, :EDGE_FRAMES], cot[:, :EDGE]),
        (mel[:, mel.shape[1] - EDGE_FRAMES :], cot[:, cot.shape[1] - EDGE :]),
    ):
        edges.append(cat([frames[:, :, :ch], frames[:, :, ch:], samples], 1))
    return edges


def moments(gradient, first, second):
    first_new = B_ONE * first + (1.0 - B_ONE) * gradient
    second_new = B_TWO * second + (1.0 - B_TWO) * gradient * gradient
    direction = (
        first_new / (1.0 - B_ONE**STEP) / (jnp.sqrt(second_new / (1.0 - B_TWO**STEP)) + EPSILON)
    )
    return (first_new, second_new, direction)


def total(value, groups):
    for group in groups:
        count = math.prod(lax.axis_size(name) for name in group)
        far = 1
        while far < count:
            near = min(4, count // far)
            terms = [value]
            for step in range(1, near):
                moves = [(i, i ^ (step * far)) for i in range(count)]
                terms.append(lax.ppermute(value, group, moves))
            while len(terms) > 1:
                terms = [one + other for one, other in zip(terms[::2], terms[1::2])]
            value = terms[0]
            far = near * far
    return value


FLIPS = {"wide": ("wide", 1), "deep": ("deep", 1), "near": ("line", 1), "far": ("line", 2), "core": ("core", 1)}
ORDERS = (
    ("wide", "deep", "near", "far"),
    ("deep", "wide", "near", "far"),
    ("far", "near", "wide", "deep"),
)
GATHER_ORDERS = ORDERS[:2] + (("near", "far", "wide", "deep"),)
LANE_ROWS = 8


def swap(value, flip):
    axis, step = FLIPS[flip]
    return lax.ppermute(value, axis, [(i, i ^ step) for i in range(lax.axis_size(axis))])


def owner_table(order, other_core):
    places = {name: lax.axis_index(name) for name in ("line", "deep", "wide", "core")}
    numbers = []
    for slot in range(16):
        here = dict(places)
        for bit, flip in enumerate(order):
            if slot >> (3 - bit) & 1:
                axis, step = FLIPS[flip]
                here[axis] = here[axis] ^ step
        core = here["core"] ^ other_core
        numbers.append(((here["line"] * 2 + here["deep"]) * 2 + here["wide"]) * 2 + core)
    return jnp.stack(numbers).astype(jnp.int32)


def slot_table(order, other_core, owners):
    numbers = jnp.arange(owners, dtype=jnp.int32)
    there = {"core": numbers % 2, "wide": numbers // 2 % 2, "deep": numbers // 4 % 2}
    there["line"] = numbers // 8
    away = {name: lax.axis_index(name).astype(jnp.int32) ^ place for name, place in there.items()}
    slot = jnp.zeros_like(numbers)
    for flip in order:
        axis, step = FLIPS[flip]
        slot = 2 * slot + (away[axis] // step) % 2
    return jnp.where(away["core"] == other_core, slot, -1)


def part_sizes(shard_rows):
    last = shard_rows * 9 // 48 // 8 * 8
    first = (shard_rows - last) // 16 * 8
    return (first, first, shard_rows - 2 * first)


def part_specs(sizes, rows, slots):
    specs = []
    offset = 0
    for part, size in enumerate(sizes):
        valid = min(size, rows - offset)
        specs.append(
            {
                "part": part,
                "slots": slots,
                "rows": size,
                "pitch": rows,
                "offset": offset,
                "valid": valid,
                "vec": valid if valid < size else -1,
            }
        )
        offset += size
    return specs


def together(*values):
    return lax.optimization_barrier(values)


def gather_by_permutes(shard, sizes, edges, tm):
    first, second, third = sizes
    both, last = shard[: first + second], shard[first + second :]
    far, near, last_deep, last_wide, edges = together(
        swap(both, "far"),
        swap(both, "near"),
        swap(last, "deep"),
        swap(last, "wide"),
        line_edges(*edges, tm),
    )
    near_far, last_both = together(swap(far, "near"), swap(last_deep, "wide"))
    parts = (both, far, near, near_far)
    a = cat([part[:first] for part in parts], 0)
    b = cat([part[first:] for part in parts], 0)
    c = cat([last, last_deep, last_wide, last_both], 0)
    a, b, c = together(a, b, c)
    c_far, c_near = swap(c, "far"), swap(c, "near")
    a_deep, b_wide = swap(a, "deep"), swap(b, "wide")
    c_far, c_near, a_deep, b_wide, a, b = together(c_far, c_near, a_deep, b_wide, a, b)
    a_both, b_both = swap(a_deep, "wide"), swap(b_wide, "deep")
    a_wide, b_deep = swap(a, "wide"), swap(b, "deep")
    c_both = swap(c_far, "near")
    ready = [(0, 0, a), (1, 0, b), (2, 0, c), (0, 1, a_deep), (1, 1, b_wide), (2, 1, c_far)]
    ready.append((2, 2, c_near))
    others = [swap(array, "core") for _, _, array in ready]
    a_both, b_both, a_wide, b_deep, c_both, others = together(
        a_both, b_both, a_wide, b_deep, c_both, others
    )
    held = [(n, quarter, 0, array) for n, quarter, array in ready]
    held += [(n, quarter, 1, array) for (n, quarter, _), array in zip(ready, others)]
    rest = [(0, 2, a_wide), (1, 2, b_deep), (0, 3, a_both), (1, 3, b_both)]
    rest.append((2, 3, c_both))
    for n, quarter, array in rest:
        held += [(n, quarter, 0, array), (n, quarter, 1, swap(array, "core"))]
    return held, edges


def scatter_by_permutes(mine, theirs, sizes, beside):
    came = [swap(value, "core") for value in theirs]
    terms = [[own, other] for own, other in zip(mine, came)]
    slots = 16
    for level in range(4):
        slots = slots // 2
        away = []
        for number, (part, size) in enumerate(zip(terms, sizes)):
            if level == 0 and number > 0:
                part[1], away[-1] = together(part[1], away[-1])
            away.append(sum(term[slots * size : 2 * slots * size] for term in part))
        came = [swap(value, order[level]) for value, order in zip(away, ORDERS)]
        if level == 0:
            came, other = together(came, beside())
        else:
            came = together(*came)
        for part, value in zip(terms, came):
            part.append(value)
    summed = cat([sum(term[:size] for term in part) for part, size in zip(terms, sizes)], 0)
    return summed, other


def by_owner(mine, theirs, plan):
    grid, core_dim = plan["grid"], plan["core_dim"]
    first = lax.axis_index("core") == 0
    parts = [jnp.where(first, mine, theirs), jnp.where(first, theirs, mine)]
    chips = [size for place, size in enumerate(grid) if place != core_dim]
    parts = [part.reshape(chips + list(mine.shape[1:])) for part in parts]
    return jnp.stack(parts, axis=core_dim).reshape((-1,) + mine.shape[1:])


def by_core(shards, plan):
    grid, core_dim = plan["grid"], plan["core_dim"]
    grouped = shards.reshape(tuple(grid) + shards.shape[1:])
    core = lax.axis_index("core")
    mine = lax.dynamic_index_in_dim(grouped, core, core_dim, keepdims=False)
    theirs = lax.dynamic_index_in_dim(grouped, 1 - core, core_dim, keepdims=False)
    after = (-1,) + shards.shape[1:]
    return mine.reshape(after), theirs.reshape(after)


def body(
    plan,
    mel_frames,
    lengths,
    cotangent,
    matrices,
    vectors,
    matrix_first,
    matrix_second,
    vector_first,
    vector_second,
):
    tm, every, chip_axes = plan["tm"], plan["every"], plan["chip_axes"]
    segments, frames, in_ch = mel_frames.shape
    ch = cotangent.shape[2]
    pieces = math.prod(lax.axis_size(name) for name in tm)
    rows = matrices.shape[0] // LANES
    shard_rows = -(-(rows + 2) // 48) * 48
    vec_count = vectors.shape[0]
    spare = shard_rows - rows - 2
    owners = math.prod(plan["grid"])
    geo = {"in_ch": in_ch, "ch": ch, "owners": owners, "vec_count": vec_count}
    vec_first = lax.axis_index(every) * vec_count % LANES
    placed = lax.dynamic_update_slice(jnp.zeros((2 * LANES,), F32), vectors, (vec_first,))
    shard = jnp.concatenate(
        [
            matrices.reshape(rows, LANES),
            placed.reshape(2, LANES),
            jnp.zeros((spare, LANES), F32),
        ]
    )
    edges = packed_edges(mel_frames, cotangent)
    cubic = rows % 8 == 0 and plan["grid"] == (4, 2, 2, 2)
    sizes = part_sizes(shard_rows)
    if cubic:
        specs = part_specs(sizes, rows, 16)
        numbers = [[owner_table(order, core) for order in ORDERS] for core in range(2)]
        held, edges = gather_by_permutes(shard, sizes, edges, tm)
        places = [[owner_table(order, core) for order in GATHER_ORDERS] for core in range(2)]
        held_numbers = jnp.concatenate(
            [places[c][n][4 * quarter : 4 * quarter + 4] for n, quarter, c, _ in held]
        )
        held_specs = [dict(specs[n], slots=4) for n, _, _, _ in held]
        held = [array for _, _, _, array in held]
        given = []
    else:
        edges = line_edges(*edges, tm)
        mine = lax.all_gather(shard, chip_axes, axis=0, tiled=False)
        gathered = by_owner(mine, swap(mine, "core"), plan)
        held = [gathered[:, :rows].reshape(-1, LANES)]
        whole = held[0].shape[0]
        specs = [
            {
                "part": 0,
                "slots": 1,
                "rows": whole,
                "pitch": 0,
                "offset": 0,
                "valid": whole,
                "vec": -1,
            }
        ]
        held_specs, held_numbers = specs, jnp.zeros((1,), jnp.int32)
        vec_rows = jnp.pad(gathered[:, rows : rows + 2], ((0, 0), (0, LANE_ROWS - 2), (0, 0)))
        given = [vec_rows.reshape(-1, LANES)]
    mel_parts = (edges[0], mel_frames, edges[1])
    cot_parts = (edges[0], cotangent, edges[1])
    scalars = jnp.concatenate(
        [lengths[0], jnp.stack([lax.axis_index(tm), jnp.int32(pieces)]).astype(jnp.int32)]
    )
    up_high, up_low, *mats, short, inverse, gain, items, squares = prepare(
        held, held_specs, held_numbers, given, geo
    )
    start = upsample(scalars, mel_parts, items, up_high, up_low, pieces * frames)
    waveform, back, block_grads, sums = blocks(scalars, items, start, cot_parts, *mats, short)
    if cubic:
        out_specs = specs * 2
        out_numbers = jnp.concatenate(numbers[0] + numbers[1])
        out_slots = jnp.concatenate(
            [slot_table(order, core, owners) for core in range(2) for order in ORDERS]
        )
    else:
        out_specs, out_numbers, out_slots = held_specs, held_numbers, held_numbers
    grads = weight_back(
        scalars,
        mel_frames,
        gain,
        inverse,
        sums,
        back,
        up_high,
        up_low,
        block_grads,
        out_specs,
        out_numbers,
        out_slots,
        geo,
    )
    if cubic:
        summed, frames_grad = scatter_by_permutes(
            grads[:3],
            grads[3:],
            sizes,
            lambda: frames_back(scalars, mel_frames, back, up_high, up_low),
        )
    else:
        vec_rows = grads[1].reshape(owners, LANE_ROWS, LANES)[:, :2]
        shards = jnp.concatenate(
            [
                grads[0].reshape(owners, rows, LANES),
                vec_rows,
                jnp.zeros((owners, spare, LANES), F32),
            ],
            axis=1,
        )
        mine, theirs = by_core(shards, plan)
        mine = mine + swap(theirs, "core")
        summed = lax.psum_scatter(mine, chip_axes, scatter_dimension=0, tiled=True)[0]
        frames_grad = frames_back(scalars, mel_frames, back, up_high, up_low)
    matrix_grad = summed[:rows]
    vec_rows = summed[rows : rows + 2].reshape(-1)
    vector_grad = lax.dynamic_slice(vec_rows, (vec_first,), (vec_count,))

    shapes, starts, whole = layout(in_ch, ch)
    matrices = matrices.reshape(rows, LANES)
    position = lax.axis_index(every) * rows + jnp.arange(rows, dtype=jnp.int32)
    lower = jnp.array([first // LANES for first in starts], jnp.int32)
    upper = jnp.array([first // LANES for first in starts[1:] + [whole]], jnp.int32)
    member = (position[:, None] >= lower[None, :]) & (position[:, None] < upper[None, :])
    member = member.astype(F32)
    matrix_first_new, matrix_second_new, direction = moments(
        matrix_grad, matrix_first.reshape(rows, LANES), matrix_second.reshape(rows, LANES)
    )
    update = direction + DECAY * matrices
    update_sq = jnp.sum(member * jnp.sum(update * update, axis=1)[:, None], axis=0)
    update_sq = total(update_sq, (("core",), ("deep", "wide"), ("line",)))
    weight_norm = jnp.sqrt(jnp.sum(squares[:10], axis=1))
    update_norm = jnp.sqrt(update_sq)
    trust = weight_norm / update_norm
    row_trust = jnp.sum(member * trust[None, :], axis=1)
    new_matrices = (matrices - RATE * row_trust[:, None] * update).reshape(-1)
    vector_first_new, vector_second_new, vector_step = moments(
        vector_grad, vector_first, vector_second
    )
    new_vectors = vectors - RATE * vector_step
    norm_table = jnp.stack([weight_norm, update_norm])
    return (
        waveform,
        frames_grad,
        new_matrices,
        new_matrices.astype(BF16),
        matrix_first_new.reshape(-1),
        matrix_second_new.reshape(-1),
        new_vectors,
        new_vectors.astype(BF16),
        vector_first_new,
        vector_second_new,
        norm_table,
    )


def make_plan(mesh):
    tm, batch = mesh.shape["tm"], mesh.shape["batch"]
    if tm > 4:
        root = math.isqrt(batch)
        grid = (tm // 2, 2, root, batch // root)
        names = ("line", "core", "deep", "wide")
        tm_axes, batch_axes = ("line", "core"), ("deep", "wide")
        core_dim = 1
    else:
        root = math.isqrt(batch // 2)
        grid = (tm, root, batch // 2 // root, 2)
        names = ("line", "deep", "wide", "core")
        tm_axes, batch_axes = ("line",), ("deep", "wide", "core")
        core_dim = 3
    inner = Mesh(mesh.devices.reshape(grid), names)
    plan = {
        "tm": tm_axes,
        "batch": batch_axes,
        "every": names,
        "grid": grid,
        "core_dim": core_dim,
        "chip_axes": tuple(name for name in names if name != "core"),
    }
    return inner, plan


def solution(mesh):
    inner, plan = make_plan(mesh)
    tm, batch, every = plan["tm"], plan["batch"], plan["every"]
    pieces, flat = P(batch, tm, None), P(every)
    in_specs = (pieces, P(batch, None), pieces, flat, flat, flat, flat, flat, flat)
    out_specs = (pieces, pieces, flat, flat, flat, flat, flat, flat, flat, flat, P())
    return jax.shard_map(
        functools.partial(body, plan),
        mesh=inner,
        in_specs=in_specs,
        out_specs=out_specs,
        check_vma=False,
    )
```

```python
import functools
import math

import jax
import jax.numpy as jnp
from jax import lax
from jax.experimental import pallas as pl
from jax.experimental.pallas import tpu as pltpu
from jax.sharding import Mesh
from jax.sharding import PartitionSpec as P

STEP = 5
B_ONE = 0.5
B_TWO = 0.5
EPSILON = 1e-06
RATE = 0.5
DECAY = 0.01
LANES = 128
EDGE_FRAMES = 8
EDGE = 32
PAD = 16
VMEM_LIMIT = 60 * 1024 * 1024
BF16 = jnp.bfloat16
F32 = jnp.float32


def soft_leaky(value):
    small = jnp.exp2(jnp.abs(value) * (-1.0 / math.log(2.0)))
    return jnp.maximum(value, 0.2 * value) + (0.8 * math.log(2.0)) * jnp.log2(1.0 + small)


def leaky_slope(value):
    return 0.6 + 0.4 * jnp.tanh(0.5 * value)


def split(value):
    high = value.astype(BF16)
    return high, (value - high.astype(F32)).astype(BF16)


def cat(parts, axis):
    return jnp.concatenate(parts, axis=axis)


def dot(left, right, dims=((1,), (0,))):
    return lax.dot_general(left, right, (dims, ((), ())), preferred_element_type=F32)


ROWS_COLS = ((1,), (0,))
ROWS_ROWS = ((1,), (1,))
COLS_COLS = ((0,), (0,))


def layout(in_channels, channels):
    shapes = [(in_channels, 16, channels)]
    for _ in range(3):
        shapes = shapes + [(3, channels, channels), (channels, channels), (channels, channels)]
    starts = []
    position = 0
    for shape in shapes:
        starts.append(position)
        position = position + math.prod(shape)
    return (shapes, starts, position)


def start_all(copies):
    for copy in copies:
        copy.start()


def wait_all(copies):
    for copy in copies:
        copy.wait()


def piece_copies(specs, numbers, pieces, flat, vecs, sem, vec_sem, outward):
    copies, vec_copies = [], []
    at = 0

    def move(one, other, signal):
        source, target = (other, one) if outward else (one, other)
        return pltpu.make_async_copy(source, target, signal)

    for spec, piece in zip(specs, pieces):
        for slot in range(spec["slots"]):
            owner = numbers[at]
            first = slot * spec["rows"]
            place = pl.multiple_of(owner * spec["pitch"] + spec["offset"], 8)
            signal = sem.at[at] if outward else sem.at[spec["part"], owner]
            copies.append(
                move(
                    piece.at[pl.ds(first, spec["valid"])],
                    flat.at[pl.ds(place, spec["valid"])],
                    signal,
                )
            )
            if spec["vec"] >= 0:
                place = pl.multiple_of(owner * 8, 8)
                vec_copies.append(
                    move(
                        piece.at[pl.ds(first + spec["vec"], 8)],
                        vecs.at[pl.ds(place, 8)],
                        vec_sem.at[at],
                    )
                )
            at += 1
    return copies, vec_copies


def copy_count(specs):
    return sum(spec["slots"] for spec in specs)


def prepare_kernel(geo, *refs):
    specs, in_ch, ch = geo["specs"], geo["in_ch"], geo["ch"]
    count = len(specs)
    numbers, slots = refs[:2]
    pieces = refs[2 : 2 + count]
    given = refs[2 + count : 2 + count + geo["given"]]
    outs = refs[2 + count + geo["given"] :]
    short, inverse, gains, items, squares = outs[6:11]
    flat, scratch, full, sem, vec_sem = outs[11:16]
    up_high, up_low, mat_high, mat_low, turn_high, turn_low = outs[16:22]
    up_sem, mat_sem = outs[22:]

    def up_copies(i):
        span = pl.ds(pl.multiple_of(i * 16, 16), 16)
        pairs = zip(outs[:2], (up_high, up_low))
        return [
            pltpu.make_async_copy(made.at[:, span], out.at[:, span], up_sem.at[n, i])
            for n, (out, made) in enumerate(pairs)
        ]

    def mat_copies(b):
        pairs = zip(outs[2:6], (mat_high, mat_low, turn_high, turn_low))
        return [
            pltpu.make_async_copy(made.at[b], out.at[b], mat_sem.at[n, b])
            for n, (out, made) in enumerate(pairs)
        ]
    vecs = given[0] if geo["given"] else scratch
    _, vec_copies = piece_copies(specs, numbers, pieces, flat, scratch, sem, vec_sem, False)
    start_all(vec_copies)
    held = flat.shape[0] // (specs[0]["pitch"] or flat.shape[0])

    def fetch(owner, carry):
        for number, (spec, piece) in enumerate(zip(specs, pieces)):
            slot = slots[number * held + owner]

            @pl.when(slot >= 0)
            def _():
                first = pl.multiple_of(slot * spec["rows"], 8)
                place = pl.multiple_of(owner * spec["pitch"] + spec["offset"], 8)
                pltpu.make_async_copy(
                    piece.at[pl.ds(first, spec["valid"])],
                    flat.at[pl.ds(place, spec["valid"])],
                    sem.at[spec["part"], owner],
                ).start()

        return carry

    lax.fori_loop(0, held, fetch, 0)
    parts = {spec["part"]: spec for spec in specs}
    pitch = specs[0]["pitch"] or flat.shape[0]

    def wait_for(owner):
        for part, spec in parts.items():
            span = pl.ds(0, spec["valid"])
            pltpu.make_async_copy(pieces[0].at[span], flat.at[span], sem.at[part, owner]).wait()

    wait_all(vec_copies)
    full[...] = jnp.zeros_like(full)
    for owner in range(geo["owners"]):
        row = owner * geo["vec_count"] // LANES
        full[row : row + 2] += vecs[8 * owner : 8 * owner + 2]
    columns = full[0:8].T
    gain = cat([columns[:, j : j + 1] for j in range(in_ch // LANES)], 0)
    gains[...] = jnp.broadcast_to(gain, gains.shape)
    items[...] = jnp.zeros_like(items)
    per_row = ch // LANES
    for i in range(13):
        for part in range(per_row):
            row = in_ch // LANES + per_row * i + part
            items[i : i + 1, part * LANES : (part + 1) * LANES] = full[row : row + 1]
    wide = 16 * ch // LANES
    squares[...] = jnp.zeros_like(squares)
    group = 16

    def channels(i, carry):
        first = i * (group * wide)
        now = (first + group * wide - 1) // pitch

        @pl.when((i == 0) | (now > (first - 1) // pitch))
        def _():
            wait_for(now)

        block = flat[pl.ds(pl.multiple_of(first, group * wide), group * wide), :]
        block = jnp.swapaxes(block.reshape(group, wide, LANES), 0, 1)
        square = jnp.sum(block * block, axis=0)
        squares[0:1, :] += jnp.sum(square, axis=0, keepdims=True)
        inv = lax.rsqrt(jnp.sum(square, axis=1, keepdims=True))
        span = pl.ds(pl.multiple_of(i * group, group), group)
        inverse[span, :] = jnp.broadcast_to(inv, (group, LANES))
        scale = gains[span, 0:1] * inv
        for place in range(wide):
            high, low = split(block[place] * scale)
            lanes = slice(place % 2 * LANES, place % 2 * LANES + LANES)
            up_high[place // 2, span, lanes] = high
            up_low[place // 2, span, lanes] = low
        start_all(up_copies(i))
        return carry

    lax.fori_loop(0, in_ch // group, channels, 0)
    for owner in range((in_ch * wide - 1) // pitch + 1, flat.shape[0] // pitch):
        wait_for(owner)
    base = in_ch * wide
    step = ch * ch // LANES
    for block in range(3):
        for number in range(5):
            first = base + (block * 5 + number) * step
            value = cat(
                [flat[pl.ds(first + part, ch, stride=per_row), :] for part in range(per_row)], 1
            )
            column = jnp.sum(value * value, axis=0, keepdims=True)
            which = 1 + 3 * block + max(number - 2, 0)
            squares[which : which + 1, :] += column[:, :LANES] + column[:, LANES:]
            if number == 4:
                short[block, 0:ch] = value
                root = lax.rsqrt(column)
                short[block, ch : ch + 8] = jnp.broadcast_to(root, (8, ch))
                value = value * (items[3 + 4 * block : 4 + 4 * block, :] * root)
            high, low = split(value)
            mat_high[block, number] = high
            mat_low[block, number] = low
            high, low = split(value.T)
            turn_high[block, number] = high
            turn_low[block, number] = low
        start_all(mat_copies(block))

    def finish(i, carry):
        wait_all(up_copies(i))
        return carry

    lax.fori_loop(0, in_ch // group, finish, 0)
    for block in range(3):
        wait_all(mat_copies(block))


def upsample_kernel(
    geo,
    scalars,
    mel_low,
    mel,
    mel_high,
    bias,
    mid_high,
    mid_low,
    side_high,
    side_low,
    out,
    wide,
    mid,
    sides,
):
    segments, frames, ahead = geo["segments"], geo["frames"], geo["ahead"]
    step = pl.program_id(0)
    kept = frames + 2 * (EDGE // 8)
    size = kept + 8
    in_ch = mel.shape[2]

    @pl.when(step == 0)
    def _():
        rows = frames + 2 * EDGE_FRAMES
        wide[...] = jnp.zeros_like(wide)
        place = scalars[segments] * frames - EDGE_FRAMES
        place = place + lax.broadcasted_iota(jnp.int32, (rows, 1), 0)
        inside = ((place >= 0) & (place < ahead)).astype(F32)
        for s in range(segments):
            live = (place < scalars[s]).astype(F32)
            first = 0
            for part in (mel_low, mel, mel_high):
                value = part[s]
                if part is not mel:
                    value = cat([value[0:EDGE_FRAMES], value[EDGE_FRAMES : 2 * EDGE_FRAMES]], 1)
                span = slice(first, first + value.shape[0])
                wide[s, span] = soft_leaky(value * live[span]) * inside[span]
                first = span.stop
        for s in range(segments):
            span = slice(s * size, (s + 1) * size)
            first = EDGE_FRAMES - EDGE // 8
            for target, shift in ((mid, 0), (sides.at[0], -1), (sides.at[1], 1)):
                high, low = split(wide[s, first + shift : first + shift + size])
                target[0, span] = high
                target[1, span] = low

    side = step // 2
    left_high = cat([mid[0], sides[side, 0]], 1)
    left_low = cat([mid[1], sides[side, 1]], 1)
    left = cat([left_high, left_low, left_high], 1)
    for n in range(mid_high.shape[0]):
        right_high = cat([mid_high[n], side_high[n]], 0)
        right_low = cat([mid_low[n], side_low[n]], 0)
        value = dot(left, cat([right_high, right_high, right_low], 0)) + bias[0:1, :]
        place = step * mid_high.shape[0] + n
        for s in range(segments):
            for half in range(out.shape[1]):
                out[s, half, pl.ds(place, kept, stride=8), :] = value[
                    s * size : s * size + kept, half * LANES : (half + 1) * LANES
                ]


def blocks_kernel(
    geo,
    scalars,
    items,
    start,
    cot_low,
    cot,
    cot_high,
    mat_high,
    mat_low,
    turn_high,
    turn_low,
    short,
    wave,
    back,
    grads,
    sums,
    hidden,
    middle,
    padded,
    triple,
    act,
    mid_act,
    hid,
    flow,
    flow_pair,
    dil_acc,
    pair_acc,
):
    segments, ch, samples = geo["segments"], geo["ch"], geo["samples"]
    rows = samples + 2 * EDGE
    count = geo["tiles"]
    tile = rows // count
    tiles = [slice(r, r + tile) for r in range(0, rows, tile)]
    own = slice(EDGE, EDGE + samples)
    segment = pl.program_id(0)
    piece = scalars[segments]
    low_edge = jnp.where(piece > 0, 1.0, 0.0)
    high_edge = jnp.where(piece < scalars[segments + 1] - 1, 1.0, 0.0)
    position = piece * samples - EDGE + lax.broadcasted_iota(jnp.int32, (rows, 1), 0)
    live = position < 8 * scalars[segment]

    @pl.when(segment == 0)
    def _():
        for n in range(2):
            padded[n, 0:PAD] = jnp.zeros((PAD, ch), F32)
            padded[n, PAD + rows : PAD + rows + PAD] = jnp.zeros((PAD, ch), F32)
        dil_acc[...] = jnp.zeros_like(dil_acc)
        pair_acc[...] = jnp.zeros_like(pair_acc)
        sums[...] = jnp.zeros_like(sums)

    def put_padded(n, t, value):
        first, last = PAD + t * tile, PAD + (t + 1) * tile
        if t == 0:
            padded[n, first : first + EDGE] = value[:EDGE] * low_edge
            value, first = value[EDGE:], first + EDGE
        if t == count - 1:
            padded[n, last - EDGE : last] = value[value.shape[0] - EDGE :] * high_edge
            value, last = value[: value.shape[0] - EDGE], last - EDGE
        padded[n, first:last] = value

    def shift(n, t, gap):
        for k in range(3):
            first = PAD + t * tile + (k - 1) * gap
            high, low = split(padded[n, first : first + tile])
            triple[n, 0, tiles[t], k * ch : (k + 1) * ch] = high
            triple[n, 1, tiles[t], k * ch : (k + 1) * ch] = low

    def operand(parts, axis):
        high, low = parts
        return cat([high, high, low] if axis == 0 else [high, low, high], axis)

    def stack(refs, b, numbers):
        return [cat([ref[b, number] for number in numbers], 0) for ref in refs]

    weights = (mat_high, mat_low)
    turned = (turn_high, turn_low)

    def activate(b, t):
        value = hidden[b, tiles[t]]
        put_padded(b % 2, t, soft_leaky(value))
        hid[b, 0, tiles[t]], hid[b, 1, tiles[t]] = split(value)

    def widen(b, t):
        shift(b % 2, t, 3**b)
        act[b, :, tiles[t]] = triple[b % 2, :, tiles[t], ch : 2 * ch]

    def dilated(b, t):
        left = operand([triple[b % 2, n, tiles[t]] for n in range(2)], 1)
        right = operand(stack(weights, b, range(3)), 0)
        middle[b, tiles[t]] = dot(left, right) + items[1 + 4 * b : 2 + 4 * b, :]

    def bend(b, t):
        mid_act[b, 0, tiles[t]], mid_act[b, 1, tiles[t]] = split(soft_leaky(middle[b, tiles[t]]))

    def leave(b, t):
        left = cat(
            [
                operand([mid_act[b, n, tiles[t]] for n in range(2)], 1),
                operand([hid[b, n, tiles[t]] for n in range(2)], 1),
            ],
            1,
        )
        right = cat([operand(stack(weights, b, [number]), 0) for number in (3, 4)], 0)
        offset = items[2 + 4 * b : 3 + 4 * b, :] + items[4 + 4 * b : 5 + 4 * b, :]
        hidden[b + 1, tiles[t]] = dot(left, right) + offset

    for t in range(count):
        hidden[0, tiles[t]] = cat([start[0, half, tiles[t]] for half in range(start.shape[1])], 1)
        activate(0, t)
    for b in range(3):
        for t in range(count + 2):
            if t < count:
                widen(b, t)
                dilated(b, t)
            if 1 <= t <= count:
                bend(b, t - 1)
            if t >= 2:
                leave(b, t - 2)
                if b < 2:
                    activate(b + 1, t - 2)
    wave[0] = jnp.where(live[own], hidden[3, own], 0.0)
    first = 0
    for part in (cot_low[:, 2 * EDGE_FRAMES :], cot, cot_high[:, 2 * EDGE_FRAMES :]):
        span = slice(first, first + part.shape[1])
        flow[span] = jnp.where(live[span], part[0], 0.0)
        first = span.stop

    def part_flow(b, t):
        high, low = split(flow[tiles[t]])
        flow_pair[b % 2, 0, tiles[t]] = high
        flow_pair[b % 2, 1, tiles[t]] = low

    def inner(b, t):
        left = operand([flow_pair[b % 2, n, tiles[t]] for n in range(2)], 1)
        value = dot(left, operand(stack(turned, b, [3]), 0))
        put_padded(b % 2, t, value * leaky_slope(middle[b, tiles[t]]))

    def outer(b, t):
        left = operand([triple[b % 2, n, tiles[t]] for n in range(2)], 1)
        value = dot(left, operand(stack(turned, b, range(3)), 0))
        left = operand([flow_pair[b % 2, n, tiles[t]] for n in range(2)], 1)
        short_part = dot(left, operand(stack(turned, b, [4]), 0))
        flow[tiles[t]] = value * leaky_slope(hidden[b, tiles[t]]) + short_part

    def biases(b):
        body = padded[b % 2, PAD + EDGE : PAD + EDGE + samples]
        sums[8 * b : 8 * b + 1, :] += jnp.sum(body, axis=0, keepdims=True)
        sums[8 * b + 1 : 8 * b + 2, :] += jnp.sum(flow[own], axis=0, keepdims=True)

    def pair_weights(b):
        left = cat([flow_pair[b % 2, n, own].T for n in range(2)], 0)
        right = [cat([mid_act[b, n, own], hid[b, n, own]], 1) for n in range(2)]
        value = dot(left, right[0])
        pair_acc[b] += value[0:ch] + value[ch : 2 * ch] + dot(left[0:ch], right[1])

    def dilated_weights(b):
        left = cat([act[b, n, own].T for n in range(2)], 0)
        value = dot(left, triple[b % 2, 0, own])
        value = value[0:ch] + value[ch : 2 * ch]
        dil_acc[b] += value + dot(left[0:ch], triple[b % 2, 1, own])

    def backward_shift(b, t):
        shift(b % 2, t, -(3**b))

    for t in range(count):
        part_flow(2, t)
    for b in (2, 1, 0):
        for t in range(count):
            inner(b, t)
        pair_weights(b)
        backward_shift(b, 0)
        biases(b)
        for t in range(count):
            if t + 1 < count:
                backward_shift(b, t + 1)
            outer(b, t)
            if b > 0 and t >= 1:
                part_flow(b - 1, t - 1)
        dilated_weights(b)
        if b > 0:
            part_flow(b - 1, count - 1)
    flow[0:EDGE] = flow[0:EDGE] * low_edge
    flow[rows - EDGE : rows] = flow[rows - EDGE : rows] * high_edge
    sums[24:25, :] += jnp.sum(flow[own], axis=0, keepdims=True)
    for half in range(back.shape[1]):
        back[0, half] = flow[:, half * LANES : (half + 1) * LANES]

    @pl.when(segment == segments - 1)
    def _():
        step = ch * ch // LANES
        per_row = ch // LANES

        def put(number, value):
            for part in range(per_row):
                grads[pl.ds(number * step + part, ch, stride=per_row), :] = value[
                    :, part * LANES : (part + 1) * LANES
                ]

        for b in range(3):
            for k in range(3):
                put(5 * b + k, dil_acc[b, :, k * ch : (k + 1) * ch])
            put(5 * b + 3, pair_acc[b, :, 0:ch].T)
            whole = pair_acc[b, :, ch : 2 * ch].T
            inv = short[b, ch : ch + 1]
            direction = short[b, 0:ch] * inv
            along = jnp.sum(whole * direction, axis=0, keepdims=True)
            sums[8 * b + 2 : 8 * b + 3, :] = along
            gain = items[3 + 4 * b : 4 + 4 * b, :]
            put(5 * b + 4, gain * inv * (whole - along * direction))


def tap_window(back, tap, segments, frames):
    first = EDGE - 4 + tap
    halves = range(back.shape[1])
    return cat(
        [
            cat([back[s, half, pl.ds(first, frames, stride=8), :] for half in halves], 1)
            for s in range(segments)
        ],
        0,
    )


def weight_back_kernel(
    geo, scalars, numbers, slots, mel, gain, inverse, sums, back, high, low, blocks, *refs
):
    specs, segments, frames = geo["specs"], geo["segments"], geo["frames"]
    count = len(specs)
    pieces = refs[:count]
    outs = refs[count:]
    extra = outs[0] if geo["given"] else None
    turned, whole, kept, slope, flat, scratch, full, block_sem, sem, vec_sem = outs[geo["given"] :]
    vecs = extra if geo["given"] else scratch
    in_ch = mel.shape[2]
    ch = high.shape[2]
    wide = 16 * ch // LANES
    body = in_ch * wide
    pitch = specs[0]["pitch"] or flat.shape[0]
    owners = flat.shape[0] // pitch
    loads = [
        pltpu.make_async_copy(blocks, flat.at[pl.ds(body, blocks.shape[0])], block_sem.at[0]),
        pltpu.make_async_copy(high, kept.at[0], block_sem.at[1]),
        pltpu.make_async_copy(low, kept.at[1], block_sem.at[2]),
    ]
    start_all(loads)

    def send(owner):
        for number, (spec, piece) in enumerate(zip(specs, pieces)):

            @pl.when(slots[number * owners + owner] >= 0)
            def _():
                slot = slots[number * owners + owner]
                first = pl.multiple_of(slot * spec["rows"], 8)
                place = pl.multiple_of(owner * pitch + spec["offset"], 8)
                pltpu.make_async_copy(
                    flat.at[pl.ds(place, spec["valid"])],
                    piece.at[pl.ds(first, spec["valid"])],
                    sem.at[number, slot],
                ).start()

    def send_each(first, last):
        def step(owner, carry):
            send(owner)
            return carry

        lax.fori_loop(first, last, step, 0)

    place = scalars[segments] * frames + lax.broadcasted_iota(jnp.int32, (frames, 1), 0)
    for s in range(segments):
        live = (place < scalars[s]).astype(F32)
        upper, lower = split(soft_leaky(mel[s] * live).T)
        for part, piece in enumerate((upper, lower, upper)):
            first = (part * segments + s) * frames
            turned[:, first : first + frames] = piece

    def taps(tap, carry):
        upper, lower = split(tap_window(back, tap, segments, frames))
        whole[tap] = dot(turned[...], cat([upper, upper, lower], 0))
        return carry

    lax.fori_loop(0, 16, taps, 0)
    wait_all(loads)
    shared = body // pitch
    send_each(-(-body // pitch), owners)
    group = 16

    def channels(i, carry):
        span = pl.ds(pl.multiple_of(i * group, group), group)
        along = jnp.zeros((group, ch), F32)
        for tap in range(16):
            raw = kept[0, tap, span].astype(F32) + kept[1, tap, span].astype(F32)
            along = along + raw * whole[tap, span]
        factor = gain[span, 0:1]
        column = jnp.sum(along, axis=1, keepdims=True) / factor
        slope[span] = jnp.broadcast_to(column, (group, LANES))
        inv = inverse[span, 0:1]
        scale = factor * inv
        turn = inv * column
        values = []
        for tap in range(16):
            raw = kept[0, tap, span].astype(F32) + kept[1, tap, span].astype(F32)
            value = scale * whole[tap, span] - turn * raw
            for half in range(ch // LANES):
                values.append(value[:, half * LANES : (half + 1) * LANES])
        block = jnp.swapaxes(jnp.stack(values), 0, 1).reshape(group * wide, LANES)
        first = pl.multiple_of(i * (group * wide), group * wide)
        flat[pl.ds(first, group * wide), :] = block
        done = (first + group * wide) // pitch

        @pl.when(done > first // pitch)
        def _():
            send(done - 1)

        return carry

    lax.fori_loop(0, in_ch // group, channels, 0)
    if body % pitch:
        send(shared)
    for j in range(in_ch // LANES):
        full[j : j + 1] = slope[j * LANES : (j + 1) * LANES].T[0:1]
    order = [24]
    for b in range(3):
        order += [8 * b, 8 * b + 1, 8 * b + 2, 8 * b + 1]
    row = in_ch // LANES
    for number in order:
        for part in range(ch // LANES):
            full[row : row + 1] = sums[number : number + 1, part * LANES : (part + 1) * LANES]
            row += 1
    vecs[...] = jnp.zeros_like(vecs)
    for owner in range(geo["owners"]):
        row = owner * geo["vec_count"] // LANES
        vecs[8 * owner : 8 * owner + 2] = full[row : row + 2]
    _, vec_copies = piece_copies(specs, numbers, pieces, flat, scratch, vec_sem, vec_sem, True)
    start_all(vec_copies)
    for number, (spec, piece) in enumerate(zip(specs, pieces)):
        for slot in range(spec["slots"]):
            pltpu.make_async_copy(
                flat.at[pl.ds(0, spec["valid"])],
                piece.at[pl.ds(slot * spec["rows"], spec["valid"])],
                sem.at[number, slot],
            ).wait()
    wait_all(vec_copies)


def frames_back_kernel(geo, scalars, mel, back, high, low, out, total):
    segments, frames = geo["segments"], geo["frames"]
    step = pl.program_id(0)

    @pl.when(step == 0)
    def _():
        total[...] = jnp.zeros_like(total)

    upper, lower = split(tap_window(back, step, segments, frames))
    total[...] += dot(
        cat([upper, lower, upper], 1), cat([high[0], high[0], low[0]], 1), ROWS_ROWS
    )

    @pl.when(step == pl.num_programs(0) - 1)
    def _():
        place = scalars[segments] * frames + lax.broadcasted_iota(jnp.int32, (frames, 1), 0)
        for s in range(segments):
            live = (place < scalars[s]).astype(F32)
            value = total[s * frames : (s + 1) * frames]
            out[s] = value * leaky_slope(mel[s] * live) * live


def whole_spec(shape):
    return pl.BlockSpec(shape, lambda *_: (0,) * len(shape))


def vmem():
    return pl.BlockSpec(memory_space=pltpu.VMEM)


def smem():
    return pl.BlockSpec(memory_space=pltpu.SMEM)


def anywhere():
    return pl.BlockSpec(memory_space=pl.ANY)


def shape(dims, dtype=F32):
    return jax.ShapeDtypeStruct(dims, dtype)


def params():
    return pltpu.CompilerParams(vmem_limit_bytes=VMEM_LIMIT)


def prepare(pieces, specs, numbers, slots, given, geo):
    in_ch, ch = geo["in_ch"], geo["ch"]
    entries = (in_ch * 16 * ch + 15 * ch * ch) // LANES
    geo = dict(geo, specs=specs, given=len(given))
    return pl.pallas_call(
        functools.partial(prepare_kernel, geo),
        out_shape=(
            shape((16, in_ch, ch), BF16),
            shape((16, in_ch, ch), BF16),
            shape((3, 5, ch, ch), BF16),
            shape((3, 5, ch, ch), BF16),
            shape((3, 5, ch, ch), BF16),
            shape((3, 5, ch, ch), BF16),
            shape((3, ch + 8, ch)),
            shape((in_ch, LANES)),
            shape((in_ch, LANES)),
            shape((16, ch)),
            shape((16, LANES)),
        ),
        in_specs=[smem()] * 2 + [anywhere()] * len(pieces) + [vmem()] * len(given),
        out_specs=(anywhere(),) * 6 + (vmem(),) * 5,
        scratch_shapes=[
            pltpu.VMEM((entries, LANES), F32),
            pltpu.VMEM((8 * geo["owners"], LANES), F32),
            pltpu.VMEM((40, LANES), F32),
            pltpu.SemaphoreType.DMA((3, geo["owners"])),
            pltpu.SemaphoreType.DMA((copy_count(specs),)),
            pltpu.VMEM((16, in_ch, ch), BF16),
            pltpu.VMEM((16, in_ch, ch), BF16),
        ]
        + [pltpu.VMEM((3, 5, ch, ch), BF16)] * 4
        + [
            pltpu.SemaphoreType.DMA((2, in_ch // 16)),
            pltpu.SemaphoreType.DMA((4, 3)),
        ],
        compiler_params=params(),
    )(numbers, slots, *pieces, *given)


def upsample(scalars, mel_parts, items, up_high, up_low, ahead):
    segments, frames, in_ch = mel_parts[1].shape
    ch = up_high.shape[2]
    kept = frames + 2 * (EDGE // 8)
    size = kept + 8
    geo = {"segments": segments, "frames": frames, "ahead": ahead}
    out = (segments, ch // LANES, 8 * kept, LANES)
    return pl.pallas_call(
        functools.partial(upsample_kernel, geo),
        grid=(4,),
        out_shape=shape(out),
        in_specs=[smem()]
        + [whole_spec(part.shape) for part in mel_parts]
        + [
            whole_spec(items.shape),
            pl.BlockSpec((2, in_ch, ch), lambda j: (j + 2, 0, 0)),
            pl.BlockSpec((2, in_ch, ch), lambda j: (j + 2, 0, 0)),
            pl.BlockSpec((2, in_ch, ch), lambda j: ((j + 6) % 8, 0, 0)),
            pl.BlockSpec((2, in_ch, ch), lambda j: ((j + 6) % 8, 0, 0)),
        ],
        out_specs=whole_spec(out),
        scratch_shapes=[
            pltpu.VMEM((segments, frames + 2 * EDGE_FRAMES + 16, in_ch), F32),
            pltpu.VMEM((2, segments * size, in_ch), BF16),
            pltpu.VMEM((2, 2, segments * size, in_ch), BF16),
        ],
        compiler_params=params(),
    )(scalars, *mel_parts, items, up_high, up_low, up_high, up_low)


def blocks(scalars, items, start, cot_parts, mat_high, mat_low, turn_high, turn_low, short):
    segments, samples, ch = cot_parts[1].shape
    rows = samples + 2 * EDGE
    geo = {"segments": segments, "samples": samples, "ch": ch, "tiles": 4}
    halves = start.shape[1]
    flat = (15 * ch * ch // LANES, LANES)
    once = pl.Buffered(1)

    def fixed(dims):
        return pl.BlockSpec(dims, lambda s: (0,) * len(dims), pipeline_mode=once)

    return pl.pallas_call(
        functools.partial(blocks_kernel, geo),
        grid=(segments,),
        out_shape=(
            shape((segments, samples, ch)),
            shape((segments, halves, rows, LANES)),
            shape(flat),
            shape((32, ch)),
        ),
        in_specs=[
            smem(),
            fixed(items.shape),
            pl.BlockSpec((1, halves, rows, LANES), lambda s: (s, 0, 0, 0)),
        ]
        + [pl.BlockSpec((1,) + part.shape[1:], lambda s: (s, 0, 0)) for part in cot_parts]
        + [
            fixed(mat_high.shape),
            fixed(mat_low.shape),
            fixed(turn_high.shape),
            fixed(turn_low.shape),
            fixed(short.shape),
        ],
        out_specs=(
            pl.BlockSpec((1, samples, ch), lambda s: (s, 0, 0)),
            pl.BlockSpec((1, halves, rows, LANES), lambda s: (s, 0, 0, 0)),
            pl.BlockSpec(flat, lambda s: (0, 0), pipeline_mode=once),
            pl.BlockSpec((32, ch), lambda s: (0, 0)),
        ),
        scratch_shapes=[
            pltpu.VMEM((4, rows, ch), F32),
            pltpu.VMEM((3, rows, ch), F32),
            pltpu.VMEM((2, rows + 2 * PAD, ch), F32),
            pltpu.VMEM((2, 2, rows, 3 * ch), BF16),
            pltpu.VMEM((3, 2, rows, ch), BF16),
            pltpu.VMEM((3, 2, rows, ch), BF16),
            pltpu.VMEM((3, 2, rows, ch), BF16),
            pltpu.VMEM((rows, ch), F32),
            pltpu.VMEM((2, 2, rows, ch), BF16),
            pltpu.VMEM((3, ch, 3 * ch), F32),
            pltpu.VMEM((3, ch, 2 * ch), F32),
        ],
        compiler_params=params(),
    )(scalars, items, start, *cot_parts, mat_high, mat_low, turn_high, turn_low, short)


def weight_back(
    scalars, mel, gain, inverse, sums, back, high, low, block_grads, specs, numbers, slots, geo
):
    segments, frames, in_ch = mel.shape
    ch = high.shape[2]
    body = in_ch * 16 * ch // LANES
    given = 0 if specs[-1]["vec"] >= 0 else 1
    geo = dict(geo, specs=specs, segments=segments, frames=frames, given=given)
    vec_shape = (8 * geo["owners"], LANES)
    return pl.pallas_call(
        functools.partial(weight_back_kernel, geo),
        out_shape=tuple(shape((spec["slots"] * spec["rows"], LANES)) for spec in specs)
        + (shape(vec_shape),) * given,
        in_specs=[smem()] * 3 + [vmem()] * 5 + [anywhere()] * 3,
        out_specs=(anywhere(),) * len(specs) + (vmem(),) * given,
        scratch_shapes=[
            pltpu.VMEM((in_ch, 3 * segments * frames), BF16),
            pltpu.VMEM((16, in_ch, ch), F32),
            pltpu.VMEM((2, 16, in_ch, ch), BF16),
            pltpu.VMEM((in_ch, LANES), F32),
            pltpu.VMEM((body + block_grads.shape[0], LANES), F32),
            pltpu.VMEM(vec_shape, F32),
            pltpu.VMEM((40, LANES), F32),
            pltpu.SemaphoreType.DMA((3,)),
            pltpu.SemaphoreType.DMA((len(specs), max(spec["slots"] for spec in specs))),
            pltpu.SemaphoreType.DMA((copy_count(specs),)),
        ],
        compiler_params=params(),
    )(scalars, numbers, slots, mel, gain, inverse, sums, back, high, low, block_grads)


def finish_kernel(geo, place, matrices, first, second, *refs):
    sizes, rows = geo["sizes"], geo["rows"]
    given = refs[: len(refs) - 6]
    first_new, second_new, update, squares, vectors, whole = refs[len(refs) - 6 :]
    each = len(given) // len(sizes)
    at = 0
    for number, size in enumerate(sizes):
        parts = [ref[...] for ref in given[number * each : (number + 1) * each]]
        whole[at : at + size] = sum(parts)
        at += size
    vectors[...] = whole[rows : rows + 8]
    made = moments(whole[0:rows], first[...], second[...])
    first_new[...], second_new[...] = made[:2]
    change = made[2] + DECAY * matrices[...]
    update[...] = change
    square = change * change
    position = place[0] * rows + lax.broadcasted_iota(jnp.int32, (rows, 1), 0)
    lane = lax.broadcasted_iota(jnp.int32, (8, LANES), 1)
    result = jnp.zeros((8, LANES), F32)
    for j, (low, high) in enumerate(geo["spans"]):
        kept = jnp.where((position >= low) & (position < high), square, 0.0)
        result = jnp.where(lane == j, jnp.sum(kept), result)
    squares[...] = result


def finish(terms, sizes, place, matrices, first, second, spans):
    rows = matrices.shape[0]
    geo = {"sizes": sizes, "rows": rows, "spans": spans}
    flat = [term for part in terms for term in part]
    heads = [size for size, part in zip(sizes, terms) for _ in part]
    entry = pl.BlockSpec((rows, LANES), lambda i: (0, 0))
    return pl.pallas_call(
        functools.partial(finish_kernel, geo),
        grid=(1,),
        out_shape=(shape((rows, LANES)),) * 3 + (shape((8, LANES)),) * 2,
        in_specs=[smem(), entry, entry, entry]
        + [pl.BlockSpec((size, LANES), lambda i: (0, 0)) for size in heads],
        out_specs=(entry,) * 3 + (pl.BlockSpec((8, LANES), lambda i: (0, 0)),) * 2,
        scratch_shapes=[pltpu.VMEM((sum(sizes), LANES), F32)],
        compiler_params=params(),
    )(place, matrices, first, second, *flat)


def frames_back(scalars, mel, back, high, low):
    segments, frames, in_ch = mel.shape
    ch = high.shape[2]
    geo = {"segments": segments, "frames": frames}
    weight = pl.BlockSpec((1, in_ch, ch), lambda k: (k, 0, 0))
    return pl.pallas_call(
        functools.partial(frames_back_kernel, geo),
        grid=(16,),
        out_shape=shape(mel.shape),
        in_specs=[smem(), whole_spec(mel.shape), whole_spec(back.shape), weight, weight],
        out_specs=whole_spec(mel.shape),
        scratch_shapes=[pltpu.VMEM((segments * frames, in_ch), F32)],
        compiler_params=params(),
        cost_estimate=pl.CostEstimate(
            flops=6 * segments * frames * in_ch * 16 * ch,
            bytes_accessed=4 * 16 * in_ch * ch + 8 * mel.size + 4 * back.size,
            transcendentals=0,
        ),
    )(scalars, mel, back, high, low)


def line_edges(low, high, axis):
    count = math.prod(lax.axis_size(name) for name in axis)
    forward = [(i, i + 1) for i in range(count - 1)]
    backward = [(target, source) for source, target in forward]
    return lax.ppermute(high, axis, forward), lax.ppermute(low, axis, backward)


def packed_edges(mel, cot):
    ch = cot.shape[2]
    edges = []
    for frames, samples in (
        (mel[:, :EDGE_FRAMES], cot[:, :EDGE]),
        (mel[:, mel.shape[1] - EDGE_FRAMES :], cot[:, cot.shape[1] - EDGE :]),
    ):
        edges.append(cat([frames[:, :, :ch], frames[:, :, ch:], samples], 1))
    return edges


def moments(gradient, first, second):
    first_new = B_ONE * first + (1.0 - B_ONE) * gradient
    second_new = B_TWO * second + (1.0 - B_TWO) * gradient * gradient
    direction = (
        first_new / (1.0 - B_ONE**STEP) / (jnp.sqrt(second_new / (1.0 - B_TWO**STEP)) + EPSILON)
    )
    return (first_new, second_new, direction)


def total(value, groups):
    for group in groups:
        count = math.prod(lax.axis_size(name) for name in group)
        far = 1
        while far < count:
            near = min(4, count // far)
            terms = [value]
            for step in range(1, near):
                moves = [(i, i ^ (step * far)) for i in range(count)]
                terms.append(lax.ppermute(value, group, moves))
            while len(terms) > 1:
                terms = [one + other for one, other in zip(terms[::2], terms[1::2])]
            value = terms[0]
            far = near * far
    return value


FLIPS = {"wide": ("wide", 1), "deep": ("deep", 1), "near": ("line", 1), "far": ("line", 2), "core": ("core", 1)}
ORDERS = (
    ("wide", "deep", "near", "far"),
    ("deep", "wide", "near", "far"),
    ("far", "near", "wide", "deep"),
)
GATHER_ORDERS = ORDERS[:2] + (("near", "far", "wide", "deep"),)
HELD = [(n, quarter, c) for n in range(3) for quarter in range(4) for c in range(2)]
LANE_ROWS = 8


def swap(value, flip):
    axis, step = FLIPS[flip]
    return lax.ppermute(value, axis, [(i, i ^ step) for i in range(lax.axis_size(axis))])


def owner_table(order, other_core):
    places = {name: lax.axis_index(name) for name in ("line", "deep", "wide", "core")}
    numbers = []
    for slot in range(16):
        here = dict(places)
        for bit, flip in enumerate(order):
            if slot >> (3 - bit) & 1:
                axis, step = FLIPS[flip]
                here[axis] = here[axis] ^ step
        core = here["core"] ^ other_core
        numbers.append(((here["line"] * 2 + here["deep"]) * 2 + here["wide"]) * 2 + core)
    return jnp.stack(numbers).astype(jnp.int32)


def slot_table(order, other_core, owners):
    numbers = jnp.arange(owners, dtype=jnp.int32)
    there = {"core": numbers % 2, "wide": numbers // 2 % 2, "deep": numbers // 4 % 2}
    there["line"] = numbers // 8
    away = {name: lax.axis_index(name).astype(jnp.int32) ^ place for name, place in there.items()}
    slot = jnp.zeros_like(numbers)
    for flip in order:
        axis, step = FLIPS[flip]
        slot = 2 * slot + (away[axis] // step) % 2
    return jnp.where(away["core"] == other_core, slot, -1)


def part_sizes(shard_rows):
    last = shard_rows * 9 // 48 // 8 * 8
    first = (shard_rows - last) // 16 * 8
    return (first, first, shard_rows - 2 * first)


def part_specs(sizes, rows, slots):
    specs = []
    offset = 0
    for part, size in enumerate(sizes):
        valid = min(size, rows - offset)
        specs.append(
            {
                "part": part,
                "slots": slots,
                "rows": size,
                "pitch": rows,
                "offset": offset,
                "valid": valid,
                "vec": valid if valid < size else -1,
            }
        )
        offset += size
    return specs


def together(*values):
    return lax.optimization_barrier(values)


def gather_by_permutes(shard, sizes, edges, tm, tables):
    first, second, third = sizes
    both, last = shard[: first + second], shard[first + second :]
    far, near, last_deep, last_wide, edges, tables = together(
        swap(both, "far"),
        swap(both, "near"),
        swap(last, "deep"),
        swap(last, "wide"),
        line_edges(*edges, tm),
        tables,
    )
    near_far, last_both = together(swap(far, "near"), swap(last_deep, "wide"))
    parts = (both, far, near, near_far)
    a = cat([part[:first] for part in parts], 0)
    b = cat([part[first:] for part in parts], 0)
    c = cat([last, last_deep, last_wide, last_both], 0)
    a, b, c = together(a, b, c)
    c_far, c_near = swap(c, "far"), swap(c, "near")
    a_deep, b_wide = swap(a, "deep"), swap(b, "wide")
    c_far, c_near, a_deep, b_wide, a, b = together(c_far, c_near, a_deep, b_wide, a, b)
    a_both, b_both = swap(a_deep, "wide"), swap(b_wide, "deep")
    a_wide, b_deep = swap(a, "wide"), swap(b, "deep")
    c_both = swap(c_far, "near")
    ready = [(0, 0, a), (1, 0, b), (2, 0, c), (0, 1, a_deep), (1, 1, b_wide), (2, 1, c_far)]
    ready.append((2, 2, c_near))
    others = [swap(array, "core") for _, _, array in ready]
    a_both, b_both, a_wide, b_deep, c_both, others = together(
        a_both, b_both, a_wide, b_deep, c_both, others
    )
    held = [(n, quarter, 0, array) for n, quarter, array in ready]
    held += [(n, quarter, 1, array) for (n, quarter, _), array in zip(ready, others)]
    rest = [(0, 2, a_wide), (1, 2, b_deep), (0, 3, a_both), (1, 3, b_both)]
    rest.append((2, 3, c_both))
    for n, quarter, array in rest:
        held += [(n, quarter, 0, array), (n, quarter, 1, swap(array, "core"))]
    return held, edges, tables


def scatter_by_permutes(mine, theirs, sizes, beside):
    came = [swap(value, "core") for value in theirs]
    terms = [[own, other] for own, other in zip(mine, came)]
    slots = 16
    for level in range(4):
        slots = slots // 2
        away = []
        for number, (part, size) in enumerate(zip(terms, sizes)):
            if level == 0 and number > 0:
                part[1], away[-1] = together(part[1], away[-1])
            away.append(sum(term[slots * size : 2 * slots * size] for term in part))
        came = [swap(value, order[level]) for value, order in zip(away, ORDERS)]
        if level == 0:
            came, other = together(came, beside())
        else:
            came = together(*came)
        for part, value in zip(terms, came):
            part.append(value)
    return terms, other


def by_owner(mine, theirs, plan):
    grid, core_dim = plan["grid"], plan["core_dim"]
    first = lax.axis_index("core") == 0
    parts = [jnp.where(first, mine, theirs), jnp.where(first, theirs, mine)]
    chips = [size for place, size in enumerate(grid) if place != core_dim]
    parts = [part.reshape(chips + list(mine.shape[1:])) for part in parts]
    return jnp.stack(parts, axis=core_dim).reshape((-1,) + mine.shape[1:])


def by_core(shards, plan):
    grid, core_dim = plan["grid"], plan["core_dim"]
    grouped = shards.reshape(tuple(grid) + shards.shape[1:])
    core = lax.axis_index("core")
    mine = lax.dynamic_index_in_dim(grouped, core, core_dim, keepdims=False)
    theirs = lax.dynamic_index_in_dim(grouped, 1 - core, core_dim, keepdims=False)
    after = (-1,) + shards.shape[1:]
    return mine.reshape(after), theirs.reshape(after)


def body(
    plan,
    mel_frames,
    lengths,
    cotangent,
    matrices,
    vectors,
    matrix_first,
    matrix_second,
    vector_first,
    vector_second,
):
    tm, every, chip_axes = plan["tm"], plan["every"], plan["chip_axes"]
    segments, frames, in_ch = mel_frames.shape
    ch = cotangent.shape[2]
    pieces = math.prod(lax.axis_size(name) for name in tm)
    rows = matrices.shape[0] // LANES
    shard_rows = -(-(rows + 2) // 48) * 48
    vec_count = vectors.shape[0]
    spare = shard_rows - rows - 2
    owners = math.prod(plan["grid"])
    geo = {"in_ch": in_ch, "ch": ch, "owners": owners, "vec_count": vec_count}
    vec_first = lax.axis_index(every) * vec_count % LANES
    placed = lax.dynamic_update_slice(jnp.zeros((2 * LANES,), F32), vectors, (vec_first,))
    shard = jnp.concatenate(
        [
            matrices.reshape(rows, LANES),
            placed.reshape(2, LANES),
            jnp.zeros((spare, LANES), F32),
        ]
    )
    edges = packed_edges(mel_frames, cotangent)
    scalars = jnp.concatenate(
        [lengths[0], jnp.stack([lax.axis_index(tm), jnp.int32(pieces)]).astype(jnp.int32)]
    )
    cubic = rows % 8 == 0 and plan["grid"] == (4, 2, 2, 2)
    sizes = part_sizes(shard_rows)
    if cubic:
        specs = part_specs(sizes, rows, 16)
        out_numbers = jnp.concatenate(
            [owner_table(order, core) for core in range(2) for order in ORDERS]
        )
        out_slots = jnp.concatenate(
            [slot_table(order, core, owners) for core in range(2) for order in ORDERS]
        )
        places = [[owner_table(order, core) for order in GATHER_ORDERS] for core in range(2)]
        found = [[slot_table(order, core, owners) for order in GATHER_ORDERS] for core in range(2)]
        held_numbers = jnp.concatenate(
            [places[c][n][4 * quarter : 4 * quarter + 4] for n, quarter, c in HELD]
        )
        held_slots = jnp.concatenate(
            [jnp.where(found[c][n] // 4 == quarter, found[c][n] % 4, -1) for n, quarter, c in HELD]
        )
        tables = (out_numbers, out_slots, held_numbers, held_slots, scalars)
        held, edges, tables = gather_by_permutes(shard, sizes, edges, tm, tables)
        out_numbers, out_slots, held_numbers, held_slots, scalars = tables
        held.sort(key=lambda entry: HELD.index(entry[:3]))
        held_specs = [dict(specs[n], slots=4) for n, _, _, _ in held]
        held = [array for _, _, _, array in held]
        given = []
    else:
        edges = line_edges(*edges, tm)
        mine = lax.all_gather(shard, chip_axes, axis=0, tiled=False)
        gathered = by_owner(mine, swap(mine, "core"), plan)
        held = [gathered[:, :rows].reshape(-1, LANES)]
        whole = held[0].shape[0]
        specs = [
            {
                "part": 0,
                "slots": 1,
                "rows": whole,
                "pitch": 0,
                "offset": 0,
                "valid": whole,
                "vec": -1,
            }
        ]
        held_specs, held_numbers = specs, jnp.zeros((1,), jnp.int32)
        held_slots = held_numbers
        vec_rows = jnp.pad(gathered[:, rows : rows + 2], ((0, 0), (0, LANE_ROWS - 2), (0, 0)))
        given = [vec_rows.reshape(-1, LANES)]
    mel_parts = (edges[0], mel_frames, edges[1])
    cot_parts = (edges[0], cotangent, edges[1])
    up_high, up_low, *mats, short, inverse, gain, items, squares = prepare(
        held, held_specs, held_numbers, held_slots, given, geo
    )
    start = upsample(scalars, mel_parts, items, up_high, up_low, pieces * frames)
    waveform, back, block_grads, sums = blocks(scalars, items, start, cot_parts, *mats, short)
    if cubic:
        out_specs = specs * 2
    else:
        out_specs, out_numbers, out_slots = held_specs, held_numbers, held_numbers
    grads = weight_back(
        scalars,
        mel_frames,
        gain,
        inverse,
        sums,
        back,
        up_high,
        up_low,
        block_grads,
        out_specs,
        out_numbers,
        out_slots,
        geo,
    )
    if cubic:
        terms, frames_grad = scatter_by_permutes(
            grads[:3],
            grads[3:],
            sizes,
            lambda: frames_back(scalars, mel_frames, back, up_high, up_low),
        )
    else:
        vec_rows = grads[1].reshape(owners, LANE_ROWS, LANES)[:, :2]
        shards = jnp.concatenate(
            [
                grads[0].reshape(owners, rows, LANES),
                vec_rows,
                jnp.zeros((owners, spare, LANES), F32),
            ],
            axis=1,
        )
        mine, theirs = by_core(shards, plan)
        mine = mine + swap(theirs, "core")
        summed = lax.psum_scatter(mine, chip_axes, scatter_dimension=0, tiled=True)[0]
        frames_grad = frames_back(scalars, mel_frames, back, up_high, up_low)
    shapes, starts, whole = layout(in_ch, ch)
    spans = [(low // LANES, high // LANES) for low, high in zip(starts, starts[1:] + [whole])]
    matrices = matrices.reshape(rows, LANES)
    first, second = matrix_first.reshape(rows, LANES), matrix_second.reshape(rows, LANES)
    place = lax.axis_index(every).astype(jnp.int32)
    position = place * rows + jnp.arange(rows, dtype=jnp.int32)
    lower = jnp.array([low for low, _ in spans], jnp.int32)
    upper = jnp.array([high for _, high in spans], jnp.int32)
    member = (position[:, None] >= lower[None, :]) & (position[:, None] < upper[None, :])
    member = member.astype(F32)
    if cubic:
        matrix_first_new, matrix_second_new, update, update_sq, vec_rows = finish(
            terms, sizes, place.reshape(1), matrices, first, second, spans
        )
        update_sq = update_sq[0:1]
        vec_rows = vec_rows[:2].reshape(-1)
    else:
        matrix_first_new, matrix_second_new, direction = moments(summed[:rows], first, second)
        update = direction + DECAY * matrices
        update_sq = jnp.sum(member * jnp.sum(update * update, axis=1)[:, None], axis=0)
        vec_rows = summed[rows : rows + 2].reshape(-1)
    vector_grad = lax.dynamic_slice(vec_rows, (vec_first,), (vec_count,))
    update_sq = total(update_sq, (("core",), ("deep", "wide"), ("line",)))
    update_sq = update_sq.reshape(-1)[:10]
    weight_norm = jnp.sqrt(jnp.sum(squares[:10], axis=1))
    update_norm = jnp.sqrt(update_sq)
    trust = weight_norm / update_norm
    row_trust = jnp.sum(member * trust[None, :], axis=1)
    new_matrices = (matrices - RATE * row_trust[:, None] * update).reshape(-1)
    vector_first_new, vector_second_new, vector_step = moments(
        vector_grad, vector_first, vector_second
    )
    new_vectors = vectors - RATE * vector_step
    norm_table = jnp.stack([weight_norm, update_norm])
    return (
        waveform,
        frames_grad,
        new_matrices,
        new_matrices.astype(BF16),
        matrix_first_new.reshape(-1),
        matrix_second_new.reshape(-1),
        new_vectors,
        new_vectors.astype(BF16),
        vector_first_new,
        vector_second_new,
        norm_table,
    )


def make_plan(mesh):
    tm, batch = mesh.shape["tm"], mesh.shape["batch"]
    if tm > 4:
        root = math.isqrt(batch)
        grid = (tm // 2, 2, root, batch // root)
        names = ("line", "core", "deep", "wide")
        tm_axes, batch_axes = ("line", "core"), ("deep", "wide")
        core_dim = 1
    else:
        root = math.isqrt(batch // 2)
        grid = (tm, root, batch // 2 // root, 2)
        names = ("line", "deep", "wide", "core")
        tm_axes, batch_axes = ("line",), ("deep", "wide", "core")
        core_dim = 3
    inner = Mesh(mesh.devices.reshape(grid), names)
    plan = {
        "tm": tm_axes,
        "batch": batch_axes,
        "every": names,
        "grid": grid,
        "core_dim": core_dim,
        "chip_axes": tuple(name for name in names if name != "core"),
    }
    return inner, plan


def solution(mesh):
    inner, plan = make_plan(mesh)
    tm, batch, every = plan["tm"], plan["batch"], plan["every"]
    pieces, flat = P(batch, tm, None), P(every)
    in_specs = (pieces, P(batch, None), pieces, flat, flat, flat, flat, flat, flat)
    out_specs = (pieces, pieces, flat, flat, flat, flat, flat, flat, flat, flat, P())
    return jax.shard_map(
        functools.partial(body, plan),
        mesh=inner,
        in_specs=in_specs,
        out_specs=out_specs,
        check_vma=False,
    )
```

```python
import functools
import math

import jax
import jax.numpy as jnp
from jax import lax
from jax.experimental import pallas as pl
from jax.experimental.pallas import tpu as pltpu
from jax.sharding import Mesh
from jax.sharding import PartitionSpec as P

STEP = 5
B_ONE = 0.5
B_TWO = 0.5
EPSILON = 1e-06
RATE = 0.5
DECAY = 0.01
LANES = 128
EDGE_FRAMES = 8
EDGE = 32
PAD = 16
VMEM_LIMIT = 60 * 1024 * 1024
BF16 = jnp.bfloat16
F32 = jnp.float32


def soft_leaky(value):
    small = jnp.exp2(jnp.abs(value) * (-1.0 / math.log(2.0)))
    return jnp.maximum(value, 0.2 * value) + (0.8 * math.log(2.0)) * jnp.log2(1.0 + small)


def leaky_slope(value):
    return 0.6 + 0.4 * jnp.tanh(0.5 * value)


def split(value):
    high = value.astype(BF16)
    return high, (value - high.astype(F32)).astype(BF16)


def cat(parts, axis):
    return jnp.concatenate(parts, axis=axis)


def dot(left, right, dims=((1,), (0,))):
    return lax.dot_general(left, right, (dims, ((), ())), preferred_element_type=F32)


ROWS_COLS = ((1,), (0,))
ROWS_ROWS = ((1,), (1,))
COLS_COLS = ((0,), (0,))


def layout(in_channels, channels):
    shapes = [(in_channels, 16, channels)]
    for _ in range(3):
        shapes = shapes + [(3, channels, channels), (channels, channels), (channels, channels)]
    starts = []
    position = 0
    for shape in shapes:
        starts.append(position)
        position = position + math.prod(shape)
    return (shapes, starts, position)


def start_all(copies):
    for copy in copies:
        copy.start()


def wait_all(copies):
    for copy in copies:
        copy.wait()


def piece_copies(specs, numbers, pieces, flat, vecs, sem, vec_sem, outward):
    copies, vec_copies = [], []
    at = 0

    def move(one, other, signal):
        source, target = (other, one) if outward else (one, other)
        return pltpu.make_async_copy(source, target, signal)

    for spec, piece in zip(specs, pieces):
        for slot in range(spec["slots"]):
            owner = numbers[at]
            first = slot * spec["rows"]
            place = pl.multiple_of(owner * spec["pitch"] + spec["offset"], 8)
            signal = sem.at[at] if outward else sem.at[spec["part"], owner]
            copies.append(
                move(
                    piece.at[pl.ds(first, spec["valid"])],
                    flat.at[pl.ds(place, spec["valid"])],
                    signal,
                )
            )
            if spec["vec"] >= 0:
                place = pl.multiple_of(owner * 8, 8)
                vec_copies.append(
                    move(
                        piece.at[pl.ds(first + spec["vec"], 8)],
                        vecs.at[pl.ds(place, 8)],
                        vec_sem.at[at],
                    )
                )
            at += 1
    return copies, vec_copies


def copy_count(specs):
    return sum(spec["slots"] for spec in specs)


def prepare_kernel(geo, *refs):
    specs, in_ch, ch = geo["specs"], geo["in_ch"], geo["ch"]
    count = len(specs)
    numbers = refs[0]
    pieces = refs[1 : 1 + count]
    given = refs[1 + count : 1 + count + geo["given"]]
    outs = refs[1 + count + geo["given"] :]
    short, inverse, gains, items, squares = outs[6:11]
    flat, scratch, full, sem, vec_sem = outs[11:16]
    up_high, up_low, mat_high, mat_low, turn_high, turn_low = outs[16:22]
    up_sem, mat_sem = outs[22:]

    def up_copies(i):
        span = pl.ds(pl.multiple_of(i * 16, 16), 16)
        pairs = zip(outs[:2], (up_high, up_low))
        return [
            pltpu.make_async_copy(made.at[:, span], out.at[:, span], up_sem.at[n, i])
            for n, (out, made) in enumerate(pairs)
        ]

    def mat_copies(b):
        pairs = zip(outs[2:6], (mat_high, mat_low, turn_high, turn_low))
        return [
            pltpu.make_async_copy(made.at[b], out.at[b], mat_sem.at[n, b])
            for n, (out, made) in enumerate(pairs)
        ]
    vecs = given[0] if geo["given"] else scratch
    copies, vec_copies = piece_copies(specs, numbers, pieces, flat, scratch, sem, vec_sem, False)
    start_all(vec_copies)
    start_all(copies)
    parts = {spec["part"]: spec for spec in specs}
    pitch = specs[0]["pitch"] or flat.shape[0]

    def wait_for(owner):
        for part, spec in parts.items():
            span = pl.ds(0, spec["valid"])
            pltpu.make_async_copy(pieces[0].at[span], flat.at[span], sem.at[part, owner]).wait()

    wait_all(vec_copies)
    full[...] = jnp.zeros_like(full)
    for owner in range(geo["owners"]):
        row = owner * geo["vec_count"] // LANES
        full[row : row + 2] += vecs[8 * owner : 8 * owner + 2]
    columns = full[0:8].T
    gain = cat([columns[:, j : j + 1] for j in range(in_ch // LANES)], 0)
    gains[...] = jnp.broadcast_to(gain, gains.shape)
    items[...] = jnp.zeros_like(items)
    per_row = ch // LANES
    for i in range(13):
        for part in range(per_row):
            row = in_ch // LANES + per_row * i + part
            items[i : i + 1, part * LANES : (part + 1) * LANES] = full[row : row + 1]
    wide = 16 * ch // LANES
    squares[...] = jnp.zeros_like(squares)
    group = 16

    def channels(i, carry):
        first = i * (group * wide)
        now = (first + group * wide - 1) // pitch

        @pl.when((i == 0) | (now > (first - 1) // pitch))
        def _():
            wait_for(now)

        block = flat[pl.ds(pl.multiple_of(first, group * wide), group * wide), :]
        block = jnp.swapaxes(block.reshape(group, wide, LANES), 0, 1)
        square = jnp.sum(block * block, axis=0)
        squares[0:1, :] += jnp.sum(square, axis=0, keepdims=True)
        inv = lax.rsqrt(jnp.sum(square, axis=1, keepdims=True))
        span = pl.ds(pl.multiple_of(i * group, group), group)
        inverse[span, :] = jnp.broadcast_to(inv, (group, LANES))
        scale = gains[span, 0:1] * inv
        for place in range(wide):
            high, low = split(block[place] * scale)
            lanes = slice(place % 2 * LANES, place % 2 * LANES + LANES)
            up_high[place // 2, span, lanes] = high
            up_low[place // 2, span, lanes] = low
        start_all(up_copies(i))
        return carry

    lax.fori_loop(0, in_ch // group, channels, 0)
    for owner in range((in_ch * wide - 1) // pitch + 1, flat.shape[0] // pitch):
        wait_for(owner)
    base = in_ch * wide
    step = ch * ch // LANES
    for block in range(3):
        for number in range(5):
            first = base + (block * 5 + number) * step
            value = cat(
                [flat[pl.ds(first + part, ch, stride=per_row), :] for part in range(per_row)], 1
            )
            column = jnp.sum(value * value, axis=0, keepdims=True)
            which = 1 + 3 * block + max(number - 2, 0)
            squares[which : which + 1, :] += column[:, :LANES] + column[:, LANES:]
            if number == 4:
                short[block, 0:ch] = value
                root = lax.rsqrt(column)
                short[block, ch : ch + 8] = jnp.broadcast_to(root, (8, ch))
                value = value * (items[3 + 4 * block : 4 + 4 * block, :] * root)
            high, low = split(value)
            mat_high[block, number] = high
            mat_low[block, number] = low
            high, low = split(value.T)
            turn_high[block, number] = high
            turn_low[block, number] = low
        start_all(mat_copies(block))

    def finish(i, carry):
        wait_all(up_copies(i))
        return carry

    lax.fori_loop(0, in_ch // group, finish, 0)
    for block in range(3):
        wait_all(mat_copies(block))


def upsample_kernel(
    geo,
    scalars,
    mel_low,
    mel,
    mel_high,
    bias,
    mid_high,
    mid_low,
    side_high,
    side_low,
    out,
    wide,
    mid,
    sides,
):
    segments, frames, ahead = geo["segments"], geo["frames"], geo["ahead"]
    step = pl.program_id(0)
    kept = frames + 2 * (EDGE // 8)
    size = kept + 8
    in_ch = mel.shape[2]

    @pl.when(step == 0)
    def _():
        rows = frames + 2 * EDGE_FRAMES
        wide[...] = jnp.zeros_like(wide)
        place = scalars[segments] * frames - EDGE_FRAMES
        place = place + lax.broadcasted_iota(jnp.int32, (rows, 1), 0)
        inside = ((place >= 0) & (place < ahead)).astype(F32)
        for s in range(segments):
            live = (place < scalars[s]).astype(F32)
            first = 0
            for part in (mel_low, mel, mel_high):
                value = part[s]
                if part is not mel:
                    value = cat([value[0:EDGE_FRAMES], value[EDGE_FRAMES : 2 * EDGE_FRAMES]], 1)
                span = slice(first, first + value.shape[0])
                wide[s, span] = soft_leaky(value * live[span]) * inside[span]
                first = span.stop
        for s in range(segments):
            span = slice(s * size, (s + 1) * size)
            first = EDGE_FRAMES - EDGE // 8
            for target, shift in ((mid, 0), (sides.at[0], -1), (sides.at[1], 1)):
                high, low = split(wide[s, first + shift : first + shift + size])
                target[0, span] = high
                target[1, span] = low

    side = step // 4
    left_high = cat([mid[0], sides[side, 0]], 1)
    left_low = cat([mid[1], sides[side, 1]], 1)
    right_high = cat([mid_high[0], side_high[0]], 0)
    right_low = cat([mid_low[0], side_low[0]], 0)
    value = dot(cat([left_high, left_low, left_high], 1), cat([right_high, right_high, right_low], 0))
    value = value + bias[0:1, :]
    for s in range(segments):
        for half in range(out.shape[1]):
            out[s, half, pl.ds(step, kept, stride=8), :] = value[
                s * size : s * size + kept, half * LANES : (half + 1) * LANES
            ]


def blocks_kernel(
    geo,
    scalars,
    items,
    start,
    cot_low,
    cot,
    cot_high,
    mat_high,
    mat_low,
    turn_high,
    turn_low,
    short,
    wave,
    back,
    grads,
    sums,
    hidden,
    middle,
    padded,
    triple,
    act,
    mid_act,
    hid,
    flow,
    flow_pair,
    dil_acc,
    pair_acc,
):
    segments, ch, samples = geo["segments"], geo["ch"], geo["samples"]
    rows = samples + 2 * EDGE
    count = geo["tiles"]
    tile = rows // count
    tiles = [slice(r, r + tile) for r in range(0, rows, tile)]
    own = slice(EDGE, EDGE + samples)
    segment = pl.program_id(0)
    piece = scalars[segments]
    low_edge = jnp.where(piece > 0, 1.0, 0.0)
    high_edge = jnp.where(piece < scalars[segments + 1] - 1, 1.0, 0.0)
    position = piece * samples - EDGE + lax.broadcasted_iota(jnp.int32, (rows, 1), 0)
    live = position < 8 * scalars[segment]

    @pl.when(segment == 0)
    def _():
        for n in range(2):
            padded[n, 0:PAD] = jnp.zeros((PAD, ch), F32)
            padded[n, PAD + rows : PAD + rows + PAD] = jnp.zeros((PAD, ch), F32)
        dil_acc[...] = jnp.zeros_like(dil_acc)
        pair_acc[...] = jnp.zeros_like(pair_acc)
        sums[...] = jnp.zeros_like(sums)

    def put_padded(n, t, value):
        first, last = PAD + t * tile, PAD + (t + 1) * tile
        if t == 0:
            padded[n, first : first + EDGE] = value[:EDGE] * low_edge
            value, first = value[EDGE:], first + EDGE
        if t == count - 1:
            padded[n, last - EDGE : last] = value[value.shape[0] - EDGE :] * high_edge
            value, last = value[: value.shape[0] - EDGE], last - EDGE
        padded[n, first:last] = value

    def shift(n, t, gap):
        for k in range(3):
            first = PAD + t * tile + (k - 1) * gap
            high, low = split(padded[n, first : first + tile])
            triple[n, 0, tiles[t], k * ch : (k + 1) * ch] = high
            triple[n, 1, tiles[t], k * ch : (k + 1) * ch] = low

    def operand(parts, axis):
        high, low = parts
        return cat([high, high, low] if axis == 0 else [high, low, high], axis)

    def stack(refs, b, numbers):
        return [cat([ref[b, number] for number in numbers], 0) for ref in refs]

    weights = (mat_high, mat_low)
    turned = (turn_high, turn_low)

    def activate(b, t):
        value = hidden[b, tiles[t]]
        put_padded(b % 2, t, soft_leaky(value))
        hid[b, 0, tiles[t]], hid[b, 1, tiles[t]] = split(value)

    def widen(b, t):
        shift(b % 2, t, 3**b)
        act[b, :, tiles[t]] = triple[b % 2, :, tiles[t], ch : 2 * ch]

    def dilated(b, t):
        left = operand([triple[b % 2, n, tiles[t]] for n in range(2)], 1)
        right = operand(stack(weights, b, range(3)), 0)
        middle[b, tiles[t]] = dot(left, right) + items[1 + 4 * b : 2 + 4 * b, :]

    def bend(b, t):
        mid_act[b, 0, tiles[t]], mid_act[b, 1, tiles[t]] = split(soft_leaky(middle[b, tiles[t]]))

    def leave(b, t):
        left = cat(
            [
                operand([mid_act[b, n, tiles[t]] for n in range(2)], 1),
                operand([hid[b, n, tiles[t]] for n in range(2)], 1),
            ],
            1,
        )
        right = cat([operand(stack(weights, b, [number]), 0) for number in (3, 4)], 0)
        offset = items[2 + 4 * b : 3 + 4 * b, :] + items[4 + 4 * b : 5 + 4 * b, :]
        hidden[b + 1, tiles[t]] = dot(left, right) + offset

    for t in range(count):
        hidden[0, tiles[t]] = cat([start[0, half, tiles[t]] for half in range(start.shape[1])], 1)
        activate(0, t)
    for b in range(3):
        for t in range(count + 2):
            if t < count:
                widen(b, t)
                dilated(b, t)
            if 1 <= t <= count:
                bend(b, t - 1)
            if t >= 2:
                leave(b, t - 2)
                if b < 2:
                    activate(b + 1, t - 2)
    wave[0] = jnp.where(live[own], hidden[3, own], 0.0)
    first = 0
    for part in (cot_low[:, 2 * EDGE_FRAMES :], cot, cot_high[:, 2 * EDGE_FRAMES :]):
        span = slice(first, first + part.shape[1])
        flow[span] = jnp.where(live[span], part[0], 0.0)
        first = span.stop

    def part_flow(b, t):
        high, low = split(flow[tiles[t]])
        flow_pair[b % 2, 0, tiles[t]] = high
        flow_pair[b % 2, 1, tiles[t]] = low

    def inner(b, t):
        left = operand([flow_pair[b % 2, n, tiles[t]] for n in range(2)], 1)
        value = dot(left, operand(stack(turned, b, [3]), 0))
        put_padded(b % 2, t, value * leaky_slope(middle[b, tiles[t]]))

    def outer(b, t):
        left = operand([triple[b % 2, n, tiles[t]] for n in range(2)], 1)
        value = dot(left, operand(stack(turned, b, range(3)), 0))
        left = operand([flow_pair[b % 2, n, tiles[t]] for n in range(2)], 1)
        short_part = dot(left, operand(stack(turned, b, [4]), 0))
        flow[tiles[t]] = value * leaky_slope(hidden[b, tiles[t]]) + short_part

    def biases(b):
        body = padded[b % 2, PAD + EDGE : PAD + EDGE + samples]
        sums[8 * b : 8 * b + 1, :] += jnp.sum(body, axis=0, keepdims=True)
        sums[8 * b + 1 : 8 * b + 2, :] += jnp.sum(flow[own], axis=0, keepdims=True)

    def pair_weights(b):
        left = cat([flow_pair[b % 2, n, own].T for n in range(2)], 0)
        right = [cat([mid_act[b, n, own], hid[b, n, own]], 1) for n in range(2)]
        value = dot(left, right[0])
        pair_acc[b] += value[0:ch] + value[ch : 2 * ch] + dot(left[0:ch], right[1])

    def dilated_weights(b):
        left = cat([act[b, n, own].T for n in range(2)], 0)
        value = dot(left, triple[b % 2, 0, own])
        value = value[0:ch] + value[ch : 2 * ch]
        dil_acc[b] += value + dot(left[0:ch], triple[b % 2, 1, own])

    def backward_shift(b, t):
        shift(b % 2, t, -(3**b))

    for t in range(count):
        part_flow(2, t)
    for b in (2, 1, 0):
        for t in range(count):
            inner(b, t)
        pair_weights(b)
        backward_shift(b, 0)
        biases(b)
        for t in range(count):
            if t + 1 < count:
                backward_shift(b, t + 1)
            outer(b, t)
            if b > 0 and t >= 1:
                part_flow(b - 1, t - 1)
        dilated_weights(b)
        if b > 0:
            part_flow(b - 1, count - 1)
    flow[0:EDGE] = flow[0:EDGE] * low_edge
    flow[rows - EDGE : rows] = flow[rows - EDGE : rows] * high_edge
    sums[24:25, :] += jnp.sum(flow[own], axis=0, keepdims=True)
    for half in range(back.shape[1]):
        back[0, half] = flow[:, half * LANES : (half + 1) * LANES]

    @pl.when(segment == segments - 1)
    def _():
        step = ch * ch // LANES
        per_row = ch // LANES

        def put(number, value):
            for part in range(per_row):
                grads[pl.ds(number * step + part, ch, stride=per_row), :] = value[
                    :, part * LANES : (part + 1) * LANES
                ]

        for b in range(3):
            for k in range(3):
                put(5 * b + k, dil_acc[b, :, k * ch : (k + 1) * ch])
            put(5 * b + 3, pair_acc[b, :, 0:ch].T)
            whole = pair_acc[b, :, ch : 2 * ch].T
            inv = short[b, ch : ch + 1]
            direction = short[b, 0:ch] * inv
            along = jnp.sum(whole * direction, axis=0, keepdims=True)
            sums[8 * b + 2 : 8 * b + 3, :] = along
            gain = items[3 + 4 * b : 4 + 4 * b, :]
            put(5 * b + 4, gain * inv * (whole - along * direction))


def tap_window(back, tap, segments, frames):
    first = EDGE - 4 + tap
    halves = range(back.shape[1])
    return cat(
        [
            cat([back[s, half, pl.ds(first, frames, stride=8), :] for half in halves], 1)
            for s in range(segments)
        ],
        0,
    )


def weight_back_kernel(
    geo, scalars, numbers, slots, mel, gain, inverse, sums, back, high, low, blocks, *refs
):
    specs, segments, frames = geo["specs"], geo["segments"], geo["frames"]
    count = len(specs)
    pieces = refs[:count]
    outs = refs[count:]
    extra = outs[0] if geo["given"] else None
    turned, whole, kept, slope, flat, scratch, full, block_sem, sem, vec_sem = outs[geo["given"] :]
    vecs = extra if geo["given"] else scratch
    in_ch = mel.shape[2]
    ch = high.shape[2]
    wide = 16 * ch // LANES
    body = in_ch * wide
    pitch = specs[0]["pitch"] or flat.shape[0]
    owners = flat.shape[0] // pitch
    loads = [
        pltpu.make_async_copy(blocks, flat.at[pl.ds(body, blocks.shape[0])], block_sem.at[0]),
        pltpu.make_async_copy(high, kept.at[0], block_sem.at[1]),
        pltpu.make_async_copy(low, kept.at[1], block_sem.at[2]),
    ]
    start_all(loads)

    def send(owner):
        for number, (spec, piece) in enumerate(zip(specs, pieces)):

            @pl.when(slots[number * owners + owner] >= 0)
            def _():
                slot = slots[number * owners + owner]
                first = pl.multiple_of(slot * spec["rows"], 8)
                place = pl.multiple_of(owner * pitch + spec["offset"], 8)
                pltpu.make_async_copy(
                    flat.at[pl.ds(place, spec["valid"])],
                    piece.at[pl.ds(first, spec["valid"])],
                    sem.at[number, slot],
                ).start()

    def send_each(first, last):
        def step(owner, carry):
            send(owner)
            return carry

        lax.fori_loop(first, last, step, 0)

    place = scalars[segments] * frames + lax.broadcasted_iota(jnp.int32, (frames, 1), 0)
    for s in range(segments):
        live = (place < scalars[s]).astype(F32)
        upper, lower = split(soft_leaky(mel[s] * live).T)
        for part, piece in enumerate((upper, lower, upper)):
            first = (part * segments + s) * frames
            turned[:, first : first + frames] = piece

    def taps(tap, carry):
        upper, lower = split(tap_window(back, tap, segments, frames))
        whole[tap] = dot(turned[...], cat([upper, upper, lower], 0))
        return carry

    lax.fori_loop(0, 16, taps, 0)
    wait_all(loads)
    shared = body // pitch
    send_each(-(-body // pitch), owners)
    group = 16

    def channels(i, carry):
        span = pl.ds(pl.multiple_of(i * group, group), group)
        along = jnp.zeros((group, ch), F32)
        for tap in range(16):
            raw = kept[0, tap, span].astype(F32) + kept[1, tap, span].astype(F32)
            along = along + raw * whole[tap, span]
        factor = gain[span, 0:1]
        column = jnp.sum(along, axis=1, keepdims=True) / factor
        slope[span] = jnp.broadcast_to(column, (group, LANES))
        inv = inverse[span, 0:1]
        scale = factor * inv
        turn = inv * column
        values = []
        for tap in range(16):
            raw = kept[0, tap, span].astype(F32) + kept[1, tap, span].astype(F32)
            value = scale * whole[tap, span] - turn * raw
            for half in range(ch // LANES):
                values.append(value[:, half * LANES : (half + 1) * LANES])
        block = jnp.swapaxes(jnp.stack(values), 0, 1).reshape(group * wide, LANES)
        first = pl.multiple_of(i * (group * wide), group * wide)
        flat[pl.ds(first, group * wide), :] = block
        done = (first + group * wide) // pitch

        @pl.when(done > first // pitch)
        def _():
            send(done - 1)

        return carry

    lax.fori_loop(0, in_ch // group, channels, 0)
    if body % pitch:
        send(shared)
    for j in range(in_ch // LANES):
        full[j : j + 1] = slope[j * LANES : (j + 1) * LANES].T[0:1]
    order = [24]
    for b in range(3):
        order += [8 * b, 8 * b + 1, 8 * b + 2, 8 * b + 1]
    row = in_ch // LANES
    for number in order:
        for part in range(ch // LANES):
            full[row : row + 1] = sums[number : number + 1, part * LANES : (part + 1) * LANES]
            row += 1
    vecs[...] = jnp.zeros_like(vecs)
    for owner in range(geo["owners"]):
        row = owner * geo["vec_count"] // LANES
        vecs[8 * owner : 8 * owner + 2] = full[row : row + 2]
    _, vec_copies = piece_copies(specs, numbers, pieces, flat, scratch, vec_sem, vec_sem, True)
    start_all(vec_copies)
    for number, (spec, piece) in enumerate(zip(specs, pieces)):
        for slot in range(spec["slots"]):
            pltpu.make_async_copy(
                flat.at[pl.ds(0, spec["valid"])],
                piece.at[pl.ds(slot * spec["rows"], spec["valid"])],
                sem.at[number, slot],
            ).wait()
    wait_all(vec_copies)


def frames_back_kernel(geo, scalars, mel, back, high, low, out, total):
    segments, frames = geo["segments"], geo["frames"]
    step = pl.program_id(0)

    @pl.when(step == 0)
    def _():
        total[...] = jnp.zeros_like(total)

    upper, lower = split(tap_window(back, step, segments, frames))
    total[...] += dot(
        cat([upper, lower, upper], 1), cat([high[0], high[0], low[0]], 1), ROWS_ROWS
    )

    @pl.when(step == pl.num_programs(0) - 1)
    def _():
        place = scalars[segments] * frames + lax.broadcasted_iota(jnp.int32, (frames, 1), 0)
        for s in range(segments):
            live = (place < scalars[s]).astype(F32)
            value = total[s * frames : (s + 1) * frames]
            out[s] = value * leaky_slope(mel[s] * live) * live


def whole_spec(shape):
    return pl.BlockSpec(shape, lambda *_: (0,) * len(shape))


def vmem():
    return pl.BlockSpec(memory_space=pltpu.VMEM)


def smem():
    return pl.BlockSpec(memory_space=pltpu.SMEM)


def anywhere():
    return pl.BlockSpec(memory_space=pl.ANY)


def shape(dims, dtype=F32):
    return jax.ShapeDtypeStruct(dims, dtype)


def params():
    return pltpu.CompilerParams(vmem_limit_bytes=VMEM_LIMIT)


def prepare(pieces, specs, numbers, given, geo):
    in_ch, ch = geo["in_ch"], geo["ch"]
    entries = (in_ch * 16 * ch + 15 * ch * ch) // LANES
    geo = dict(geo, specs=specs, given=len(given))
    return pl.pallas_call(
        functools.partial(prepare_kernel, geo),
        out_shape=(
            shape((16, in_ch, ch), BF16),
            shape((16, in_ch, ch), BF16),
            shape((3, 5, ch, ch), BF16),
            shape((3, 5, ch, ch), BF16),
            shape((3, 5, ch, ch), BF16),
            shape((3, 5, ch, ch), BF16),
            shape((3, ch + 8, ch)),
            shape((in_ch, LANES)),
            shape((in_ch, LANES)),
            shape((16, ch)),
            shape((16, LANES)),
        ),
        in_specs=[smem()] + [anywhere()] * len(pieces) + [vmem()] * len(given),
        out_specs=(anywhere(),) * 6 + (vmem(),) * 5,
        scratch_shapes=[
            pltpu.VMEM((entries, LANES), F32),
            pltpu.VMEM((8 * geo["owners"], LANES), F32),
            pltpu.VMEM((40, LANES), F32),
            pltpu.SemaphoreType.DMA((3, geo["owners"])),
            pltpu.SemaphoreType.DMA((copy_count(specs),)),
            pltpu.VMEM((16, in_ch, ch), BF16),
            pltpu.VMEM((16, in_ch, ch), BF16),
        ]
        + [pltpu.VMEM((3, 5, ch, ch), BF16)] * 4
        + [
            pltpu.SemaphoreType.DMA((2, in_ch // 16)),
            pltpu.SemaphoreType.DMA((4, 3)),
        ],
        compiler_params=params(),
    )(numbers, *pieces, *given)


def upsample(scalars, mel_parts, items, up_high, up_low, ahead):
    segments, frames, in_ch = mel_parts[1].shape
    ch = up_high.shape[2]
    kept = frames + 2 * (EDGE // 8)
    size = kept + 8
    geo = {"segments": segments, "frames": frames, "ahead": ahead}
    out = (segments, ch // LANES, 8 * kept, LANES)
    return pl.pallas_call(
        functools.partial(upsample_kernel, geo),
        grid=(8,),
        out_shape=shape(out),
        in_specs=[smem()]
        + [whole_spec(part.shape) for part in mel_parts]
        + [
            whole_spec(items.shape),
            pl.BlockSpec((1, in_ch, ch), lambda j: (j + 4, 0, 0)),
            pl.BlockSpec((1, in_ch, ch), lambda j: (j + 4, 0, 0)),
            pl.BlockSpec((1, in_ch, ch), lambda j: ((j + 12) % 16, 0, 0)),
            pl.BlockSpec((1, in_ch, ch), lambda j: ((j + 12) % 16, 0, 0)),
        ],
        out_specs=whole_spec(out),
        scratch_shapes=[
            pltpu.VMEM((segments, frames + 2 * EDGE_FRAMES + 16, in_ch), F32),
            pltpu.VMEM((2, segments * size, in_ch), BF16),
            pltpu.VMEM((2, 2, segments * size, in_ch), BF16),
        ],
        compiler_params=params(),
    )(scalars, *mel_parts, items, up_high, up_low, up_high, up_low)


def blocks(scalars, items, start, cot_parts, mat_high, mat_low, turn_high, turn_low, short):
    segments, samples, ch = cot_parts[1].shape
    rows = samples + 2 * EDGE
    geo = {"segments": segments, "samples": samples, "ch": ch, "tiles": 4}
    halves = start.shape[1]
    flat = (15 * ch * ch // LANES, LANES)
    once = pl.Buffered(1)

    def fixed(dims):
        return pl.BlockSpec(dims, lambda s: (0,) * len(dims), pipeline_mode=once)

    return pl.pallas_call(
        functools.partial(blocks_kernel, geo),
        grid=(segments,),
        out_shape=(
            shape((segments, samples, ch)),
            shape((segments, halves, rows, LANES)),
            shape(flat),
            shape((32, ch)),
        ),
        in_specs=[
            smem(),
            fixed(items.shape),
            pl.BlockSpec((1, halves, rows, LANES), lambda s: (s, 0, 0, 0)),
        ]
        + [pl.BlockSpec((1,) + part.shape[1:], lambda s: (s, 0, 0)) for part in cot_parts]
        + [
            fixed(mat_high.shape),
            fixed(mat_low.shape),
            fixed(turn_high.shape),
            fixed(turn_low.shape),
            fixed(short.shape),
        ],
        out_specs=(
            pl.BlockSpec((1, samples, ch), lambda s: (s, 0, 0)),
            pl.BlockSpec((1, halves, rows, LANES), lambda s: (s, 0, 0, 0)),
            pl.BlockSpec(flat, lambda s: (0, 0), pipeline_mode=once),
            pl.BlockSpec((32, ch), lambda s: (0, 0)),
        ),
        scratch_shapes=[
            pltpu.VMEM((4, rows, ch), F32),
            pltpu.VMEM((3, rows, ch), F32),
            pltpu.VMEM((2, rows + 2 * PAD, ch), F32),
            pltpu.VMEM((2, 2, rows, 3 * ch), BF16),
            pltpu.VMEM((3, 2, rows, ch), BF16),
            pltpu.VMEM((3, 2, rows, ch), BF16),
            pltpu.VMEM((3, 2, rows, ch), BF16),
            pltpu.VMEM((rows, ch), F32),
            pltpu.VMEM((2, 2, rows, ch), BF16),
            pltpu.VMEM((3, ch, 3 * ch), F32),
            pltpu.VMEM((3, ch, 2 * ch), F32),
        ],
        compiler_params=params(),
    )(scalars, items, start, *cot_parts, mat_high, mat_low, turn_high, turn_low, short)


def weight_back(
    scalars, mel, gain, inverse, sums, back, high, low, block_grads, specs, numbers, slots, geo
):
    segments, frames, in_ch = mel.shape
    ch = high.shape[2]
    body = in_ch * 16 * ch // LANES
    given = 0 if specs[-1]["vec"] >= 0 else 1
    geo = dict(geo, specs=specs, segments=segments, frames=frames, given=given)
    vec_shape = (8 * geo["owners"], LANES)
    return pl.pallas_call(
        functools.partial(weight_back_kernel, geo),
        out_shape=tuple(shape((spec["slots"] * spec["rows"], LANES)) for spec in specs)
        + (shape(vec_shape),) * given,
        in_specs=[smem()] * 3 + [vmem()] * 5 + [anywhere()] * 3,
        out_specs=(anywhere(),) * len(specs) + (vmem(),) * given,
        scratch_shapes=[
            pltpu.VMEM((in_ch, 3 * segments * frames), BF16),
            pltpu.VMEM((16, in_ch, ch), F32),
            pltpu.VMEM((2, 16, in_ch, ch), BF16),
            pltpu.VMEM((in_ch, LANES), F32),
            pltpu.VMEM((body + block_grads.shape[0], LANES), F32),
            pltpu.VMEM(vec_shape, F32),
            pltpu.VMEM((40, LANES), F32),
            pltpu.SemaphoreType.DMA((3,)),
            pltpu.SemaphoreType.DMA((len(specs), max(spec["slots"] for spec in specs))),
            pltpu.SemaphoreType.DMA((copy_count(specs),)),
        ],
        compiler_params=params(),
    )(scalars, numbers, slots, mel, gain, inverse, sums, back, high, low, block_grads)


def frames_back(scalars, mel, back, high, low):
    segments, frames, in_ch = mel.shape
    ch = high.shape[2]
    geo = {"segments": segments, "frames": frames}
    weight = pl.BlockSpec((1, in_ch, ch), lambda k: (k, 0, 0))
    return pl.pallas_call(
        functools.partial(frames_back_kernel, geo),
        grid=(16,),
        out_shape=shape(mel.shape),
        in_specs=[smem(), whole_spec(mel.shape), whole_spec(back.shape), weight, weight],
        out_specs=whole_spec(mel.shape),
        scratch_shapes=[pltpu.VMEM((segments * frames, in_ch), F32)],
        compiler_params=params(),
        cost_estimate=pl.CostEstimate(
            flops=6 * segments * frames * in_ch * 16 * ch,
            bytes_accessed=4 * 16 * in_ch * ch + 8 * mel.size + 4 * back.size,
            transcendentals=0,
        ),
    )(scalars, mel, back, high, low)


def line_edges(low, high, axis):
    count = math.prod(lax.axis_size(name) for name in axis)
    forward = [(i, i + 1) for i in range(count - 1)]
    backward = [(target, source) for source, target in forward]
    return lax.ppermute(high, axis, forward), lax.ppermute(low, axis, backward)


def packed_edges(mel, cot):
    ch = cot.shape[2]
    edges = []
    for frames, samples in (
        (mel[:, :EDGE_FRAMES], cot[:, :EDGE]),
        (mel[:, mel.shape[1] - EDGE_FRAMES :], cot[:, cot.shape[1] - EDGE :]),
    ):
        edges.append(cat([frames[:, :, :ch], frames[:, :, ch:], samples], 1))
    return edges


def moments(gradient, first, second):
    first_new = B_ONE * first + (1.0 - B_ONE) * gradient
    second_new = B_TWO * second + (1.0 - B_TWO) * gradient * gradient
    direction = (
        first_new / (1.0 - B_ONE**STEP) / (jnp.sqrt(second_new / (1.0 - B_TWO**STEP)) + EPSILON)
    )
    return (first_new, second_new, direction)


def total(value, groups):
    for group in groups:
        count = math.prod(lax.axis_size(name) for name in group)
        far = 1
        while far < count:
            near = min(4, count // far)
            terms = [value]
            for step in range(1, near):
                moves = [(i, i ^ (step * far)) for i in range(count)]
                terms.append(lax.ppermute(value, group, moves))
            while len(terms) > 1:
                terms = [one + other for one, other in zip(terms[::2], terms[1::2])]
            value = terms[0]
            far = near * far
    return value


FLIPS = {"wide": ("wide", 1), "deep": ("deep", 1), "near": ("line", 1), "far": ("line", 2), "core": ("core", 1)}
ORDERS = (("wide", "deep", "near", "far"), ("deep", "wide", "near", "far"), ("near", "far", "wide", "deep"))
SCATTER_ORDERS = ORDERS[:2] + (("far", "near", "wide", "deep"),)
LANE_ROWS = 8


def swap(value, flip):
    axis, step = FLIPS[flip]
    return lax.ppermute(value, axis, [(i, i ^ step) for i in range(lax.axis_size(axis))])


def owner_table(order, other_core):
    places = {name: lax.axis_index(name) for name in ("line", "deep", "wide", "core")}
    numbers = []
    for slot in range(16):
        here = dict(places)
        for bit, flip in enumerate(order):
            if slot >> (3 - bit) & 1:
                axis, step = FLIPS[flip]
                here[axis] = here[axis] ^ step
        core = here["core"] ^ other_core
        numbers.append(((here["line"] * 2 + here["deep"]) * 2 + here["wide"]) * 2 + core)
    return jnp.stack(numbers).astype(jnp.int32)


def slot_table(order, other_core, owners):
    numbers = jnp.arange(owners, dtype=jnp.int32)
    there = {"core": numbers % 2, "wide": numbers // 2 % 2, "deep": numbers // 4 % 2}
    there["line"] = numbers // 8
    away = {name: lax.axis_index(name).astype(jnp.int32) ^ place for name, place in there.items()}
    slot = jnp.zeros_like(numbers)
    for flip in order:
        axis, step = FLIPS[flip]
        slot = 2 * slot + (away[axis] // step) % 2
    return jnp.where(away["core"] == other_core, slot, -1)


def part_sizes(shard_rows):
    last = shard_rows * 7 // 48 // 8 * 8
    first = (shard_rows - last) // 16 * 8
    return (first, first, shard_rows - 2 * first)


def part_specs(sizes, rows, slots):
    specs = []
    offset = 0
    for part, size in enumerate(sizes):
        valid = min(size, rows - offset)
        specs.append(
            {
                "part": part,
                "slots": slots,
                "rows": size,
                "pitch": rows,
                "offset": offset,
                "valid": valid,
                "vec": valid if valid < size else -1,
            }
        )
        offset += size
    return specs


def together(*values):
    return lax.optimization_barrier(values)


def gather_by_permutes(shard, sizes, edges, tm):
    first, second, third = sizes
    both, last = shard[: first + second], shard[first + second :]
    far, near, last_deep, last_wide, edges = together(
        swap(both, "far"),
        swap(both, "near"),
        swap(last, "deep"),
        swap(last, "wide"),
        line_edges(*edges, tm),
    )
    near_far, last_both = together(swap(far, "near"), swap(last_deep, "wide"))
    parts = (both, far, near, near_far)
    a = cat([part[:first] for part in parts], 0)
    b = cat([part[first:] for part in parts], 0)
    c = cat([last, last_deep, last_wide, last_both], 0)
    a, b, c = together(a, b, c)
    a_deep, b_wide, c_far = swap(a, "deep"), swap(b, "wide"), swap(c, "far")
    c_near = swap(c, "near")
    a_deep, b_wide, c_far, c_near, a, b = together(a_deep, b_wide, c_far, c_near, a, b)
    c_both = swap(c_far, "near")
    a_both, b_both = swap(a_deep, "wide"), swap(b_wide, "deep")
    a_wide, b_deep = swap(a, "wide"), swap(b, "deep")
    ready = [(0, 0, a), (1, 0, b), (2, 0, c), (0, 1, a_deep), (1, 1, b_wide), (2, 1, c_far)]
    ready.append((2, 2, c_near))
    others = [swap(array, "core") for _, _, array in ready]
    a_both, b_both, a_wide, b_deep, c_both, others = together(
        a_both, b_both, a_wide, b_deep, c_both, others
    )
    held = [(n, quarter, 0, array) for n, quarter, array in ready]
    held += [(n, quarter, 1, array) for (n, quarter, _), array in zip(ready, others)]
    rest = [(0, 2, a_wide), (1, 2, b_deep), (0, 3, a_both), (1, 3, b_both), (2, 3, c_both)]
    for n, quarter, array in rest:
        held += [(n, quarter, 0, array), (n, quarter, 1, swap(array, "core"))]
    return held, edges


def scatter_by_permutes(mine, theirs, sizes, beside):
    came = [swap(value, "core") for value in theirs]
    terms = [[own, other] for own, other in zip(mine, came)]
    slots = 16
    for level in range(4):
        slots = slots // 2
        away = []
        for number, (part, size) in enumerate(zip(terms, sizes)):
            if level == 0 and number > 0:
                part[1], away[-1] = together(part[1], away[-1])
            away.append(sum(term[slots * size : 2 * slots * size] for term in part))
        came = [swap(value, order[level]) for value, order in zip(away, SCATTER_ORDERS)]
        if level == 0:
            came, other = together(came, beside())
        else:
            came = together(*came)
        for part, value in zip(terms, came):
            part.append(value)
    summed = cat([sum(term[:size] for term in part) for part, size in zip(terms, sizes)], 0)
    return summed, other


def by_owner(mine, theirs, plan):
    grid, core_dim = plan["grid"], plan["core_dim"]
    first = lax.axis_index("core") == 0
    parts = [jnp.where(first, mine, theirs), jnp.where(first, theirs, mine)]
    chips = [size for place, size in enumerate(grid) if place != core_dim]
    parts = [part.reshape(chips + list(mine.shape[1:])) for part in parts]
    return jnp.stack(parts, axis=core_dim).reshape((-1,) + mine.shape[1:])


def by_core(shards, plan):
    grid, core_dim = plan["grid"], plan["core_dim"]
    grouped = shards.reshape(tuple(grid) + shards.shape[1:])
    core = lax.axis_index("core")
    mine = lax.dynamic_index_in_dim(grouped, core, core_dim, keepdims=False)
    theirs = lax.dynamic_index_in_dim(grouped, 1 - core, core_dim, keepdims=False)
    after = (-1,) + shards.shape[1:]
    return mine.reshape(after), theirs.reshape(after)


def body(
    plan,
    mel_frames,
    lengths,
    cotangent,
    matrices,
    vectors,
    matrix_first,
    matrix_second,
    vector_first,
    vector_second,
):
    tm, every, chip_axes = plan["tm"], plan["every"], plan["chip_axes"]
    segments, frames, in_ch = mel_frames.shape
    ch = cotangent.shape[2]
    pieces = math.prod(lax.axis_size(name) for name in tm)
    rows = matrices.shape[0] // LANES
    shard_rows = -(-(rows + 2) // 48) * 48
    vec_count = vectors.shape[0]
    spare = shard_rows - rows - 2
    owners = math.prod(plan["grid"])
    geo = {"in_ch": in_ch, "ch": ch, "owners": owners, "vec_count": vec_count}
    vec_first = lax.axis_index(every) * vec_count % LANES
    placed = lax.dynamic_update_slice(jnp.zeros((2 * LANES,), F32), vectors, (vec_first,))
    shard = jnp.concatenate(
        [
            matrices.reshape(rows, LANES),
            placed.reshape(2, LANES),
            jnp.zeros((spare, LANES), F32),
        ]
    )
    edges = packed_edges(mel_frames, cotangent)
    cubic = rows % 8 == 0 and plan["grid"] == (4, 2, 2, 2)
    sizes = part_sizes(shard_rows)
    if cubic:
        specs = part_specs(sizes, rows, 16)
        numbers = [[owner_table(order, core) for order in ORDERS] for core in range(2)]
        held, edges = gather_by_permutes(shard, sizes, edges, tm)
        held_numbers = jnp.concatenate(
            [numbers[c][n][4 * quarter : 4 * quarter + 4] for n, quarter, c, _ in held]
        )
        held_specs = [dict(specs[n], slots=4) for n, _, _, _ in held]
        held = [array for _, _, _, array in held]
        given = []
    else:
        edges = line_edges(*edges, tm)
        mine = lax.all_gather(shard, chip_axes, axis=0, tiled=False)
        gathered = by_owner(mine, swap(mine, "core"), plan)
        held = [gathered[:, :rows].reshape(-1, LANES)]
        whole = held[0].shape[0]
        specs = [
            {
                "part": 0,
                "slots": 1,
                "rows": whole,
                "pitch": 0,
                "offset": 0,
                "valid": whole,
                "vec": -1,
            }
        ]
        held_specs, held_numbers = specs, jnp.zeros((1,), jnp.int32)
        vec_rows = jnp.pad(gathered[:, rows : rows + 2], ((0, 0), (0, LANE_ROWS - 2), (0, 0)))
        given = [vec_rows.reshape(-1, LANES)]
    mel_parts = (edges[0], mel_frames, edges[1])
    cot_parts = (edges[0], cotangent, edges[1])
    scalars = jnp.concatenate(
        [lengths[0], jnp.stack([lax.axis_index(tm), jnp.int32(pieces)]).astype(jnp.int32)]
    )
    up_high, up_low, *mats, short, inverse, gain, items, squares = prepare(
        held, held_specs, held_numbers, given, geo
    )
    start = upsample(scalars, mel_parts, items, up_high, up_low, pieces * frames)
    waveform, back, block_grads, sums = blocks(scalars, items, start, cot_parts, *mats, short)
    if cubic:
        out_specs = specs * 2
        out_numbers = jnp.concatenate(
            [owner_table(order, core) for core in range(2) for order in SCATTER_ORDERS]
        )
        out_slots = jnp.concatenate(
            [slot_table(order, core, owners) for core in range(2) for order in SCATTER_ORDERS]
        )
    else:
        out_specs, out_numbers, out_slots = held_specs, held_numbers, held_numbers
    grads = weight_back(
        scalars,
        mel_frames,
        gain,
        inverse,
        sums,
        back,
        up_high,
        up_low,
        block_grads,
        out_specs,
        out_numbers,
        out_slots,
        geo,
    )
    if cubic:
        summed, frames_grad = scatter_by_permutes(
            grads[:3],
            grads[3:],
            sizes,
            lambda: frames_back(scalars, mel_frames, back, up_high, up_low),
        )
    else:
        vec_rows = grads[1].reshape(owners, LANE_ROWS, LANES)[:, :2]
        shards = jnp.concatenate(
            [
                grads[0].reshape(owners, rows, LANES),
                vec_rows,
                jnp.zeros((owners, spare, LANES), F32),
            ],
            axis=1,
        )
        mine, theirs = by_core(shards, plan)
        mine = mine + swap(theirs, "core")
        summed = lax.psum_scatter(mine, chip_axes, scatter_dimension=0, tiled=True)[0]
        frames_grad = frames_back(scalars, mel_frames, back, up_high, up_low)
    matrix_grad = summed[:rows]
    vec_rows = summed[rows : rows + 2].reshape(-1)
    vector_grad = lax.dynamic_slice(vec_rows, (vec_first,), (vec_count,))

    shapes, starts, whole = layout(in_ch, ch)
    matrices = matrices.reshape(rows, LANES)
    position = lax.axis_index(every) * rows + jnp.arange(rows, dtype=jnp.int32)
    lower = jnp.array([first // LANES for first in starts], jnp.int32)
    upper = jnp.array([first // LANES for first in starts[1:] + [whole]], jnp.int32)
    member = (position[:, None] >= lower[None, :]) & (position[:, None] < upper[None, :])
    member = member.astype(F32)
    matrix_first_new, matrix_second_new, direction = moments(
        matrix_grad, matrix_first.reshape(rows, LANES), matrix_second.reshape(rows, LANES)
    )
    update = direction + DECAY * matrices
    update_sq = jnp.sum(member * jnp.sum(update * update, axis=1)[:, None], axis=0)
    update_sq = total(update_sq, (("core",), ("deep", "wide"), ("line",)))
    weight_norm = jnp.sqrt(jnp.sum(squares[:10], axis=1))
    update_norm = jnp.sqrt(update_sq)
    trust = weight_norm / update_norm
    row_trust = jnp.sum(member * trust[None, :], axis=1)
    new_matrices = (matrices - RATE * row_trust[:, None] * update).reshape(-1)
    vector_first_new, vector_second_new, vector_step = moments(
        vector_grad, vector_first, vector_second
    )
    new_vectors = vectors - RATE * vector_step
    norm_table = jnp.stack([weight_norm, update_norm])
    return (
        waveform,
        frames_grad,
        new_matrices,
        new_matrices.astype(BF16),
        matrix_first_new.reshape(-1),
        matrix_second_new.reshape(-1),
        new_vectors,
        new_vectors.astype(BF16),
        vector_first_new,
        vector_second_new,
        norm_table,
    )


def make_plan(mesh):
    tm, batch = mesh.shape["tm"], mesh.shape["batch"]
    if tm > 4:
        root = math.isqrt(batch)
        grid = (tm // 2, 2, root, batch // root)
        names = ("line", "core", "deep", "wide")
        tm_axes, batch_axes = ("line", "core"), ("deep", "wide")
        core_dim = 1
    else:
        root = math.isqrt(batch // 2)
        grid = (tm, root, batch // 2 // root, 2)
        names = ("line", "deep", "wide", "core")
        tm_axes, batch_axes = ("line",), ("deep", "wide", "core")
        core_dim = 3
    inner = Mesh(mesh.devices.reshape(grid), names)
    plan = {
        "tm": tm_axes,
        "batch": batch_axes,
        "every": names,
        "grid": grid,
        "core_dim": core_dim,
        "chip_axes": tuple(name for name in names if name != "core"),
    }
    return inner, plan


def solution(mesh):
    inner, plan = make_plan(mesh)
    tm, batch, every = plan["tm"], plan["batch"], plan["every"]
    pieces, flat = P(batch, tm, None), P(every)
    in_specs = (pieces, P(batch, None), pieces, flat, flat, flat, flat, flat, flat)
    out_specs = (pieces, pieces, flat, flat, flat, flat, flat, flat, flat, flat, P())
    return jax.shard_map(
        functools.partial(body, plan),
        mesh=inner,
        in_specs=in_specs,
        out_specs=out_specs,
        check_vma=False,
    )
```
